256 devices in a mesh: cells: 16 (over z, x_hi), samples: 16 (over y, x_lo, core).
Axes of the slice: x: 4 (x_hi: 2, x_lo: 2; x = x_hi * 2 + x_lo), y: 4, z: 8, core: 2. Of those that a mesh axis runs over, the one named last changes fastest.
Arguments:
- init_state: float32 [128, 32768], P('samples', 'cells'), may hold values from -6 to 6
- tiles_exp: bfloat16 [256, 6, 128, 128], P(('cells', 'samples')), may hold values from -1 to 2
- cols_exp: int32 [256, 6], P('cells'), may hold values from 12 to 35, as said below
- tiles_imp: bfloat16 [256, 6, 128, 128], P(('cells', 'samples')), may hold values from -1 to 2
- cols_imp: int32 [256, 6], P('cells'), may hold values from 12 to 35
- surface: int32 [32768], P('cells'), may hold values 0 or 1
- piston: float32 [128], P('samples'), may hold values from 0.5 to 2
- atmosphere: float32 [128], P('samples'), may hold values from -1 to 1
- final_cot: float32 [128, 32768], P('samples', 'cells'), may hold values from -12 to 12
Outputs:
- final_state: float32 [128, 32768], P('samples', 'cells')
- initial_adjoint: float32 [128, 32768], P('samples', 'cells')
- piston_grad: float32 [128], P('samples')
The draws below stay inside these ranges and needn't reach their ends.
Inputs may be any that keep to these rules, and one draw needn't show every extreme that they name: cols_exp[g, 0] = 16 + g % 16, the tile on the diagonal; in the first row tile of each block of 16 slot 1 is the lowest value, in the last one slot 1 is the highest; values may repeat in a row.
All inputs are finite; a program needn't handle non-finite values. No bound on the sum of `surface` on one device may be relied on, other than what follows from the above.
Results may differ from the reference program's by a relative error of at most 0.03.
Values may be sent and summed in bfloat16 or wider, within the bound.
A program may use at most 64 MiB of HBM per device.

```python
import math
import jax
import jax.numpy as jnp
from jax import lax

TILE = 128
RT = 16
K = 6
STEPS = 8
NB = 4
NT = 256
CELLS = 32768
SAMPLES = 128
N_CELLS = 16


def tile_values(noise, diagonal, spread):
    shape = noise.shape
    slot = lax.broadcasted_iota(jnp.int32, shape, 1)
    row_inner = lax.broadcasted_iota(jnp.int32, shape, 2)
    col_inner = lax.broadcasted_iota(jnp.int32, shape, 3)
    on_diagonal = ((slot == 0) & (row_inner == col_inner)).astype(jnp.float32)
    return (noise * (spread / math.sqrt(K * TILE)) + diagonal * on_diagonal).astype(jnp.bfloat16)


def column_pattern(key):
    shape = (NT, K)
    drawn = jax.random.randint(key, shape, RT - NB, 2 * RT + NB, jnp.int32)
    slot = lax.broadcasted_iota(jnp.int32, shape, 1)
    within = lax.broadcasted_iota(jnp.int32, shape, 0) % RT
    drawn = jnp.where((slot == 1) & (within == 0), RT - NB, drawn)
    drawn = jnp.where((slot == 1) & (within == RT - 1), 2 * RT + NB - 1, drawn)
    return jnp.where(slot == 0, RT + within, drawn).astype(jnp.int32)


def draw_tiles_exp(key, part):
    key = jax.random.fold_in(key, 11)
    shape = (NT, K, TILE, TILE)
    noise = jax.random.truncated_normal(key, -4.0, 4.0, shape, jnp.float32)
    return tile_values(noise, 0.85, 0.3)


def draw_tiles_imp(key, part):
    key = jax.random.fold_in(key, 13)
    shape = (NT, K, TILE, TILE)
    noise = jax.random.truncated_normal(key, -4.0, 4.0, shape, jnp.float32)
    return tile_values(noise, 0.8, 0.35)


def draw_cols_exp(key, part):
    key = jax.random.fold_in(key, 17)
    return column_pattern(key)


def draw_cols_imp(key, part):
    key = jax.random.fold_in(key, 19)
    return column_pattern(key)


def draw_final_cot(key, part):
    key = jax.random.fold_in(key, 31)
    shape = (SAMPLES, CELLS)
    place = lax.broadcasted_iota(jnp.int32, shape, 1).astype(jnp.float32) / CELLS
    noise = jax.random.truncated_normal(key, -4.0, 4.0, shape, jnp.float32) * (1.0 + 2.0 * place)
    return noise


def place_ends(values, key, least, high):
    shape = values.shape
    spot = [jax.random.randint(jax.random.fold_in(key, axis), (), 0, shape[axis]) for axis in range(len(shape))]
    values = values.at[tuple(spot)].set(least)
    longest = shape.index(max(shape))
    spot[longest] = (spot[longest] + 1) % shape[longest]
    return values.at[tuple(spot)].set(high)


def levels(rng, extent, pieces, smallest, high):
    def one(dim, blocks):
        heights = jax.random.uniform(jax.random.fold_in(jax.random.fold_in(rng, 6), dim), (blocks,), jnp.float32, smallest / len(pieces), high / len(pieces))
        return jnp.repeat(jnp.exp(heights), extent[dim] // blocks).reshape((-1,) + (1,) * (len(extent) - dim - 1))

    level = one(*pieces[0])
    for cut in pieces[1:]:
        level = level * one(*cut)
    return level


def bell_draw(own_key, dims, deviation, bound, cuts=(), held_as=jnp.bfloat16):
    loudness = levels(own_key, dims, cuts, -0.22, 0.18) if cuts else 1.0
    array = jax.random.normal(own_key, dims, jnp.float32) * deviation * loudness
    return jnp.minimum(jnp.maximum(array, -bound), bound).astype(held_as)


def setup_inputs(seed: int = 0) -> dict:
    streams_of = jax.random.split(jax.random.key(seed), 10)
    return {
        "init_state": bell_draw(streams_of[0], (SAMPLES, CELLS), 1.0, 6.0, ((0, 16), (1, 16)), jnp.float32),
        "tiles_exp": draw_tiles_exp(jax.random.fold_in(streams_of[9], 71), 0),
        "cols_exp": draw_cols_exp(jax.random.fold_in(streams_of[9], 71), 0),
        "tiles_imp": draw_tiles_imp(jax.random.fold_in(streams_of[9], 71), 0),
        "cols_imp": draw_cols_imp(jax.random.fold_in(streams_of[9], 71), 0),
        "surface": place_ends((jax.random.randint(streams_of[5], (CELLS,), 0, 4) < 1).astype(jnp.int32), jax.random.fold_in(streams_of[5], 1), 0, 1),
        "piston": jnp.clip(jnp.exp(math.log(2.0) - 1.3862944 * jax.random.uniform(streams_of[6], (SAMPLES,), jnp.float32) ** levels(streams_of[6], (SAMPLES,), ((0, 16),), -0.2, 0.2)), 0.5, 2.0),
        "atmosphere": jnp.clip(jax.random.uniform(streams_of[7], (SAMPLES,), jnp.float32, -1.0, 1.0) * levels(streams_of[7], (SAMPLES,), ((0, 16),), -0.4, 0.0), -1.0, 1.0),
        "final_cot": draw_final_cot(jax.random.fold_in(streams_of[9], 71), 0),
    }


step_length = 0.5
buffer_gain = 0.5

def carbonate(tracer):
    return tracer * (1.0 + buffer_gain * jnp.tanh(tracer))

def carbonate_slope(tracer):
    bend = jnp.tanh(tracer)
    return 1.0 + buffer_gain * bend + buffer_gain * tracer * (1.0 - bend * bend)

def column_blocks(cols):
    owner = jnp.arange(NT, dtype=jnp.int32) // RT * RT
    return ((owner[:, None] + cols - RT) % NT).astype(jnp.int32)

def apply_forward(tiles, cols, field):
    field = lax.optimization_barrier(field)
    blocks = field.astype(jnp.float32).reshape(SAMPLES, NT, TILE)
    globals_index = column_blocks(cols).reshape(N_CELLS, RT, K)
    tile_groups = tiles.reshape(N_CELLS, RT, K, TILE, TILE)

    def per_block(packed):
        tile_group, block_index = packed
        picked = blocks[:, block_index]
        return jnp.einsum('rkoc,srkc->sro', tile_group.astype(jnp.float32), picked)
    results = lax.map(per_block, (tile_groups, globals_index))
    return jnp.transpose(results, (1, 0, 2, 3)).reshape(SAMPLES, CELLS)

def apply_adjoint(tiles, cols, field):
    field = lax.optimization_barrier(field)
    weights = field.astype(jnp.float32).reshape(SAMPLES, N_CELLS, RT, TILE)
    globals_index = column_blocks(cols).reshape(N_CELLS, RT * K)
    tile_groups = tiles.reshape(N_CELLS, RT, K, TILE, TILE)

    def accumulate(running, packed):
        tile_group, block_index, row_values = packed
        contrib = jnp.einsum('rkoc,sro->srkc', tile_group.astype(jnp.float32), row_values)
        running = running.at[:, block_index].add(contrib.reshape(SAMPLES, RT * K, TILE))
        return (running, None)
    start = jnp.zeros((SAMPLES, NT, TILE), jnp.float32)
    running, unused = lax.scan(accumulate, start, (tile_groups, globals_index, jnp.transpose(weights, (1, 0, 2, 3))))
    return running.reshape(SAMPLES, CELLS)

def reference(init_state, tiles_exp, cols_exp, tiles_imp, cols_imp, surface, piston, atmosphere, final_cot):
    surface_weight = surface.astype(jnp.float32)[None, :]
    piston_rate = piston[:, None]
    air_level = atmosphere[:, None]
    tracer = init_state
    history = []
    for section in range(STEPS):
        history.append(tracer)
        moved = apply_forward(tiles_exp, cols_exp, tracer.astype(jnp.bfloat16))
        source = moved + step_length * surface_weight * piston_rate * (air_level - carbonate(tracer))
        tracer = apply_forward(tiles_imp, cols_imp, source.astype(jnp.bfloat16))
    adjoint = final_cot
    gradient = jnp.zeros((SAMPLES,), jnp.float32)
    for section in reversed(range(STEPS)):
        state = history[section]
        upper = apply_adjoint(tiles_imp, cols_imp, adjoint.astype(jnp.bfloat16))
        gradient = gradient + lax.optimization_barrier(jnp.sum(upper * step_length * surface_weight * (air_level - carbonate(state)), axis=1))
        adjoint = apply_adjoint(tiles_exp, cols_exp, upper.astype(jnp.bfloat16)) - step_length * surface_weight * piston_rate * carbonate_slope(state) * upper
    return (tracer, adjoint, gradient / math.sqrt(CELLS))
```

```python
import math

import jax
import jax.numpy as jnp
from jax import lax
from jax.experimental import pallas as pl
from jax.experimental.pallas import tpu as pltpu
from jax.sharding import PartitionSpec as P

STEPS = 8
RT = 16
K = 6
NB = 4
TILE = 128
ROWS = 8
GROUP = 4 * K
WIN = RT + 2 * NB
WIDE = WIN + 2 * RT
LOW = RT - NB
EDGE = RT + NB
SEG = GROUP + 1

step_length = 0.5
buffer_gain = 0.5
MESH = pl.DeviceIdType.MESH
f32, bf16 = jnp.float32, jnp.bfloat16


def kernel(
    n_cells,
    init_ref, te_ref, ti_ref, cols_ref, surf_ref, piston_ref, air_ref, cot_ref,
    final_ref, adj_ref, grad_ref,
    te, ti, x, src, gas, bend, half, meta, meta_in, idx,
    surf_own, surf_in, send1, recv1, recv2, a, u, part, contrib, seg,
    out1, out2, in1, in2, gacc, gin,
    s_small, r_small, l_sem, s_gather, r_gather, s_core, r_core, s_halo, r_halo, s_hcore, r_hcore,
    s_fwd, r_fwd, s_adj, r_adj, s_grad, r_grad,
):
    c = lax.axis_index("cells")
    s = lax.axis_index("samples")
    y, l, k = s // 4, (s // 2) % 2, s % 2

    def rem(v, m):
        return lax.rem(v + m, m)

    def block(delta):
        return (rem(c + delta, n_cells), s)

    def plane(yy, ll, kk):
        return (c, yy * 4 + ll * 2 + kk)

    up, down = plane(rem(y + 1, 4), l, k), plane(rem(y - 1, 4), l, k)
    across, other = plane(y, 1 - l, k), plane(y, l, 1 - k)

    def copy(source, target, send, recv, device):
        return pltpu.make_async_remote_copy(source, target, send, recv, device_id=device, device_id_type=MESH)

    barrier = pltpu.get_barrier_semaphore()
    peers = [up, down, across, other] + [block(d) for d in range(1, n_cells)]
    for device in peers:
        pl.semaphore_signal(barrier, inc=1, device_id=device, device_id_type=MESH)

    for i in range(RT):
        x[EDGE + i] = init_ref[:, i * TILE:(i + 1) * TILE]
        a[i] = cot_ref[:, i * TILE:(i + 1) * TILE]
    surf_own[...] = surf_ref[...].astype(f32) * step_length
    row_of = lax.broadcasted_iota(jnp.int32, (ROWS, TILE), 0)
    piston = jnp.zeros((ROWS, TILE), f32)
    air = jnp.zeros((ROWS, TILE), f32)
    for i in range(ROWS):
        piston = jnp.where(row_of == i, piston_ref[i], piston)
        air = jnp.where(row_of == i, air_ref[i], air)
    gacc[...] = jnp.zeros((ROWS, TILE), f32)
    for g in range(6):
        seg[g * SEG + GROUP] = jnp.zeros((ROWS, TILE), f32)

    cols = jnp.clip(cols_ref[...], LOW, LOW + WIN - 1)
    lane = lax.broadcasted_iota(jnp.int32, (8, TILE), 1)
    key = cols * 32 + lane
    rank = jnp.zeros((8, TILE), jnp.int32)
    upto = jnp.zeros((8, TILE), jnp.int32)
    here = jnp.zeros((8, TILE), jnp.int32)
    for i in range(GROUP):
        one = jnp.broadcast_to(cols[:, i:i + 1], (8, TILE))
        rank = rank + jnp.where(one * 32 + i < key, 1, 0)
        upto = upto + jnp.where(one - LOW <= lane, 1, 0)
        here = here + jnp.where(one - LOW == lane, 1, 0)
    order = jnp.zeros((8, TILE), jnp.int32)
    ordered = jnp.zeros((8, TILE), jnp.int32)
    before = jnp.zeros((8, TILE), jnp.int32)
    for i in range(GROUP):
        place = jnp.broadcast_to(rank[:, i:i + 1], (8, TILE))
        one = jnp.broadcast_to(cols[:, i:i + 1], (8, TILE))
        order = order + jnp.where(place == lane, i, 0)
        ordered = ordered + jnp.where(place == lane, one, 0)
        before = before + jnp.where(place + 1 == lane, one, 0)
    meta[0] = cols
    meta[1] = order
    meta[2] = jnp.where(ordered == before, 1, 0)
    meta[3] = jnp.where(here > 0, upto - 1, GROUP)

    def pack_state(slot):
        for j in range(RT // 2):
            pair = jnp.concatenate([x[EDGE + 2 * j], x[EDGE + 2 * j + 1]], axis=0)
            send1[slot, j] = pair.astype(bf16)

    half_nb = NB // 2

    def state_copies(slot):
        mine = send1.at[slot]
        return [
            copy(mine, recv1.at[slot, 1], s_fwd.at[slot, 0], r_fwd.at[slot, 1], block(-1)),
            copy(mine, recv1.at[slot, 0], s_fwd.at[slot, 1], r_fwd.at[slot, 0], block(1)),
            copy(mine.at[pl.ds(0, half_nb)], recv2.at[slot, 1], s_fwd.at[slot, 2], r_fwd.at[slot, 3], block(-2)),
            copy(mine.at[pl.ds(RT // 2 - half_nb, half_nb)], recv2.at[slot, 0], s_fwd.at[slot, 3], r_fwd.at[slot, 2], block(2)),
        ]

    pack_state(0)
    pl.semaphore_wait(barrier, len(peers))

    small = []
    for side, device in ((0, block(1)), (1, block(-1))):
        small.append(copy(surf_own, surf_in.at[side], s_small.at[side], r_small.at[side], device))
        small.append(copy(meta, meta_in.at[side], s_small.at[2 + side], r_small.at[2 + side], device))
    for cp in small:
        cp.start()
    for cp in state_copies(0):
        cp.start()
    own_idx = pltpu.make_async_copy(meta, idx.at[1], l_sem.at[0])
    own_idx.start()

    buf = (te, ti)

    def tile_at(which, yy, ll, kk):
        row = yy * 4 + ll * 2 + kk
        return te.at[NB + row] if which == 0 else ti.at[row]

    gathers = {}

    def hop(name, which, yy, ll, device):
        at = tile_at(which, yy, ll, k)
        number = len(gathers)
        cp = copy(at, at, s_gather.at[number], r_gather.at[number], device)
        gathers[name] = (number, cp)
        cp.start()

    def arrived(name, which, yy, ll):
        number, cp = gathers[name]
        at = tile_at(which, yy, ll, k)
        copy(at, at, s_gather.at[number], r_gather.at[number], up).wait_recv()
        spread(which, yy, ll)

    core_sent = []
    halo_sent = []

    def spread(which, yy, ll):
        number = len(core_sent)
        at = tile_at(which, yy, ll, k)
        slot = which * 8 + yy * 2 + ll
        cp = copy(at, at, s_core.at[number], r_core.at[slot], other)
        core_sent.append(cp)
        cp.start()
        if which == 0:
            @pl.when(yy == 3)
            def _():
                copy(at, te.at[ll * 2 + k], s_halo.at[0, ll], r_halo.at[0, ll], block(1)).start()

            @pl.when(yy == 0)
            def _():
                copy(at, te.at[NB + RT + ll * 2 + k], s_halo.at[1, ll], r_halo.at[1, ll], block(-1)).start()

    te[NB + s] = te_ref[0]
    ti[s] = ti_ref[0]
    ym, yp, yo, lo = rem(y - 1, 4), rem(y + 1, 4), rem(y + 2, 4), 1 - l
    for w in range(2):
        hop(("x", w), w, y, l, across)
        hop(("up", w), w, y, l, up)
        hop(("down", w), w, y, l, down)
        spread(w, y, l)
    arrived(("x", 0), 0, y, lo)
    hop(("xup", 0), 0, y, lo, up)
    hop(("xdown", 0), 0, y, lo, down)
    arrived(("up", 0), 0, ym, l)
    hop(("far", 0), 0, ym, l, up)
    arrived(("down", 0), 0, yp, l)
    arrived(("x", 1), 1, y, lo)
    hop(("xup", 1), 1, y, lo, up)
    hop(("xdown", 1), 1, y, lo, down)
    arrived(("down", 1), 1, yp, l)
    hop(("far", 1), 1, yp, l, down)
    arrived(("up", 1), 1, ym, l)
    arrived(("far", 0), 0, yo, l)
    hop(("xfar", 0), 0, yo, l, across)
    arrived(("xup", 0), 0, ym, lo)
    arrived(("xdown", 0), 0, yp, lo)
    arrived(("far", 1), 1, yo, l)
    hop(("xfar", 1), 1, yo, l, across)
    arrived(("xup", 1), 1, ym, lo)
    arrived(("xdown", 1), 1, yp, lo)
    arrived(("xfar", 0), 0, yo, lo)
    arrived(("xfar", 1), 1, yo, lo)
    hcore = []
    for side in range(2):
        for ll in range(2):
            base = 0 if side == 0 else NB + RT
            at = te.at[base + ll * 2 + k]
            copy(at, at, s_halo.at[side, ll], r_halo.at[side, ll], other).wait_recv()
            cp = copy(at, at, s_hcore.at[side, ll], r_hcore.at[side, ll], other)
            cp.start()
            hcore.append(cp)

    for cp in small:
        cp.wait()
    own_idx.wait()
    for side in range(2):
        move = pltpu.make_async_copy(meta_in.at[side], idx.at[2 * side], l_sem.at[1 + side])
        move.start()
        move.wait()
    for i in range(NB):
        half[i] = jnp.broadcast_to(surf_in[0, pl.ds(RT - NB + i, 1), :], (ROWS, TILE))
        half[NB + RT + i] = jnp.broadcast_to(surf_in[1, pl.ds(i, 1), :], (ROWS, TILE))
    for i in range(RT):
        half[NB + i] = jnp.broadcast_to(surf_own[pl.ds(i, 1), :], (ROWS, TILE))

    for _, cp in gathers.values():
        cp.wait_send()
    for cp in core_sent:
        cp.wait_send()
    for w in range(2):
        for yy in range(4):
            for ll in range(2):
                at = tile_at(w, yy, ll, 1 - k)
                copy(at, at, s_core.at[0], r_core.at[w * 8 + yy * 2 + ll], other).wait_recv()
    for side in range(2):
        for ll in range(2):
            at = te.at[ll]
            copy(at, at, s_halo.at[side, ll], r_halo.at[side, ll], other).wait_send()
    for cp in hcore:
        cp.wait()

    def exchange_at(n, w):
        t = x[RT + w]
        th = jnp.tanh(t)
        hs = half[w]
        gas[n, w] = hs * (air - t * (1.0 + buffer_gain * th))
        bend[n, w] = hs * piston * (1.0 + buffer_gain * th + buffer_gain * t * (1.0 - th * th))

    wide_rows = []
    for r in range(NB):
        wide_rows.append((r, 0, 3, r, -LOW))
    for r in range(RT):
        wide_rows.append((NB + r, 1, r // 4, r % 4, NB))
    for r in range(NB):
        wide_rows.append((NB + RT + r, 2, 0, r, NB + RT))

    def forward_row(tiles, row, field, owner, group, place, shift):
        picked = [field[idx[owner, 0, group, place * K + j] + shift] for j in range(K)]
        values = jnp.concatenate(picked, axis=1).astype(bf16)
        weights = jnp.concatenate([tiles[row, j] for j in range(K)], axis=1)
        return lax.dot_general(values, weights, (((1,), (1,)), ((), ())), preferred_element_type=f32)

    @pl.loop(0, STEPS)
    def _(n):
        slot = lax.rem(n, 2)
        for i in range(RT):
            exchange_at(n, NB + i)
        for cp in state_copies(slot):
            cp.wait_recv()
        for j in range(RT // 2):
            for side, base in ((0, NB), (1, EDGE + RT)):
                pair = recv1[slot, side, j].astype(f32)
                x[base + 2 * j] = pair[:ROWS]
                x[base + 2 * j + 1] = pair[ROWS:]
        for j in range(half_nb):
            for side, base in ((0, 0), (1, EDGE + RT + RT)):
                pair = recv2[slot, side, j].astype(f32)
                x[base + 2 * j] = pair[:ROWS]
                x[base + 2 * j + 1] = pair[ROWS:]
        for i in range(NB):
            exchange_at(n, i)
            exchange_at(n, NB + RT + i)
        for row, owner, group, place, shift in wide_rows:
            moved = forward_row(te, row, x, owner, group, place, shift)
            src[row] = moved + piston * gas[n, row]
        for r in range(RT):
            x[EDGE + r] = forward_row(ti, r, src, 1, 4 + r // 4, r % 4, -LOW)

        @pl.when(n < STEPS - 1)
        def _():
            @pl.when(n > 0)
            def _():
                for cp in state_copies(1 - slot):
                    cp.wait_send()

            pack_state(1 - slot)
            for cp in state_copies(1 - slot):
                cp.start()

    for slot in range(2):
        for cp in state_copies(slot):
            cp.wait_send()
    for i in range(RT):
        final_ref[:, i * TILE:(i + 1) * TILE] = x[EDGE + i]

    def segments(first, number, owner, group):
        total = None
        for p in range(GROUP):
            value = contrib[first + idx[owner, 1, group, p]]
            if p > 0:
                value = value + total * idx[owner, 2, group, p].astype(f32)
            total = value
            seg[number * SEG + p] = total

    def landed(number, owner, group, w):
        return seg[number * SEG + idx[owner, 3, group, w]]

    def adjoint_row(tiles, row, field):
        weights = jnp.concatenate([tiles[row, j] for j in range(K)], axis=1)
        spread_out = jnp.dot(field.astype(bf16), weights, preferred_element_type=f32)
        for j in range(K):
            contrib[row * K + j] = spread_out[:, j * TILE:(j + 1) * TILE]

    def adjoint_copies(slot):
        return [
            copy(out1.at[slot, 0], in1.at[slot, 1], s_adj.at[slot, 0], r_adj.at[slot, 1], block(-1)),
            copy(out1.at[slot, 1], in1.at[slot, 0], s_adj.at[slot, 1], r_adj.at[slot, 0], block(1)),
            copy(out2.at[slot, 0], in2.at[slot, 1], s_adj.at[slot, 2], r_adj.at[slot, 3], block(-2)),
            copy(out2.at[slot, 1], in2.at[slot, 0], s_adj.at[slot, 3], r_adj.at[slot, 2], block(2)),
        ]

    def grad_copy(d):
        return copy(gacc, gin.at[c], s_grad.at[d], r_grad.at[c], block(d))

    @pl.loop(0, STEPS)
    def _(back):
        n = STEPS - 1 - back
        slot = lax.rem(back, 2)
        for r in range(RT):
            adjoint_row(ti, r, a[r])
        for g in range(4):
            segments(g * GROUP, g, 1, 4 + g)
        grad = gacc[...]
        for w in range(WIN):
            upper = landed(0, 1, 4, w)
            for g in range(1, 4):
                upper = upper + landed(g, 1, 4 + g, w)
            u[w] = upper
            grad = grad + upper * gas[n, w]
        gacc[...] = grad

        @pl.when(back == STEPS - 1)
        def _():
            for d in range(1, n_cells):
                grad_copy(d).start()

        for r in range(WIN):
            adjoint_row(te, r, u[r])
        segments(0, 0, 0, 3)
        for g in range(4):
            segments((1 + g) * GROUP, 1 + g, 1, g)
        segments(5 * GROUP, 5, 2, 0)

        def wide(i):
            total = None
            terms = []
            if i < WIN:
                terms.append(landed(0, 0, 3, i))
            if RT <= i < RT + WIN:
                for g in range(4):
                    terms.append(landed(1 + g, 1, g, i - RT))
                terms.append(-(bend[n, i - RT] * u[i - RT]))
            if i >= 2 * RT:
                terms.append(landed(5, 2, 0, i - 2 * RT))
            for term in terms:
                total = term if total is None else total + term
            return total

        @pl.when(back > 1)
        def _():
            for cp in adjoint_copies(slot):
                cp.wait_send()

        for j in range(RT // 2):
            for side, base in ((0, NB), (1, EDGE + RT)):
                pair = jnp.concatenate([wide(base + 2 * j), wide(base + 2 * j + 1)], axis=0)
                out1[slot, side, j] = pair.astype(bf16)
        for j in range(half_nb):
            for side, base in ((0, 0), (1, EDGE + 2 * RT)):
                pair = jnp.concatenate([wide(base + 2 * j), wide(base + 2 * j + 1)], axis=0)
                out2[slot, side, j] = pair.astype(bf16)
        copies = adjoint_copies(slot)
        for cp in copies:
            cp.start()
        for i in range(RT):
            part[i] = wide(EDGE + i)
        for cp in copies:
            cp.wait_recv()
        for j in range(RT // 2):
            both = in1[slot, 0, j].astype(f32) + in1[slot, 1, j].astype(f32)
            if j < half_nb:
                both = both + in2[slot, 0, j].astype(f32)
            if j >= RT // 2 - half_nb:
                both = both + in2[slot, 1, j - (RT // 2 - half_nb)].astype(f32)
            a[2 * j] = part[2 * j] + both[:ROWS]
            a[2 * j + 1] = part[2 * j + 1] + both[ROWS:]

    for slot in range(2):
        for cp in adjoint_copies(slot):
            cp.wait_send()
    for i in range(RT):
        adj_ref[:, i * TILE:(i + 1) * TILE] = a[i]
    total = gacc[...]
    for d in range(1, n_cells):
        source = rem(c - d, n_cells)
        copy(gacc, gin.at[source], s_grad.at[d], r_grad.at[source], block(d)).wait_recv()
        total = total + gin[source]
    for d in range(1, n_cells):
        grad_copy(d).wait_send()
    scale = 1.0 / math.sqrt(n_cells * RT * TILE)
    grad_ref[...] = jnp.broadcast_to(jnp.sum(total, axis=1, keepdims=True) * scale, (ROWS, TILE))


def solution(mesh):
    n_cells = mesh.shape["cells"]

    def body(init_state, tiles_exp, cols_exp, tiles_imp, cols_imp, surface, piston, atmosphere, final_cot):
        cols = jnp.concatenate([cols_exp.reshape(4, GROUP), cols_imp.reshape(4, GROUP)], axis=0)
        cols = jnp.pad(cols, ((0, 0), (0, TILE - GROUP)))
        vmem, smem = pl.BlockSpec(memory_space=pltpu.VMEM), pl.BlockSpec(memory_space=pltpu.SMEM)
        dma, i32 = pltpu.SemaphoreType.DMA, jnp.int32
        scratch = [
            pltpu.VMEM((WIN, K, TILE, TILE), bf16),
            pltpu.VMEM((RT, K, TILE, TILE), bf16),
            pltpu.VMEM((WIDE, ROWS, TILE), f32),
            pltpu.VMEM((WIN, ROWS, TILE), f32),
            pltpu.VMEM((STEPS, WIN, ROWS, TILE), f32),
            pltpu.VMEM((STEPS, WIN, ROWS, TILE), f32),
            pltpu.VMEM((WIN, ROWS, TILE), f32),
            pltpu.VMEM((4, 8, TILE), i32),
            pltpu.VMEM((2, 4, 8, TILE), i32),
            pltpu.SMEM((3, 4, 8, TILE), i32),
            pltpu.VMEM((RT, TILE), f32),
            pltpu.VMEM((2, RT, TILE), f32),
            pltpu.VMEM((2, RT // 2, 2 * ROWS, TILE), bf16),
            pltpu.VMEM((2, 2, RT // 2, 2 * ROWS, TILE), bf16),
            pltpu.VMEM((2, 2, NB // 2, 2 * ROWS, TILE), bf16),
            pltpu.VMEM((RT, ROWS, TILE), f32),
            pltpu.VMEM((WIN, ROWS, TILE), f32),
            pltpu.VMEM((RT, ROWS, TILE), f32),
            pltpu.VMEM((WIN * K, ROWS, TILE), f32),
            pltpu.VMEM((6 * SEG, ROWS, TILE), f32),
            pltpu.VMEM((2, 2, RT // 2, 2 * ROWS, TILE), bf16),
            pltpu.VMEM((2, 2, NB // 2, 2 * ROWS, TILE), bf16),
            pltpu.VMEM((2, 2, RT // 2, 2 * ROWS, TILE), bf16),
            pltpu.VMEM((2, 2, NB // 2, 2 * ROWS, TILE), bf16),
            pltpu.VMEM((ROWS, TILE), f32),
            pltpu.VMEM((n_cells, ROWS, TILE), f32),
            dma((4,)), dma((4,)), dma((3,)),
            dma((14,)), dma((14,)), dma((16,)), dma((16,)),
            dma((2, 2)), dma((2, 2)), dma((2, 2)), dma((2, 2)),
            dma((2, 4)), dma((2, 4)), dma((2, 4)), dma((2, 4)),
            dma((n_cells,)), dma((n_cells,)),
        ]

        def run(*refs):
            kernel(n_cells, *refs)

        state = jax.ShapeDtypeStruct((ROWS, RT * TILE), f32)
        final, adjoint, grad = pl.pallas_call(
            run,
            out_shape=(state, state, jax.ShapeDtypeStruct((ROWS, TILE), f32)),
            in_specs=[vmem, vmem, vmem, vmem, vmem, smem, smem, vmem],
            out_specs=(vmem, vmem, vmem),
            scratch_shapes=scratch,
            compiler_params=pltpu.CompilerParams(
                collective_id=0, has_side_effects=True, vmem_limit_bytes=48 << 20
            ),
        )(
            init_state, tiles_exp, tiles_imp, cols, surface.reshape(RT, TILE),
            piston, atmosphere, final_cot,
        )
        return final, adjoint, grad[:, 0]

    placed = (
        P("samples", "cells"),
        P(("cells", "samples"), None, None, None),
        P("cells", None),
        P(("cells", "samples"), None, None, None),
        P("cells", None),
        P("cells"),
        P("samples"),
        P("samples"),
        P("samples", "cells"),
    )
    return jax.shard_map(
        body,
        mesh=mesh,
        in_specs=placed,
        out_specs=(P("samples", "cells"), P("samples", "cells"), P("samples")),
        check_vma=False,
    )
```

```python
import math

import jax
import jax.numpy as jnp
from jax import lax
from jax.experimental import pallas as pl
from jax.experimental.pallas import tpu as pltpu
from jax.sharding import PartitionSpec as P

STEPS = 8
RT = 16
K = 6
NB = 4
TILE = 128
ROWS = 8
GROUP = 4 * K
WIN = RT + 2 * NB
WIDE = WIN + 2 * RT
LOW = RT - NB
EDGE = RT + NB
SEG = GROUP + 1

step_length = 0.5
buffer_gain = 0.5
MESH = pl.DeviceIdType.MESH
f32, bf16 = jnp.float32, jnp.bfloat16


def kernel(
    n_cells,
    init_ref, te_ref, ti_ref, cols_exp_ref, cols_imp_ref, surf_ref, piston_ref, air_ref, cot_ref,
    final_ref, adj_ref, grad_ref,
    te, ti, x, src, gas, bend, half, meta, meta_in, idx,
    surf_own, surf_in, send1, recv1, recv2, a, u, part, contrib, seg,
    out1, out2, in1, in2, gacc, gin, levels, levels_in, levels_used, states, leaving, surf_int, grad_out, grad_in,
    s_swap, r_swap, s_small, r_small, l_sem, s_gather, r_gather, s_core, r_core, s_halo, r_halo, s_hcore, r_hcore,
    s_fwd, r_fwd, s_adj, r_adj, s_grad, r_grad,
):
    c = lax.axis_index("cells")
    s = lax.axis_index("samples")
    y, l, k = s // 4, (s // 2) % 2, s % 2

    def rem(v, m):
        return lax.rem(v + m, m)

    def block(delta):
        return (rem(c + delta, n_cells), s if delta % 2 == 0 else s + 3 - 2 * (s % 4))

    def plane(yy, ll, kk):
        return (c, yy * 4 + ll * 2 + kk)

    up, down = plane(rem(y + 1, 4), l, k), plane(rem(y - 1, 4), l, k)
    across, other = plane(y, 1 - l, k), plane(y, l, 1 - k)
    partner = plane(y, 1 - l, 1 - k)
    odd = lax.rem(c, 2) == 1

    def copy(source, target, send, recv, device):
        return pltpu.make_async_remote_copy(source, target, send, recv, device_id=device, device_id_type=MESH)

    barrier = pltpu.get_barrier_semaphore()
    peers = [up, down, across, other, partner] + [block(d) for d in range(1, n_cells)]
    for device in peers:
        pl.semaphore_signal(barrier, inc=1, device_id=device, device_id_type=MESH)

    own_tiles = [
        pltpu.make_async_copy(te_ref.at[0], te.at[NB + s], l_sem.at[0]),
        pltpu.make_async_copy(ti_ref.at[0], ti.at[s], l_sem.at[1]),
    ]
    for cp in own_tiles:
        cp.start()
    surf_copy = pltpu.make_async_copy(surf_ref, surf_int, l_sem.at[2])
    surf_copy.start()
    stay = [
        pltpu.make_async_copy(init_ref, states.at[0], l_sem.at[3]),
        pltpu.make_async_copy(cot_ref, states.at[1], l_sem.at[4]),
    ]

    @pl.when(jnp.logical_not(odd))
    def _():
        for cp in stay:
            cp.start()

    row_of = lax.broadcasted_iota(jnp.int32, (ROWS, TILE), 0)
    piston = jnp.zeros((ROWS, TILE), f32)
    air = jnp.zeros((ROWS, TILE), f32)
    for i in range(ROWS):
        piston = jnp.where(row_of == i, piston_ref[i], piston)
        air = jnp.where(row_of == i, air_ref[i], air)
    levels[0] = piston
    levels[1] = air
    gacc[...] = jnp.zeros((ROWS, TILE), f32)
    for g in range(6):
        seg[g * SEG + GROUP] = jnp.zeros((ROWS, TILE), f32)

    lane = lax.broadcasted_iota(jnp.int32, (8, TILE), 1)
    spot = lax.broadcasted_iota(jnp.int32, (8, TILE), 0) * TILE + lane
    cols = jnp.zeros((8, TILE), jnp.int32)
    for m, ref in enumerate((cols_exp_ref, cols_imp_ref)):
        for r in range(RT):
            for j in range(K):
                cols = jnp.where(spot == (4 * m + r // 4) * TILE + (r % 4) * K + j, ref[r, j], cols)
    cols = jnp.clip(cols, LOW, LOW + WIN - 1)
    key = cols * 32 + lane
    rank = jnp.zeros((8, TILE), jnp.int32)
    upto = jnp.zeros((8, TILE), jnp.int32)
    here = jnp.zeros((8, TILE), jnp.int32)
    for i in range(GROUP):
        one = jnp.broadcast_to(cols[:, i:i + 1], (8, TILE))
        rank = rank + jnp.where(one * 32 + i < key, 1, 0)
        upto = upto + jnp.where(one - LOW <= lane, 1, 0)
        here = here + jnp.where(one - LOW == lane, 1, 0)
    order = jnp.zeros((8, TILE), jnp.int32)
    ordered = jnp.zeros((8, TILE), jnp.int32)
    before = jnp.zeros((8, TILE), jnp.int32)
    for i in range(GROUP):
        place = jnp.broadcast_to(rank[:, i:i + 1], (8, TILE))
        one = jnp.broadcast_to(cols[:, i:i + 1], (8, TILE))
        order = order + jnp.where(place == lane, i, 0)
        ordered = ordered + jnp.where(place == lane, one, 0)
        before = before + jnp.where(place + 1 == lane, one, 0)
    meta[0] = cols
    meta[1] = order
    meta[2] = jnp.where(ordered == before, 1, 0)
    meta[3] = jnp.where(here > 0, upto - 1, GROUP)

    def pack_state(slot):
        for j in range(RT // 2):
            pair = jnp.concatenate([x[EDGE + 2 * j], x[EDGE + 2 * j + 1]], axis=0)
            send1[slot, j] = pair.astype(bf16)

    half_nb = NB // 2

    def state_copies(slot):
        mine = send1.at[slot]
        return [
            copy(mine, recv1.at[slot, 1], s_fwd.at[slot, 0], r_fwd.at[slot, 1], block(-1)),
            copy(mine, recv1.at[slot, 0], s_fwd.at[slot, 1], r_fwd.at[slot, 0], block(1)),
            copy(mine.at[pl.ds(0, half_nb)], recv2.at[slot, 1], s_fwd.at[slot, 2], r_fwd.at[slot, 3], block(-2)),
            copy(mine.at[pl.ds(RT // 2 - half_nb, half_nb)], recv2.at[slot, 0], s_fwd.at[slot, 3], r_fwd.at[slot, 2], block(2)),
        ]

    surf_copy.wait()
    surf_own[...] = surf_int[...].astype(f32) * step_length
    pl.semaphore_wait(barrier, len(peers))
    swap = [
        copy(init_ref, states.at[0], s_swap.at[0], r_swap.at[0], partner),
        copy(cot_ref, states.at[1], s_swap.at[1], r_swap.at[1], partner),
        copy(levels, levels_in, s_swap.at[2], r_swap.at[2], partner),
    ]

    @pl.when(odd)
    def _():
        for cp in swap:
            cp.start()


    small = []
    for side, device in ((0, block(1)), (1, block(-1))):
        small.append(copy(surf_own, surf_in.at[side], s_small.at[side], r_small.at[side], device))
        small.append(copy(meta, meta_in.at[side], s_small.at[2 + side], r_small.at[2 + side], device))
    for cp in small:
        cp.start()
    own_idx = pltpu.make_async_copy(meta, idx.at[1], l_sem.at[2])
    own_idx.start()

    buf = (te, ti)

    def tile_at(which, yy, ll, kk):
        row = yy * 4 + ll * 2 + kk
        return te.at[NB + row] if which == 0 else ti.at[row]

    gathers = {}

    def hop(name, which, yy, ll, device, source=None):
        at = tile_at(which, yy, ll, k)
        number = len(gathers)
        cp = copy(at if source is None else source, at, s_gather.at[number], r_gather.at[number], device)
        gathers[name] = (number, cp)
        cp.start()

    def arrived(name, which, yy, ll):
        number, cp = gathers[name]
        at = tile_at(which, yy, ll, k)
        copy(at, at, s_gather.at[number], r_gather.at[number], up).wait_recv()
        spread(which, yy, ll)

    core_sent = []
    halo_sent = []

    def spread(which, yy, ll):
        number = len(core_sent)
        at = tile_at(which, yy, ll, k)
        slot = which * 8 + yy * 2 + ll
        cp = copy(at, at, s_core.at[number], r_core.at[slot], other)
        core_sent.append(cp)
        cp.start()
        if which == 0:
            @pl.when(yy == 3)
            def _():
                copy(at, te.at[ll * 2 + k], s_halo.at[0, ll], r_halo.at[0, ll], block(1)).start()

            @pl.when(yy == 0)
            def _():
                copy(at, te.at[NB + RT + ll * 2 + k], s_halo.at[1, ll], r_halo.at[1, ll], block(-1)).start()

    ym, yp, yo, lo = rem(y - 1, 4), rem(y + 1, 4), rem(y + 2, 4), 1 - l
    for w, own in enumerate((te_ref.at[0], ti_ref.at[0])):
        hop(("up", w), w, y, l, up, own)
        hop(("down", w), w, y, l, down, own)
        hop(("x", w), w, y, l, across, own)
    for w in range(2):
        own_tiles[w].wait()
        spread(w, y, l)

    @pl.when(odd)
    def _():
        for cp in swap:
            cp.wait_recv()
        levels_used[...] = levels_in[...]

    @pl.when(jnp.logical_not(odd))
    def _():
        for cp in stay:
            cp.wait()
        levels_used[...] = levels[...]

    piston = levels_used[0]
    air = levels_used[1]
    for i in range(RT):
        x[EDGE + i] = states[0, :, i * TILE:(i + 1) * TILE]
        a[i] = states[1, :, i * TILE:(i + 1) * TILE]
    pack_state(0)
    for cp in state_copies(0):
        cp.start()

    arrived(("up", 0), 0, ym, l)
    hop(("far", 0), 0, ym, l, up)
    arrived(("x", 0), 0, y, lo)
    hop(("xup", 0), 0, y, lo, up)
    hop(("xdown", 0), 0, y, lo, down)
    arrived(("down", 0), 0, yp, l)
    arrived(("down", 1), 1, yp, l)
    hop(("far", 1), 1, yp, l, down)
    arrived(("x", 1), 1, y, lo)
    hop(("xup", 1), 1, y, lo, up)
    hop(("xdown", 1), 1, y, lo, down)
    arrived(("up", 1), 1, ym, l)
    arrived(("far", 0), 0, yo, l)
    hop(("xfar", 0), 0, yo, l, across)
    arrived(("xup", 0), 0, ym, lo)
    arrived(("xdown", 0), 0, yp, lo)
    arrived(("far", 1), 1, yo, l)
    hop(("xfar", 1), 1, yo, l, across)
    arrived(("xup", 1), 1, ym, lo)
    arrived(("xdown", 1), 1, yp, lo)
    arrived(("xfar", 0), 0, yo, lo)
    arrived(("xfar", 1), 1, yo, lo)
    hcore = []
    for side in range(2):
        for ll in range(2):
            base = 0 if side == 0 else NB + RT
            at = te.at[base + ll * 2 + 1 - k]
            copy(at, at, s_halo.at[side, ll], r_halo.at[side, ll], other).wait_recv()
            cp = copy(at, at, s_hcore.at[side, ll], r_hcore.at[side, ll], other)
            cp.start()
            hcore.append(cp)

    for cp in small:
        cp.wait()
    own_idx.wait()
    for side in range(2):
        move = pltpu.make_async_copy(meta_in.at[side], idx.at[2 * side], l_sem.at[3 + side])
        move.start()
        move.wait()
    for i in range(NB):
        half[i] = jnp.broadcast_to(surf_in[0, pl.ds(RT - NB + i, 1), :], (ROWS, TILE))
        half[NB + RT + i] = jnp.broadcast_to(surf_in[1, pl.ds(i, 1), :], (ROWS, TILE))
    for i in range(RT):
        half[NB + i] = jnp.broadcast_to(surf_own[pl.ds(i, 1), :], (ROWS, TILE))

    @pl.when(odd)
    def _():
        for cp in swap:
            cp.wait_send()

    for _, cp in gathers.values():
        cp.wait_send()
    for cp in core_sent:
        cp.wait_send()
    for w in range(2):
        for yy in range(4):
            for ll in range(2):
                at = tile_at(w, yy, ll, 1 - k)
                copy(at, at, s_core.at[0], r_core.at[w * 8 + yy * 2 + ll], other).wait_recv()
    for side in range(2):
        for ll in range(2):
            at = te.at[ll]
            copy(at, at, s_halo.at[side, ll], r_halo.at[side, ll], other).wait_send()
    for cp in hcore:
        cp.wait()

    def exchange_at(n, w):
        t = x[RT + w]
        th = jnp.tanh(t)
        hs = half[w]
        gas[n, w] = hs * (air - t * (1.0 + buffer_gain * th))
        bend[n, w] = hs * piston * (1.0 + buffer_gain * th + buffer_gain * t * (1.0 - th * th))

    wide_rows = []
    for r in range(NB):
        wide_rows.append((r, 0, 3, r, -LOW))
    for r in range(RT):
        wide_rows.append((NB + r, 1, r // 4, r % 4, NB))
    for r in range(NB):
        wide_rows.append((NB + RT + r, 2, 0, r, NB + RT))

    def forward_row(tiles, row, field, owner, group, place, shift):
        picked = [field[idx[owner, 0, group, place * K + j] + shift] for j in range(K)]
        values = jnp.concatenate(picked, axis=1).astype(bf16)
        weights = jnp.concatenate([tiles[row, j] for j in range(K)], axis=1)
        return lax.dot_general(values, weights, (((1,), (1,)), ((), ())), preferred_element_type=f32)

    @pl.loop(0, STEPS)
    def _(n):
        slot = lax.rem(n, 2)
        for i in range(RT):
            exchange_at(n, NB + i)
        for cp in state_copies(slot):
            cp.wait_recv()
        for j in range(RT // 2):
            for side, base in ((0, NB), (1, EDGE + RT)):
                pair = recv1[slot, side, j].astype(f32)
                x[base + 2 * j] = pair[:ROWS]
                x[base + 2 * j + 1] = pair[ROWS:]
        for j in range(half_nb):
            for side, base in ((0, 0), (1, EDGE + RT + RT)):
                pair = recv2[slot, side, j].astype(f32)
                x[base + 2 * j] = pair[:ROWS]
                x[base + 2 * j + 1] = pair[ROWS:]
        for i in range(NB):
            exchange_at(n, i)
            exchange_at(n, NB + RT + i)
        for row, owner, group, place, shift in wide_rows:
            moved = forward_row(te, row, x, owner, group, place, shift)
            src[row] = moved + piston * gas[n, row]
        for r in range(RT):
            x[EDGE + r] = forward_row(ti, r, src, 1, 4 + r // 4, r % 4, -LOW)

        @pl.when(n < STEPS - 1)
        def _():
            @pl.when(n > 0)
            def _():
                for cp in state_copies(1 - slot):
                    cp.wait_send()

            pack_state(1 - slot)
            for cp in state_copies(1 - slot):
                cp.start()

    for slot in range(2):
        for cp in state_copies(slot):
            cp.wait_send()
    final_copy = copy(leaving.at[0], final_ref, s_swap.at[0], r_swap.at[0], partner)
    adj_copy = copy(leaving.at[1], adj_ref, s_swap.at[1], r_swap.at[1], partner)
    grad_swap = copy(grad_out, grad_in, s_swap.at[2], r_swap.at[2], partner)

    @pl.when(odd)
    def _():
        for i in range(RT):
            leaving[0, :, i * TILE:(i + 1) * TILE] = x[EDGE + i]
        final_copy.start()

    @pl.when(jnp.logical_not(odd))
    def _():
        for i in range(RT):
            final_ref[:, i * TILE:(i + 1) * TILE] = x[EDGE + i]


    def segments(first, number, owner, group):
        total = None
        for p in range(GROUP):
            value = contrib[first + idx[owner, 1, group, p]]
            if p > 0:
                value = value + total * idx[owner, 2, group, p].astype(f32)
            total = value
            seg[number * SEG + p] = total

    def landed(number, owner, group, w):
        return seg[number * SEG + idx[owner, 3, group, w]]

    def adjoint_row(tiles, row, field):
        weights = jnp.concatenate([tiles[row, j] for j in range(K)], axis=1)
        spread_out = jnp.dot(field.astype(bf16), weights, preferred_element_type=f32)
        for j in range(K):
            contrib[row * K + j] = spread_out[:, j * TILE:(j + 1) * TILE]

    def adjoint_copies(slot):
        return [
            copy(out1.at[slot, 0], in1.at[slot, 1], s_adj.at[slot, 0], r_adj.at[slot, 1], block(-1)),
            copy(out1.at[slot, 1], in1.at[slot, 0], s_adj.at[slot, 1], r_adj.at[slot, 0], block(1)),
            copy(out2.at[slot, 0], in2.at[slot, 1], s_adj.at[slot, 2], r_adj.at[slot, 3], block(-2)),
            copy(out2.at[slot, 1], in2.at[slot, 0], s_adj.at[slot, 3], r_adj.at[slot, 2], block(2)),
        ]

    def grad_copy(d):
        return copy(gacc, gin.at[c], s_grad.at[d], r_grad.at[c], block(d))

    @pl.loop(0, STEPS)
    def _(back):
        n = STEPS - 1 - back
        slot = lax.rem(back, 2)
        for r in range(RT):
            adjoint_row(ti, r, a[r])
        for g in range(4):
            segments(g * GROUP, g, 1, 4 + g)
        grad = gacc[...]
        for w in range(WIN):
            upper = landed(0, 1, 4, w)
            for g in range(1, 4):
                upper = upper + landed(g, 1, 4 + g, w)
            u[w] = upper
            grad = grad + upper * gas[n, w]
        gacc[...] = grad

        @pl.when(back == STEPS - 1)
        def _():
            for d in range(1, n_cells):
                grad_copy(d).start()

        for r in range(WIN):
            adjoint_row(te, r, u[r])
        segments(0, 0, 0, 3)
        for g in range(4):
            segments((1 + g) * GROUP, 1 + g, 1, g)
        segments(5 * GROUP, 5, 2, 0)

        def wide(i):
            total = None
            terms = []
            if i < WIN:
                terms.append(landed(0, 0, 3, i))
            if RT <= i < RT + WIN:
                for g in range(4):
                    terms.append(landed(1 + g, 1, g, i - RT))
                terms.append(-(bend[n, i - RT] * u[i - RT]))
            if i >= 2 * RT:
                terms.append(landed(5, 2, 0, i - 2 * RT))
            for term in terms:
                total = term if total is None else total + term
            return total

        @pl.when(back > 1)
        def _():
            for cp in adjoint_copies(slot):
                cp.wait_send()

        for j in range(RT // 2):
            for side, base in ((0, NB), (1, EDGE + RT)):
                pair = jnp.concatenate([wide(base + 2 * j), wide(base + 2 * j + 1)], axis=0)
                out1[slot, side, j] = pair.astype(bf16)
        for j in range(half_nb):
            for side, base in ((0, 0), (1, EDGE + 2 * RT)):
                pair = jnp.concatenate([wide(base + 2 * j), wide(base + 2 * j + 1)], axis=0)
                out2[slot, side, j] = pair.astype(bf16)
        copies = adjoint_copies(slot)
        for cp in copies:
            cp.start()
        for i in range(RT):
            part[i] = wide(EDGE + i)
        for cp in copies:
            cp.wait_recv()
        for j in range(RT // 2):
            both = in1[slot, 0, j].astype(f32) + in1[slot, 1, j].astype(f32)
            if j < half_nb:
                both = both + in2[slot, 0, j].astype(f32)
            if j >= RT // 2 - half_nb:
                both = both + in2[slot, 1, j - (RT // 2 - half_nb)].astype(f32)
            a[2 * j] = part[2 * j] + both[:ROWS]
            a[2 * j + 1] = part[2 * j + 1] + both[ROWS:]

    @pl.when(odd)
    def _():
        for i in range(RT):
            leaving[1, :, i * TILE:(i + 1) * TILE] = a[i]
        adj_copy.start()

    @pl.when(jnp.logical_not(odd))
    def _():
        for i in range(RT):
            adj_ref[:, i * TILE:(i + 1) * TILE] = a[i]

    total = gacc[...]
    for d in range(1, n_cells):
        source = rem(c - d, n_cells)
        copy(gacc, gin.at[source], s_grad.at[d], r_grad.at[source], block(d)).wait_recv()
        total = total + gin[source]
    scale = 1.0 / math.sqrt(n_cells * RT * TILE)
    grad_out[...] = jnp.broadcast_to(jnp.sum(total, axis=1, keepdims=True) * scale, (ROWS, TILE))

    @pl.when(odd)
    def _():
        grad_swap.start()

    for d in range(1, n_cells):
        grad_copy(d).wait_send()
    for slot in range(2):
        for cp in adjoint_copies(slot):
            cp.wait_send()

    @pl.when(odd)
    def _():
        grad_swap.wait()
        final_copy.wait()
        adj_copy.wait()
        grad_ref[...] = grad_in[...]

    @pl.when(jnp.logical_not(odd))
    def _():
        grad_ref[...] = grad_out[...]


def solution(mesh):
    n_cells = mesh.shape["cells"]

    def body(init_state, tiles_exp, cols_exp, tiles_imp, cols_imp, surface, piston, atmosphere, final_cot):
        vmem, smem = pl.BlockSpec(memory_space=pltpu.VMEM), pl.BlockSpec(memory_space=pltpu.SMEM)
        anywhere = pl.BlockSpec(memory_space=pl.ANY)
        dma, i32 = pltpu.SemaphoreType.DMA, jnp.int32
        scratch = [
            pltpu.VMEM((WIN, K, TILE, TILE), bf16),
            pltpu.VMEM((RT, K, TILE, TILE), bf16),
            pltpu.VMEM((WIDE, ROWS, TILE), f32),
            pltpu.VMEM((WIN, ROWS, TILE), f32),
            pltpu.VMEM((STEPS, WIN, ROWS, TILE), f32),
            pltpu.VMEM((STEPS, WIN, ROWS, TILE), f32),
            pltpu.VMEM((WIN, ROWS, TILE), f32),
            pltpu.VMEM((4, 8, TILE), i32),
            pltpu.VMEM((2, 4, 8, TILE), i32),
            pltpu.SMEM((3, 4, 8, TILE), i32),
            pltpu.VMEM((RT, TILE), f32),
            pltpu.VMEM((2, RT, TILE), f32),
            pltpu.VMEM((2, RT // 2, 2 * ROWS, TILE), bf16),
            pltpu.VMEM((2, 2, RT // 2, 2 * ROWS, TILE), bf16),
            pltpu.VMEM((2, 2, NB // 2, 2 * ROWS, TILE), bf16),
            pltpu.VMEM((RT, ROWS, TILE), f32),
            pltpu.VMEM((WIN, ROWS, TILE), f32),
            pltpu.VMEM((RT, ROWS, TILE), f32),
            pltpu.VMEM((WIN * K, ROWS, TILE), f32),
            pltpu.VMEM((6 * SEG, ROWS, TILE), f32),
            pltpu.VMEM((2, 2, RT // 2, 2 * ROWS, TILE), bf16),
            pltpu.VMEM((2, 2, NB // 2, 2 * ROWS, TILE), bf16),
            pltpu.VMEM((2, 2, RT // 2, 2 * ROWS, TILE), bf16),
            pltpu.VMEM((2, 2, NB // 2, 2 * ROWS, TILE), bf16),
            pltpu.VMEM((ROWS, TILE), f32),
            pltpu.VMEM((n_cells, ROWS, TILE), f32),
            pltpu.VMEM((2, ROWS, TILE), f32),
            pltpu.VMEM((2, ROWS, TILE), f32),
            pltpu.VMEM((2, ROWS, TILE), f32),
            pltpu.VMEM((2, ROWS, RT * TILE), f32),
            pltpu.VMEM((2, ROWS, RT * TILE), f32),
            pltpu.VMEM((RT, TILE), i32),
            pltpu.VMEM((ROWS, TILE), f32),
            pltpu.VMEM((ROWS, TILE), f32),
            dma((3,)), dma((3,)),
            dma((4,)), dma((4,)), dma((5,)),
            dma((14,)), dma((14,)), dma((16,)), dma((16,)),
            dma((2, 2)), dma((2, 2)), dma((2, 2)), dma((2, 2)),
            dma((2, 4)), dma((2, 4)), dma((2, 4)), dma((2, 4)),
            dma((n_cells,)), dma((n_cells,)),
        ]

        def run(*refs):
            kernel(n_cells, *refs)

        state = jax.ShapeDtypeStruct((ROWS, RT * TILE), f32)
        final, adjoint, grad = pl.pallas_call(
            run,
            out_shape=(state, state, jax.ShapeDtypeStruct((ROWS, TILE), f32)),
            in_specs=[anywhere, anywhere, anywhere, smem, smem, anywhere, smem, smem, anywhere],
            out_specs=(vmem, vmem, vmem),
            scratch_shapes=scratch,
            compiler_params=pltpu.CompilerParams(
                collective_id=0, has_side_effects=True, vmem_limit_bytes=60 << 20
            ),
        )(
            init_state, tiles_exp, tiles_imp, cols_exp, cols_imp, surface.reshape(RT, TILE),
            piston, atmosphere, final_cot,
        )
        return final, adjoint, grad[:, 0]

    placed = (
        P("samples", "cells"),
        P(("cells", "samples"), None, None, None),
        P("cells", None),
        P(("cells", "samples"), None, None, None),
        P("cells", None),
        P("cells"),
        P("samples"),
        P("samples"),
        P("samples", "cells"),
    )
    return jax.shard_map(
        body,
        mesh=mesh,
        in_specs=placed,
        out_specs=(P("samples", "cells"), P("samples", "cells"), P("samples")),
        check_vma=False,
    )
```

```python
import math

import jax
import jax.numpy as jnp
from jax import lax
from jax.experimental import pallas as pl
from jax.experimental.pallas import tpu as pltpu
from jax.sharding import PartitionSpec as P

STEPS = 8
RT = 16
K = 6
NB = 4
TILE = 128
ROWS = 8
GROUP = 4 * K
WIN = RT + 2 * NB
WIDE = WIN + 2 * RT
LOW = RT - NB
EDGE = RT + NB
SEG = GROUP + 1

step_length = 0.5
buffer_gain = 0.5
MESH = pl.DeviceIdType.MESH
f32, bf16 = jnp.float32, jnp.bfloat16


def kernel(
    n_cells,
    init_ref, te_ref, ti_ref, cols_exp_ref, cols_imp_ref, surf_ref, piston_ref, air_ref, cot_ref,
    final_ref, adj_ref, grad_ref,
    te, ti, x, src, gas, bend, half, meta, meta_in, idx,
    surf_own, surf_in, send1, recv1, recv2, a, u, part, contrib, seg,
    out1, out2, in1, in2, gacc, gin, levels, levels_in, levels_used, states, leaving, surf_int, grad_out, grad_in, upper_out, upper_in, upper_full,
    s_upper, r_upper, s_swap, r_swap, s_small, r_small, l_sem, s_gather, r_gather, s_core, r_core, s_halo, r_halo, s_hcore, r_hcore,
    s_fwd, r_fwd, s_adj, r_adj, s_grad, r_grad,
):
    c = lax.axis_index("cells")
    s = lax.axis_index("samples")
    y, l, k = s // 4, (s // 2) % 2, s % 2

    def rem(v, m):
        return lax.rem(v + m, m)

    def block(delta):
        return (rem(c + delta, n_cells), s if delta % 2 == 0 else s + 3 - 2 * (s % 4))

    def plane(yy, ll, kk):
        return (c, yy * 4 + ll * 2 + kk)

    up, down = plane(rem(y + 1, 4), l, k), plane(rem(y - 1, 4), l, k)
    across, other = plane(y, 1 - l, k), plane(y, l, 1 - k)
    partner = plane(y, 1 - l, 1 - k)
    odd = lax.rem(c, 2) == 1

    def copy(source, target, send, recv, device):
        return pltpu.make_async_remote_copy(source, target, send, recv, device_id=device, device_id_type=MESH)

    barrier = pltpu.get_barrier_semaphore()
    peers = [up, down, across, other, partner] + [block(d) for d in range(1, n_cells)]
    for device in peers:
        pl.semaphore_signal(barrier, inc=1, device_id=device, device_id_type=MESH)

    own_tiles = [
        pltpu.make_async_copy(te_ref.at[0], te.at[NB + s], l_sem.at[0]),
        pltpu.make_async_copy(ti_ref.at[0], ti.at[s], l_sem.at[1]),
    ]
    for cp in own_tiles:
        cp.start()
    surf_copy = pltpu.make_async_copy(surf_ref, surf_int, l_sem.at[2])
    surf_copy.start()
    stay = [
        pltpu.make_async_copy(init_ref, states.at[0], l_sem.at[3]),
        pltpu.make_async_copy(cot_ref, states.at[1], l_sem.at[4]),
    ]

    @pl.when(jnp.logical_not(odd))
    def _():
        for cp in stay:
            cp.start()

    row_of = lax.broadcasted_iota(jnp.int32, (ROWS, TILE), 0)
    piston = jnp.zeros((ROWS, TILE), f32)
    air = jnp.zeros((ROWS, TILE), f32)
    for i in range(ROWS):
        piston = jnp.where(row_of == i, piston_ref[i], piston)
        air = jnp.where(row_of == i, air_ref[i], air)
    levels[0] = piston
    levels[1] = air
    gacc[...] = jnp.zeros((ROWS, TILE), f32)
    for g in range(6):
        seg[g * SEG + GROUP] = jnp.zeros((ROWS, TILE), f32)

    lane = lax.broadcasted_iota(jnp.int32, (8, TILE), 1)
    spot = lax.broadcasted_iota(jnp.int32, (8, TILE), 0) * TILE + lane
    cols = jnp.zeros((8, TILE), jnp.int32)
    for m, ref in enumerate((cols_exp_ref, cols_imp_ref)):
        for r in range(RT):
            for j in range(K):
                cols = jnp.where(spot == (4 * m + r // 4) * TILE + (r % 4) * K + j, ref[r, j], cols)
    cols = jnp.clip(cols, LOW, LOW + WIN - 1)
    key = cols * 32 + lane
    rank = jnp.zeros((8, TILE), jnp.int32)
    upto = jnp.zeros((8, TILE), jnp.int32)
    here = jnp.zeros((8, TILE), jnp.int32)
    for i in range(GROUP):
        one = jnp.broadcast_to(cols[:, i:i + 1], (8, TILE))
        rank = rank + jnp.where(one * 32 + i < key, 1, 0)
        upto = upto + jnp.where(one - LOW <= lane, 1, 0)
        here = here + jnp.where(one - LOW == lane, 1, 0)
    order = jnp.zeros((8, TILE), jnp.int32)
    ordered = jnp.zeros((8, TILE), jnp.int32)
    before = jnp.zeros((8, TILE), jnp.int32)
    for i in range(GROUP):
        place = jnp.broadcast_to(rank[:, i:i + 1], (8, TILE))
        one = jnp.broadcast_to(cols[:, i:i + 1], (8, TILE))
        order = order + jnp.where(place == lane, i, 0)
        ordered = ordered + jnp.where(place == lane, one, 0)
        before = before + jnp.where(place + 1 == lane, one, 0)
    meta[0] = cols
    meta[1] = order
    meta[2] = jnp.where(ordered == before, 1, 0)
    meta[3] = jnp.where(here > 0, upto - 1, GROUP)

    def pack_state(slot):
        for j in range(RT // 2):
            pair = jnp.concatenate([x[EDGE + 2 * j], x[EDGE + 2 * j + 1]], axis=0)
            send1[slot, j] = pair.astype(bf16)

    half_nb = NB // 2

    def state_copies(slot):
        mine = send1.at[slot]
        return [
            copy(mine, recv1.at[slot, 1], s_fwd.at[slot, 0], r_fwd.at[slot, 1], block(-1)),
            copy(mine, recv1.at[slot, 0], s_fwd.at[slot, 1], r_fwd.at[slot, 0], block(1)),
            copy(mine.at[pl.ds(0, half_nb)], recv2.at[slot, 1], s_fwd.at[slot, 2], r_fwd.at[slot, 3], block(-2)),
            copy(mine.at[pl.ds(RT // 2 - half_nb, half_nb)], recv2.at[slot, 0], s_fwd.at[slot, 3], r_fwd.at[slot, 2], block(2)),
        ]

    surf_copy.wait()
    surf_own[...] = surf_int[...].astype(f32) * step_length
    pl.semaphore_wait(barrier, len(peers))
    swap = [
        copy(init_ref, states.at[0], s_swap.at[0], r_swap.at[0], partner),
        copy(cot_ref, states.at[1], s_swap.at[1], r_swap.at[1], partner),
        copy(levels, levels_in, s_swap.at[2], r_swap.at[2], partner),
    ]

    @pl.when(odd)
    def _():
        for cp in swap:
            cp.start()


    small = []
    for side, device in ((0, block(1)), (1, block(-1))):
        small.append(copy(surf_own, surf_in.at[side], s_small.at[side], r_small.at[side], device))
        small.append(copy(meta, meta_in.at[side], s_small.at[2 + side], r_small.at[2 + side], device))
    for cp in small:
        cp.start()
    own_idx = pltpu.make_async_copy(meta, idx.at[1], l_sem.at[2])
    own_idx.start()

    buf = (te, ti)

    def tile_at(which, yy, ll, kk):
        row = yy * 4 + ll * 2 + kk
        return te.at[NB + row] if which == 0 else ti.at[row]

    gathers = {}

    def hop(name, which, yy, ll, device, source=None):
        at = tile_at(which, yy, ll, k)
        number = len(gathers)
        cp = copy(at if source is None else source, at, s_gather.at[number], r_gather.at[number], device)
        gathers[name] = (number, cp)
        cp.start()

    def arrived(name, which, yy, ll):
        number, cp = gathers[name]
        at = tile_at(which, yy, ll, k)
        copy(at, at, s_gather.at[number], r_gather.at[number], up).wait_recv()
        spread(which, yy, ll)

    core_sent = []
    halo_sent = []

    def spread(which, yy, ll):
        number = len(core_sent)
        at = tile_at(which, yy, ll, k)
        slot = which * 8 + yy * 2 + ll
        cp = copy(at, at, s_core.at[number], r_core.at[slot], other)
        core_sent.append(cp)
        cp.start()
        if which == 0:
            @pl.when(yy == 3)
            def _():
                copy(at, te.at[ll * 2 + k], s_halo.at[0, ll], r_halo.at[0, ll], block(1)).start()

            @pl.when(yy == 0)
            def _():
                copy(at, te.at[NB + RT + ll * 2 + k], s_halo.at[1, ll], r_halo.at[1, ll], block(-1)).start()

    ym, yp, yo, lo = rem(y - 1, 4), rem(y + 1, 4), rem(y + 2, 4), 1 - l
    for w, own in enumerate((te_ref.at[0], ti_ref.at[0])):
        hop(("up", w), w, y, l, up, own)
        hop(("down", w), w, y, l, down, own)
        hop(("x", w), w, y, l, across, own)
    for w in range(2):
        own_tiles[w].wait()
        spread(w, y, l)

    @pl.when(odd)
    def _():
        for cp in swap:
            cp.wait_recv()
        levels_used[...] = levels_in[...]

    @pl.when(jnp.logical_not(odd))
    def _():
        for cp in stay:
            cp.wait()
        levels_used[...] = levels[...]

    piston = levels_used[0]
    air = levels_used[1]
    for i in range(RT):
        x[EDGE + i] = states[0, :, i * TILE:(i + 1) * TILE]
        a[i] = states[1, :, i * TILE:(i + 1) * TILE]
    pack_state(0)
    for cp in state_copies(0):
        cp.start()

    arrived(("up", 0), 0, ym, l)
    hop(("far", 0), 0, ym, l, up)
    hop(("xu", 0), 0, ym, l, across)
    arrived(("x", 0), 0, y, lo)
    hop(("xdown", 0), 0, y, lo, down)
    arrived(("down", 0), 0, yp, l)
    arrived(("x", 1), 1, y, lo)
    hop(("xup", 1), 1, y, lo, up)
    arrived(("down", 1), 1, yp, l)
    hop(("far", 1), 1, yp, l, down)
    hop(("xd", 1), 1, yp, l, across)
    arrived(("up", 1), 1, ym, l)
    arrived(("xu", 0), 0, ym, lo)
    hop(("farx", 0), 0, ym, lo, up)
    arrived(("far", 0), 0, yo, l)
    arrived(("xdown", 0), 0, yp, lo)
    arrived(("xd", 1), 1, yp, lo)
    hop(("farx", 1), 1, yp, lo, down)
    arrived(("farx", 0), 0, yo, lo)
    arrived(("far", 1), 1, yo, l)
    arrived(("xup", 1), 1, ym, lo)
    arrived(("farx", 1), 1, yo, lo)
    hcore = []
    for side in range(2):
        for ll in range(2):
            base = 0 if side == 0 else NB + RT
            at = te.at[base + ll * 2 + 1 - k]
            copy(at, at, s_halo.at[side, ll], r_halo.at[side, ll], other).wait_recv()
            cp = copy(at, at, s_hcore.at[side, ll], r_hcore.at[side, ll], other)
            cp.start()
            hcore.append(cp)

    for cp in small:
        cp.wait()
    own_idx.wait()
    for side in range(2):
        move = pltpu.make_async_copy(meta_in.at[side], idx.at[2 * side], l_sem.at[3 + side])
        move.start()
        move.wait()
    for i in range(NB):
        half[i] = jnp.broadcast_to(surf_in[0, pl.ds(RT - NB + i, 1), :], (ROWS, TILE))
        half[NB + RT + i] = jnp.broadcast_to(surf_in[1, pl.ds(i, 1), :], (ROWS, TILE))
    for i in range(RT):
        half[NB + i] = jnp.broadcast_to(surf_own[pl.ds(i, 1), :], (ROWS, TILE))

    @pl.when(odd)
    def _():
        for cp in swap:
            cp.wait_send()

    for _, cp in gathers.values():
        cp.wait_send()
    for cp in core_sent:
        cp.wait_send()
    for w in range(2):
        for yy in range(4):
            for ll in range(2):
                at = tile_at(w, yy, ll, 1 - k)
                copy(at, at, s_core.at[0], r_core.at[w * 8 + yy * 2 + ll], other).wait_recv()
    for side in range(2):
        for ll in range(2):
            at = te.at[ll]
            copy(at, at, s_halo.at[side, ll], r_halo.at[side, ll], other).wait_send()
    for cp in hcore:
        cp.wait()

    def exchange_at(n, w):
        t = x[RT + w]
        th = jnp.tanh(t)
        hs = half[w]
        gas[n, w] = hs * (air - t * (1.0 + buffer_gain * th))
        bend[n, w] = hs * piston * (1.0 + buffer_gain * th + buffer_gain * t * (1.0 - th * th))

    wide_rows = []
    for r in range(NB):
        wide_rows.append((r, 0, 3, r, -LOW))
    for r in range(RT):
        wide_rows.append((NB + r, 1, r // 4, r % 4, NB))
    for r in range(NB):
        wide_rows.append((NB + RT + r, 2, 0, r, NB + RT))

    def forward_row(tiles, row, field, owner, group, place, shift):
        picked = [field[idx[owner, 0, group, place * K + j] + shift] for j in range(K)]
        values = jnp.concatenate(picked, axis=1).astype(bf16)
        weights = jnp.concatenate([tiles[row, j] for j in range(K)], axis=1)
        return lax.dot_general(values, weights, (((1,), (1,)), ((), ())), preferred_element_type=f32)

    def forward_step(n, slot):
        for cp in state_copies(slot):
            cp.wait_recv()
        for j in range(RT // 2):
            for side, base in ((0, NB), (1, EDGE + RT)):
                pair = recv1[slot, side, j].astype(f32)
                x[base + 2 * j] = pair[:ROWS]
                x[base + 2 * j + 1] = pair[ROWS:]
        for j in range(half_nb):
            for side, base in ((0, 0), (1, EDGE + RT + RT)):
                pair = recv2[slot, side, j].astype(f32)
                x[base + 2 * j] = pair[:ROWS]
                x[base + 2 * j + 1] = pair[ROWS:]
        for i in range(NB):
            exchange_at(n, i)
            exchange_at(n, NB + RT + i)
        for row, owner, group, place, shift in wide_rows:
            moved = forward_row(te, row, x, owner, group, place, shift)
            src[row] = moved + piston * gas[n, row]
        for r in range(RT):
            x[EDGE + r] = forward_row(ti, r, src, 1, 4 + r // 4, r % 4, -LOW)

    def segments(first, number, owner, group):
        total = None
        for p in range(GROUP):
            value = contrib[first + idx[owner, 1, group, p]]
            if p > 0:
                value = value + total * idx[owner, 2, group, p].astype(f32)
            total = value
            seg[number * SEG + p] = total

    def landed(number, owner, group, w):
        return seg[number * SEG + idx[owner, 3, group, w]]

    def adjoint_row(tiles, row, field):
        weights = jnp.concatenate([tiles[row, j] for j in range(K)], axis=1)
        spread_out = jnp.dot(field.astype(bf16), weights, preferred_element_type=f32)
        for j in range(K):
            contrib[row * K + j] = spread_out[:, j * TILE:(j + 1) * TILE]

    def adjoint_copies(slot):
        return [
            copy(out1.at[slot, 0], in1.at[slot, 1], s_adj.at[slot, 0], r_adj.at[slot, 1], block(-1)),
            copy(out1.at[slot, 1], in1.at[slot, 0], s_adj.at[slot, 1], r_adj.at[slot, 0], block(1)),
            copy(out2.at[slot, 0], in2.at[slot, 1], s_adj.at[slot, 2], r_adj.at[slot, 3], block(-2)),
            copy(out2.at[slot, 1], in2.at[slot, 0], s_adj.at[slot, 3], r_adj.at[slot, 2], block(2)),
        ]

    def grad_copy(d):
        return copy(gacc, gin.at[c], s_grad.at[d], r_grad.at[c], block(d))

    def upper_part():
        for r in range(RT):
            adjoint_row(ti, r, a[r])
        for g in range(4):
            segments(g * GROUP, g, 1, 4 + g)
        for w in range(WIN):
            upper = landed(0, 1, 4, w)
            for g in range(1, 4):
                upper = upper + landed(g, 1, 4 + g, w)
            u[w] = upper

    def adjoint_part(n, slot):
        for r in range(WIN):
            adjoint_row(te, r, u[r])
        segments(0, 0, 0, 3)
        for g in range(4):
            segments((1 + g) * GROUP, 1 + g, 1, g)
        segments(5 * GROUP, 5, 2, 0)

        def wide(i):
            total = None
            terms = []
            if i < WIN:
                terms.append(landed(0, 0, 3, i))
            if RT <= i < RT + WIN:
                for g in range(4):
                    terms.append(landed(1 + g, 1, g, i - RT))
                if n is not None:
                    terms.append(-(bend[n, i - RT] * u[i - RT]))
            if i >= 2 * RT:
                terms.append(landed(5, 2, 0, i - 2 * RT))
            for term in terms:
                total = term if total is None else total + term
            return total

        for j in range(RT // 2):
            for side, base in ((0, NB), (1, EDGE + RT)):
                pair = jnp.concatenate([wide(base + 2 * j), wide(base + 2 * j + 1)], axis=0)
                out1[slot, side, j] = pair.astype(bf16)
        for j in range(half_nb):
            for side, base in ((0, 0), (1, EDGE + 2 * RT)):
                pair = jnp.concatenate([wide(base + 2 * j), wide(base + 2 * j + 1)], axis=0)
                out2[slot, side, j] = pair.astype(bf16)
        for cp in adjoint_copies(slot):
            cp.start()
        for i in range(RT):
            part[i] = wide(EDGE + i)

    def adjoint_sum(slot):
        for cp in adjoint_copies(slot):
            cp.wait_recv()
        for j in range(RT // 2):
            both = in1[slot, 0, j].astype(f32) + in1[slot, 1, j].astype(f32)
            if j < half_nb:
                both = both + in2[slot, 0, j].astype(f32)
            if j >= RT // 2 - half_nb:
                both = both + in2[slot, 1, j - (RT // 2 - half_nb)].astype(f32)
            a[2 * j] = part[2 * j] + both[:ROWS]
            a[2 * j + 1] = part[2 * j + 1] + both[ROWS:]

    upper_copies = [
        copy(upper_out.at[0], upper_in.at[1], s_upper.at[0], r_upper.at[1], block(-1)),
        copy(upper_out.at[1], upper_in.at[0], s_upper.at[1], r_upper.at[0], block(1)),
    ]

    def first_part():
        upper_part()
        for j in range(half_nb):
            for side, base in ((0, 0), (1, NB + RT)):
                pair = jnp.concatenate([u[base + 2 * j], u[base + 2 * j + 1]], axis=0)
                upper_out[side, j] = pair.astype(bf16)
        for cp in upper_copies:
            cp.start()
        for i in range(RT):
            upper_full[i] = u[NB + i]
        adjoint_part(None, 0)

    def first_sum():
        adjoint_sum(0)
        for cp in upper_copies:
            cp.wait_recv()
        for j in range(half_nb):
            for side, base in ((0, 0), (1, RT - NB)):
                pair = upper_in[side, j].astype(f32)
                upper_full[base + 2 * j] = upper_full[base + 2 * j] + pair[:ROWS]
                upper_full[base + 2 * j + 1] = upper_full[base + 2 * j + 1] + pair[ROWS:]

    @pl.loop(0, STEPS - 1)
    def _(n):
        slot = lax.rem(n, 2)
        for i in range(RT):
            exchange_at(n, NB + i)

        @pl.when(n == 1)
        def _():
            first_part()

        @pl.when(n == 3)
        def _():
            first_sum()

        forward_step(n, slot)

        @pl.when(n > 0)
        def _():
            for cp in state_copies(1 - slot):
                cp.wait_send()

        pack_state(1 - slot)
        for cp in state_copies(1 - slot):
            cp.start()

    last = STEPS - 1
    grad = gacc[...]
    for i in range(RT):
        exchange_at(last, NB + i)
        a[i] = a[i] - bend[last, NB + i] * upper_full[i]
        grad = grad + upper_full[i] * gas[last, NB + i]
    gacc[...] = grad

    final_stays = pltpu.make_async_copy(leaving.at[0], final_ref, l_sem.at[0])
    final_copy = copy(leaving.at[0], final_ref, s_swap.at[0], r_swap.at[0], partner)
    adj_stays = pltpu.make_async_copy(leaving.at[1], adj_ref, l_sem.at[1])
    adj_copy = copy(leaving.at[1], adj_ref, s_swap.at[1], r_swap.at[1], partner)
    grad_swap = copy(grad_out, grad_in, s_swap.at[2], r_swap.at[2], partner)

    @pl.loop(1, STEPS)
    def _(back):
        n = STEPS - 1 - back
        slot = lax.rem(back, 2)
        upper_part()
        grad = gacc[...]
        for w in range(WIN):
            grad = grad + u[w] * gas[n, w]
        gacc[...] = grad

        @pl.when(back == STEPS - 1)
        def _():
            for d in range(1, n_cells):
                grad_copy(d).start()

        @pl.when(back > 1)
        def _():
            for cp in adjoint_copies(slot):
                cp.wait_send()

        adjoint_part(n, slot)

        @pl.when(back == 1)
        def _():
            forward_step(last, last % 2)
            for i in range(RT):
                leaving[0, :, i * TILE:(i + 1) * TILE] = x[EDGE + i]

            @pl.when(odd)
            def _():
                final_copy.start()

            @pl.when(jnp.logical_not(odd))
            def _():
                final_stays.start()

        adjoint_sum(slot)

    for i in range(RT):
        leaving[1, :, i * TILE:(i + 1) * TILE] = a[i]

    @pl.when(odd)
    def _():
        adj_copy.start()

    @pl.when(jnp.logical_not(odd))
    def _():
        adj_stays.start()

    total = gacc[...]
    for d in range(1, n_cells):
        source = rem(c - d, n_cells)
        copy(gacc, gin.at[source], s_grad.at[d], r_grad.at[source], block(d)).wait_recv()
        total = total + gin[source]
    scale = 1.0 / math.sqrt(n_cells * RT * TILE)
    grad_out[...] = jnp.broadcast_to(jnp.sum(total, axis=1, keepdims=True) * scale, (ROWS, TILE))

    @pl.when(odd)
    def _():
        grad_swap.start()

    for d in range(1, n_cells):
        grad_copy(d).wait_send()
    for slot in range(2):
        for cp in adjoint_copies(slot):
            cp.wait_send()
        for cp in state_copies(slot):
            cp.wait_send()
    for cp in upper_copies:
        cp.wait_send()

    @pl.when(odd)
    def _():
        grad_swap.wait()
        final_copy.wait()
        adj_copy.wait()
        grad_ref[...] = grad_in[...]

    @pl.when(jnp.logical_not(odd))
    def _():
        final_stays.wait()
        adj_stays.wait()
        grad_ref[...] = grad_out[...]


def solution(mesh):
    n_cells = mesh.shape["cells"]

    def body(init_state, tiles_exp, cols_exp, tiles_imp, cols_imp, surface, piston, atmosphere, final_cot):
        vmem, smem = pl.BlockSpec(memory_space=pltpu.VMEM), pl.BlockSpec(memory_space=pltpu.SMEM)
        anywhere = pl.BlockSpec(memory_space=pl.ANY)
        dma, i32 = pltpu.SemaphoreType.DMA, jnp.int32
        scratch = [
            pltpu.VMEM((WIN, K, TILE, TILE), bf16),
            pltpu.VMEM((RT, K, TILE, TILE), bf16),
            pltpu.VMEM((WIDE, ROWS, TILE), f32),
            pltpu.VMEM((WIN, ROWS, TILE), f32),
            pltpu.VMEM((STEPS, WIN, ROWS, TILE), f32),
            pltpu.VMEM((STEPS, WIN, ROWS, TILE), f32),
            pltpu.VMEM((WIN, ROWS, TILE), f32),
            pltpu.VMEM((4, 8, TILE), i32),
            pltpu.VMEM((2, 4, 8, TILE), i32),
            pltpu.SMEM((3, 4, 8, TILE), i32),
            pltpu.VMEM((RT, TILE), f32),
            pltpu.VMEM((2, RT, TILE), f32),
            pltpu.VMEM((2, RT // 2, 2 * ROWS, TILE), bf16),
            pltpu.VMEM((2, 2, RT // 2, 2 * ROWS, TILE), bf16),
            pltpu.VMEM((2, 2, NB // 2, 2 * ROWS, TILE), bf16),
            pltpu.VMEM((RT, ROWS, TILE), f32),
            pltpu.VMEM((WIN, ROWS, TILE), f32),
            pltpu.VMEM((RT, ROWS, TILE), f32),
            pltpu.VMEM((WIN * K, ROWS, TILE), f32),
            pltpu.VMEM((6 * SEG, ROWS, TILE), f32),
            pltpu.VMEM((2, 2, RT // 2, 2 * ROWS, TILE), bf16),
            pltpu.VMEM((2, 2, NB // 2, 2 * ROWS, TILE), bf16),
            pltpu.VMEM((2, 2, RT // 2, 2 * ROWS, TILE), bf16),
            pltpu.VMEM((2, 2, NB // 2, 2 * ROWS, TILE), bf16),
            pltpu.VMEM((ROWS, TILE), f32),
            pltpu.VMEM((n_cells, ROWS, TILE), f32),
            pltpu.VMEM((2, ROWS, TILE), f32),
            pltpu.VMEM((2, ROWS, TILE), f32),
            pltpu.VMEM((2, ROWS, TILE), f32),
            pltpu.VMEM((2, ROWS, RT * TILE), f32),
            pltpu.VMEM((2, ROWS, RT * TILE), f32),
            pltpu.VMEM((RT, TILE), i32),
            pltpu.VMEM((ROWS, TILE), f32),
            pltpu.VMEM((ROWS, TILE), f32),
            pltpu.VMEM((2, NB // 2, 2 * ROWS, TILE), bf16),
            pltpu.VMEM((2, NB // 2, 2 * ROWS, TILE), bf16),
            pltpu.VMEM((RT, ROWS, TILE), f32),
            dma((2,)), dma((2,)),
            dma((3,)), dma((3,)),
            dma((4,)), dma((4,)), dma((5,)),
            dma((14,)), dma((14,)), dma((16,)), dma((16,)),
            dma((2, 2)), dma((2, 2)), dma((2, 2)), dma((2, 2)),
            dma((2, 4)), dma((2, 4)), dma((2, 4)), dma((2, 4)),
            dma((n_cells,)), dma((n_cells,)),
        ]

        def run(*refs):
            kernel(n_cells, *refs)

        state = jax.ShapeDtypeStruct((ROWS, RT * TILE), f32)
        final, adjoint, grad = pl.pallas_call(
            run,
            out_shape=(state, state, jax.ShapeDtypeStruct((ROWS, TILE), f32)),
            in_specs=[anywhere, anywhere, anywhere, smem, smem, anywhere, smem, smem, anywhere],
            out_specs=(anywhere, anywhere, vmem),
            scratch_shapes=scratch,
            compiler_params=pltpu.CompilerParams(
                collective_id=0, has_side_effects=True, vmem_limit_bytes=60 << 20
            ),
        )(
            init_state, tiles_exp, tiles_imp, cols_exp, cols_imp, surface.reshape(RT, TILE),
            piston, atmosphere, final_cot,
        )
        return final, adjoint, grad[:, 0]

    placed = (
        P("samples", "cells"),
        P(("cells", "samples"), None, None, None),
        P("cells", None),
        P(("cells", "samples"), None, None, None),
        P("cells", None),
        P("cells"),
        P("samples"),
        P("samples"),
        P("samples", "cells"),
    )
    return jax.shard_map(
        body,
        mesh=mesh,
        in_specs=placed,
        out_specs=(P("samples", "cells"), P("samples", "cells"), P("samples")),
        check_vma=False,
    )
```

```python
import math

import jax
import jax.numpy as jnp
from jax import lax
from jax.experimental import pallas as pl
from jax.experimental.pallas import tpu as pltpu
from jax.sharding import PartitionSpec as P

STEPS = 8
RT = 16
K = 6
NB = 4
TILE = 128
ROWS = 8
GROUP = 4 * K
WIN = RT + 2 * NB
WIDE = WIN + 2 * RT
LOW = RT - NB
EDGE = RT + NB
SEG = GROUP + 1

step_length = 0.5
buffer_gain = 0.5
MESH = pl.DeviceIdType.MESH
f32, bf16 = jnp.float32, jnp.bfloat16


def kernel(
    n_cells,
    init_ref, te_ref, ti_ref, cols_exp_ref, cols_imp_ref, surf_ref, piston_ref, air_ref, cot_ref,
    final_ref, adj_ref, grad_ref,
    te, ti, x, src, gas, bend, half, meta, meta_in, idx,
    surf_own, surf_in, send1, recv1, recv2, a, u, part, contrib, seg,
    out1, out2, in1, in2, gacc, gin, levels, levels_in, levels_used, states, leaving, surf_int, grad_out, grad_in, upper_out, upper_in, upper_full,
    s_upper, r_upper, s_out, r_out, s_swap, r_swap, s_small, r_small, l_sem, s_gather, r_gather, s_core, r_core, s_halo, r_halo, s_hcore, r_hcore,
    s_fwd, r_fwd, s_adj, r_adj, s_grad, r_grad,
):
    c = lax.axis_index("cells")
    s = lax.axis_index("samples")
    y, l, k = s // 4, (s // 2) % 2, s % 2

    def rem(v, m):
        return lax.rem(v + m, m)

    def block(delta):
        return (rem(c + delta, n_cells), s if delta % 2 == 0 else s + 3 - 2 * (s % 4))

    def plane(yy, ll, kk):
        return (c, yy * 4 + ll * 2 + kk)

    up, down = plane(rem(y + 1, 4), l, k), plane(rem(y - 1, 4), l, k)
    across, other = plane(y, 1 - l, k), plane(y, l, 1 - k)
    partner = plane(y, 1 - l, 1 - k)
    odd = lax.rem(c, 2) == 1

    def copy(source, target, send, recv, device):
        return pltpu.make_async_remote_copy(source, target, send, recv, device_id=device, device_id_type=MESH)

    barrier = pltpu.get_barrier_semaphore()
    peers = [up, down, across, other, partner] + [block(d) for d in range(1, n_cells)]
    for device in peers:
        pl.semaphore_signal(barrier, inc=1, device_id=device, device_id_type=MESH)

    own_tiles = [
        pltpu.make_async_copy(te_ref.at[0], te.at[NB + s], l_sem.at[0]),
        pltpu.make_async_copy(ti_ref.at[0], ti.at[s], l_sem.at[1]),
    ]
    for cp in own_tiles:
        cp.start()
    surf_copy = pltpu.make_async_copy(surf_ref, surf_int, l_sem.at[2])
    surf_copy.start()
    stay = [
        pltpu.make_async_copy(init_ref, states.at[0], l_sem.at[3]),
        pltpu.make_async_copy(cot_ref, states.at[1], l_sem.at[4]),
    ]

    @pl.when(jnp.logical_not(odd))
    def _():
        for cp in stay:
            cp.start()

    row_of = lax.broadcasted_iota(jnp.int32, (ROWS, TILE), 0)
    piston = jnp.zeros((ROWS, TILE), f32)
    air = jnp.zeros((ROWS, TILE), f32)
    for i in range(ROWS):
        piston = jnp.where(row_of == i, piston_ref[i], piston)
        air = jnp.where(row_of == i, air_ref[i], air)
    levels[0] = piston
    levels[1] = air

    def pack_state(slot):
        for j in range(RT // 2):
            pair = jnp.concatenate([x[EDGE + 2 * j], x[EDGE + 2 * j + 1]], axis=0)
            send1[slot, j] = pair.astype(bf16)

    half_nb = NB // 2

    def state_copies(slot):
        mine = send1.at[slot]
        return [
            copy(mine, recv1.at[slot, 1], s_fwd.at[slot, 0], r_fwd.at[slot, 1], block(-1)),
            copy(mine, recv1.at[slot, 0], s_fwd.at[slot, 1], r_fwd.at[slot, 0], block(1)),
            copy(mine.at[pl.ds(0, half_nb)], recv2.at[slot, 1], s_fwd.at[slot, 2], r_fwd.at[slot, 3], block(-2)),
            copy(mine.at[pl.ds(RT // 2 - half_nb, half_nb)], recv2.at[slot, 0], s_fwd.at[slot, 3], r_fwd.at[slot, 2], block(2)),
        ]

    pl.semaphore_wait(barrier, len(peers))
    swap = [
        copy(init_ref, states.at[0], s_swap.at[0], r_swap.at[0], partner),
        copy(cot_ref, states.at[1], s_swap.at[1], r_swap.at[1], partner),
        copy(levels, levels_in, s_swap.at[2], r_swap.at[2], partner),
    ]

    buf = (te, ti)

    def tile_at(which, yy, ll, kk):
        row = yy * 4 + ll * 2 + kk
        return te.at[NB + row] if which == 0 else ti.at[row]

    gathers = {}

    def hop(name, which, yy, ll, device, source=None):
        at = tile_at(which, yy, ll, k)
        number = len(gathers)
        cp = copy(at if source is None else source, at, s_gather.at[number], r_gather.at[number], device)
        gathers[name] = (number, cp)
        cp.start()

    def arrived(name, which, yy, ll):
        number, cp = gathers[name]
        at = tile_at(which, yy, ll, k)
        copy(at, at, s_gather.at[number], r_gather.at[number], up).wait_recv()
        spread(which, yy, ll)

    core_sent = []
    halo_sent = []

    def spread(which, yy, ll):
        number = len(core_sent)
        at = tile_at(which, yy, ll, k)
        slot = which * 8 + yy * 2 + ll
        cp = copy(at, at, s_core.at[number], r_core.at[slot], other)
        core_sent.append(cp)
        cp.start()
        if which == 0:
            @pl.when(yy == 3)
            def _():
                copy(at, te.at[ll * 2 + k], s_halo.at[0, ll], r_halo.at[0, ll], block(1)).start()

            @pl.when(yy == 0)
            def _():
                copy(at, te.at[NB + RT + ll * 2 + k], s_halo.at[1, ll], r_halo.at[1, ll], block(-1)).start()

    ym, yp, yo, lo = rem(y - 1, 4), rem(y + 1, 4), rem(y + 2, 4), 1 - l
    for w, own in enumerate((te_ref.at[0], ti_ref.at[0])):
        hop(("up", w), w, y, l, up, own)
        hop(("down", w), w, y, l, down, own)
        hop(("x", w), w, y, l, across, own)
    @pl.when(odd)
    def _():
        for cp in swap:
            cp.start()

    for w in range(2):
        own_tiles[w].wait()
        spread(w, y, l)
    gacc[...] = jnp.zeros((ROWS, TILE), f32)
    for g in range(6):
        seg[g * SEG + GROUP] = jnp.zeros((ROWS, TILE), f32)

    lane = lax.broadcasted_iota(jnp.int32, (8, TILE), 1)
    spot = lax.broadcasted_iota(jnp.int32, (8, TILE), 0) * TILE + lane
    cols = jnp.zeros((8, TILE), jnp.int32)
    for m, ref in enumerate((cols_exp_ref, cols_imp_ref)):
        for r in range(RT):
            for j in range(K):
                cols = jnp.where(spot == (4 * m + r // 4) * TILE + (r % 4) * K + j, ref[j, r], cols)
    cols = jnp.clip(cols, LOW, LOW + WIN - 1)
    key = cols * 32 + lane
    rank = jnp.zeros((8, TILE), jnp.int32)
    upto = jnp.zeros((8, TILE), jnp.int32)
    here = jnp.zeros((8, TILE), jnp.int32)
    for i in range(GROUP):
        one = jnp.broadcast_to(cols[:, i:i + 1], (8, TILE))
        rank = rank + jnp.where(one * 32 + i < key, 1, 0)
        upto = upto + jnp.where(one - LOW <= lane, 1, 0)
        here = here + jnp.where(one - LOW == lane, 1, 0)
    order = jnp.zeros((8, TILE), jnp.int32)
    ordered = jnp.zeros((8, TILE), jnp.int32)
    before = jnp.zeros((8, TILE), jnp.int32)
    for i in range(GROUP):
        place = jnp.broadcast_to(rank[:, i:i + 1], (8, TILE))
        one = jnp.broadcast_to(cols[:, i:i + 1], (8, TILE))
        order = order + jnp.where(place == lane, i, 0)
        ordered = ordered + jnp.where(place == lane, one, 0)
        before = before + jnp.where(place + 1 == lane, one, 0)
    meta[0] = cols
    meta[1] = order
    meta[2] = jnp.where(ordered == before, 1, 0)
    meta[3] = jnp.where(here > 0, upto - 1, GROUP)

    surf_copy.wait()
    surf_own[...] = surf_int[...].astype(f32) * step_length
    small = []
    for side, device in ((0, block(1)), (1, block(-1))):
        small.append(copy(surf_own, surf_in.at[side], s_small.at[side], r_small.at[side], device))
        small.append(copy(meta, meta_in.at[side], s_small.at[2 + side], r_small.at[2 + side], device))
    for cp in small:
        cp.start()
    own_idx = pltpu.make_async_copy(meta, idx.at[1], l_sem.at[2])
    own_idx.start()


    arrived(("x", 0), 0, y, lo)
    hop(("xup", 0), 0, y, lo, up)
    hop(("xdown", 0), 0, y, lo, down)
    arrived(("up", 0), 0, ym, l)
    hop(("far", 0), 0, ym, l, up)
    arrived(("down", 0), 0, yp, l)
    arrived(("down", 1), 1, yp, l)
    hop(("far", 1), 1, yp, l, down)
    hop(("xd", 1), 1, yp, l, across)
    arrived(("up", 1), 1, ym, l)
    hop(("xu", 1), 1, ym, l, across)
    arrived(("x", 1), 1, y, lo)

    @pl.when(odd)
    def _():
        for cp in swap:
            cp.wait_recv()
        levels_used[...] = levels_in[...]

    @pl.when(jnp.logical_not(odd))
    def _():
        for cp in stay:
            cp.wait()
        levels_used[...] = levels[...]

    piston = levels_used[0]
    air = levels_used[1]
    for i in range(RT):
        x[EDGE + i] = states[0, :, i * TILE:(i + 1) * TILE]
        a[i] = states[1, :, i * TILE:(i + 1) * TILE]
    pack_state(0)
    for cp in state_copies(0):
        cp.start()

    for cp in small:
        cp.wait()
    moves = [pltpu.make_async_copy(meta_in.at[side], idx.at[2 * side], l_sem.at[3 + side]) for side in range(2)]
    for cp in moves:
        cp.start()
    for i in range(NB):
        half[i] = jnp.broadcast_to(surf_in[0, pl.ds(RT - NB + i, 1), :], (ROWS, TILE))
        half[NB + RT + i] = jnp.broadcast_to(surf_in[1, pl.ds(i, 1), :], (ROWS, TILE))
    for i in range(RT):
        half[NB + i] = jnp.broadcast_to(surf_own[pl.ds(i, 1), :], (ROWS, TILE))

    arrived(("xup", 0), 0, ym, lo)
    hop(("farx", 0), 0, ym, lo, up)
    arrived(("xdown", 0), 0, yp, lo)
    arrived(("xd", 1), 1, yp, lo)
    hop(("farx", 1), 1, yp, lo, down)
    arrived(("far", 0), 0, yo, l)
    arrived(("far", 1), 1, yo, l)
    arrived(("xu", 1), 1, ym, lo)
    arrived(("farx", 0), 0, yo, lo)
    arrived(("farx", 1), 1, yo, lo)
    hcore = []
    for side in range(2):
        for ll in range(2):
            base = 0 if side == 0 else NB + RT
            at = te.at[base + ll * 2 + 1 - k]
            copy(at, at, s_halo.at[side, ll], r_halo.at[side, ll], other).wait_recv()
            cp = copy(at, at, s_hcore.at[side, ll], r_hcore.at[side, ll], other)
            cp.start()
            hcore.append(cp)

    own_idx.wait()
    for cp in moves:
        cp.wait()

    @pl.when(odd)
    def _():
        for cp in swap:
            cp.wait_send()

    for _, cp in gathers.values():
        cp.wait_send()
    for cp in core_sent:
        cp.wait_send()
    for w in range(2):
        for yy in range(4):
            for ll in range(2):
                at = tile_at(w, yy, ll, 1 - k)
                copy(at, at, s_core.at[0], r_core.at[w * 8 + yy * 2 + ll], other).wait_recv()
    for side in range(2):
        for ll in range(2):
            at = te.at[ll]
            copy(at, at, s_halo.at[side, ll], r_halo.at[side, ll], other).wait_send()
    for cp in hcore:
        cp.wait()

    def exchange_at(n, w):
        t = x[RT + w]
        th = jnp.tanh(t)
        hs = half[w]
        gas[n, w] = hs * (air - t * (1.0 + buffer_gain * th))
        bend[n, w] = hs * piston * (1.0 + buffer_gain * th + buffer_gain * t * (1.0 - th * th))

    wide_rows = []
    for r in range(NB):
        wide_rows.append((r, 0, 3, r, -LOW))
    for r in range(RT):
        wide_rows.append((NB + r, 1, r // 4, r % 4, NB))
    for r in range(NB):
        wide_rows.append((NB + RT + r, 2, 0, r, NB + RT))

    def forward_row(tiles, row, field, owner, group, place, shift):
        picked = [field[idx[owner, 0, group, place * K + j] + shift] for j in range(K)]
        values = jnp.concatenate(picked, axis=1).astype(bf16)
        weights = jnp.concatenate([tiles[row, j] for j in range(K)], axis=1)
        return lax.dot_general(values, weights, (((1,), (1,)), ((), ())), preferred_element_type=f32)

    def forward_step(n, slot):
        for cp in state_copies(slot):
            cp.wait_recv()
        for j in range(RT // 2):
            for side, base in ((0, NB), (1, EDGE + RT)):
                pair = recv1[slot, side, j].astype(f32)
                x[base + 2 * j] = pair[:ROWS]
                x[base + 2 * j + 1] = pair[ROWS:]
        for j in range(half_nb):
            for side, base in ((0, 0), (1, EDGE + RT + RT)):
                pair = recv2[slot, side, j].astype(f32)
                x[base + 2 * j] = pair[:ROWS]
                x[base + 2 * j + 1] = pair[ROWS:]
        for i in range(NB):
            exchange_at(n, i)
            exchange_at(n, NB + RT + i)
        for row, owner, group, place, shift in wide_rows:
            moved = forward_row(te, row, x, owner, group, place, shift)
            src[row] = moved + piston * gas[n, row]
        for r in range(RT):
            x[EDGE + r] = forward_row(ti, r, src, 1, 4 + r // 4, r % 4, -LOW)

    def segments(first, number, owner, group):
        total = None
        for p in range(GROUP):
            value = contrib[first + idx[owner, 1, group, p]]
            if p > 0:
                value = value + total * idx[owner, 2, group, p].astype(f32)
            total = value
            seg[number * SEG + p] = total

    def landed(number, owner, group, w):
        return seg[number * SEG + idx[owner, 3, group, w]]

    def adjoint_row(tiles, row, field):
        weights = jnp.concatenate([tiles[row, j] for j in range(K)], axis=1)
        spread_out = jnp.dot(field.astype(bf16), weights, preferred_element_type=f32)
        for j in range(K):
            contrib[row * K + j] = spread_out[:, j * TILE:(j + 1) * TILE]

    def adjoint_copies(slot):
        return [
            copy(out1.at[slot, 0], in1.at[slot, 1], s_adj.at[slot, 0], r_adj.at[slot, 1], block(-1)),
            copy(out1.at[slot, 1], in1.at[slot, 0], s_adj.at[slot, 1], r_adj.at[slot, 0], block(1)),
            copy(out2.at[slot, 0], in2.at[slot, 1], s_adj.at[slot, 2], r_adj.at[slot, 3], block(-2)),
            copy(out2.at[slot, 1], in2.at[slot, 0], s_adj.at[slot, 3], r_adj.at[slot, 2], block(2)),
        ]

    def grad_copy(d):
        return copy(gacc, gin.at[c], s_grad.at[d], r_grad.at[c], block(d))

    def upper_part():
        for r in range(RT):
            adjoint_row(ti, r, a[r])
        for g in range(4):
            segments(g * GROUP, g, 1, 4 + g)
        for w in range(WIN):
            upper = landed(0, 1, 4, w)
            for g in range(1, 4):
                upper = upper + landed(g, 1, 4 + g, w)
            u[w] = upper

    def adjoint_part(n, slot):
        for r in range(WIN):
            adjoint_row(te, r, u[r])
        segments(0, 0, 0, 3)
        for g in range(4):
            segments((1 + g) * GROUP, 1 + g, 1, g)
        segments(5 * GROUP, 5, 2, 0)

        def wide(i):
            total = None
            terms = []
            if i < WIN:
                terms.append(landed(0, 0, 3, i))
            if RT <= i < RT + WIN:
                for g in range(4):
                    terms.append(landed(1 + g, 1, g, i - RT))
                if n is not None:
                    terms.append(-(bend[n, i - RT] * u[i - RT]))
            if i >= 2 * RT:
                terms.append(landed(5, 2, 0, i - 2 * RT))
            for term in terms:
                total = term if total is None else total + term
            return total

        for j in range(RT // 2):
            for side, base in ((0, NB), (1, EDGE + RT)):
                pair = jnp.concatenate([wide(base + 2 * j), wide(base + 2 * j + 1)], axis=0)
                out1[slot, side, j] = pair.astype(bf16)
        for j in range(half_nb):
            for side, base in ((0, 0), (1, EDGE + 2 * RT)):
                pair = jnp.concatenate([wide(base + 2 * j), wide(base + 2 * j + 1)], axis=0)
                out2[slot, side, j] = pair.astype(bf16)
        for cp in adjoint_copies(slot):
            cp.start()
        for i in range(RT):
            part[i] = wide(EDGE + i)

    def adjoint_sum(slot):
        for cp in adjoint_copies(slot):
            cp.wait_recv()
        for j in range(RT // 2):
            both = in1[slot, 0, j].astype(f32) + in1[slot, 1, j].astype(f32)
            if j < half_nb:
                both = both + in2[slot, 0, j].astype(f32)
            if j >= RT // 2 - half_nb:
                both = both + in2[slot, 1, j - (RT // 2 - half_nb)].astype(f32)
            a[2 * j] = part[2 * j] + both[:ROWS]
            a[2 * j + 1] = part[2 * j + 1] + both[ROWS:]

    upper_copies = [
        copy(upper_out.at[0], upper_in.at[1], s_upper.at[0], r_upper.at[1], block(-1)),
        copy(upper_out.at[1], upper_in.at[0], s_upper.at[1], r_upper.at[0], block(1)),
    ]

    def first_part():
        upper_part()
        for j in range(half_nb):
            for side, base in ((0, 0), (1, NB + RT)):
                pair = jnp.concatenate([u[base + 2 * j], u[base + 2 * j + 1]], axis=0)
                upper_out[side, j] = pair.astype(bf16)
        for cp in upper_copies:
            cp.start()
        for i in range(RT):
            upper_full[i] = u[NB + i]
        adjoint_part(None, 0)

    def first_sum():
        adjoint_sum(0)
        for cp in upper_copies:
            cp.wait_recv()
        for j in range(half_nb):
            for side, base in ((0, 0), (1, RT - NB)):
                pair = upper_in[side, j].astype(f32)
                upper_full[base + 2 * j] = upper_full[base + 2 * j] + pair[:ROWS]
                upper_full[base + 2 * j + 1] = upper_full[base + 2 * j + 1] + pair[ROWS:]

    @pl.loop(0, STEPS - 1)
    def _(n):
        slot = lax.rem(n, 2)
        for i in range(RT):
            exchange_at(n, NB + i)

        @pl.when(n == 1)
        def _():
            first_part()

        @pl.when(n == 3)
        def _():
            first_sum()

        forward_step(n, slot)

        @pl.when(n > 0)
        def _():
            for cp in state_copies(1 - slot):
                cp.wait_send()

        pack_state(1 - slot)
        for cp in state_copies(1 - slot):
            cp.start()

    last = STEPS - 1
    grad = gacc[...]
    for i in range(RT):
        exchange_at(last, NB + i)
        a[i] = a[i] - bend[last, NB + i] * upper_full[i]
        grad = grad + upper_full[i] * gas[last, NB + i]
    gacc[...] = grad

    final_stays = pltpu.make_async_copy(leaving.at[0], final_ref, l_sem.at[0])
    final_copy = copy(leaving.at[0], final_ref, s_out.at[0], r_out.at[0], partner)
    adj_stays = pltpu.make_async_copy(leaving.at[1], adj_ref, l_sem.at[1])
    adj_copy = copy(leaving.at[1], adj_ref, s_out.at[1], r_out.at[1], partner)
    grad_swap = copy(grad_out, grad_in, s_out.at[2], r_out.at[2], partner)

    @pl.loop(1, STEPS)
    def _(back):
        n = STEPS - 1 - back
        slot = lax.rem(back, 2)
        upper_part()
        grad = gacc[...]
        for w in range(WIN):
            grad = grad + u[w] * gas[n, w]
        gacc[...] = grad

        @pl.when(back == STEPS - 1)
        def _():
            for d in range(1, n_cells):
                grad_copy(d).start()

        @pl.when(back > 1)
        def _():
            for cp in adjoint_copies(slot):
                cp.wait_send()

        adjoint_part(n, slot)

        @pl.when(back == 1)
        def _():
            forward_step(last, last % 2)
            for i in range(RT):
                leaving[0, :, i * TILE:(i + 1) * TILE] = x[EDGE + i]

            @pl.when(odd)
            def _():
                final_copy.start()

            @pl.when(jnp.logical_not(odd))
            def _():
                final_stays.start()

        adjoint_sum(slot)

    for i in range(RT):
        leaving[1, :, i * TILE:(i + 1) * TILE] = a[i]

    @pl.when(odd)
    def _():
        adj_copy.start()

    @pl.when(jnp.logical_not(odd))
    def _():
        adj_stays.start()

    total = gacc[...]
    for d in range(1, n_cells):
        source = rem(c - d, n_cells)
        copy(gacc, gin.at[source], s_grad.at[d], r_grad.at[source], block(d)).wait_recv()
        total = total + gin[source]
    scale = 1.0 / math.sqrt(n_cells * RT * TILE)
    grad_out[...] = jnp.broadcast_to(jnp.sum(total, axis=1, keepdims=True) * scale, (ROWS, TILE))

    @pl.when(odd)
    def _():
        grad_swap.start()

    for d in range(1, n_cells):
        grad_copy(d).wait_send()
    for slot in range(2):
        for cp in adjoint_copies(slot):
            cp.wait_send()
        for cp in state_copies(slot):
            cp.wait_send()
    for cp in upper_copies:
        cp.wait_send()

    @pl.when(odd)
    def _():
        grad_swap.wait()
        final_copy.wait()
        adj_copy.wait()
        grad_ref[...] = grad_in[...]

    @pl.when(jnp.logical_not(odd))
    def _():
        final_stays.wait()
        adj_stays.wait()
        grad_ref[...] = grad_out[...]


def solution(mesh):
    n_cells = mesh.shape["cells"]

    def body(init_state, tiles_exp, cols_exp, tiles_imp, cols_imp, surface, piston, atmosphere, final_cot):
        vmem, smem = pl.BlockSpec(memory_space=pltpu.VMEM), pl.BlockSpec(memory_space=pltpu.SMEM)
        anywhere = pl.BlockSpec(memory_space=pl.ANY)
        dma, i32 = pltpu.SemaphoreType.DMA, jnp.int32
        scratch = [
            pltpu.VMEM((WIN, K, TILE, TILE), bf16),
            pltpu.VMEM((RT, K, TILE, TILE), bf16),
            pltpu.VMEM((WIDE, ROWS, TILE), f32),
            pltpu.VMEM((WIN, ROWS, TILE), f32),
            pltpu.VMEM((STEPS, WIN, ROWS, TILE), f32),
            pltpu.VMEM((STEPS, WIN, ROWS, TILE), f32),
            pltpu.VMEM((WIN, ROWS, TILE), f32),
            pltpu.VMEM((4, 8, TILE), i32),
            pltpu.VMEM((2, 4, 8, TILE), i32),
            pltpu.SMEM((3, 4, 8, TILE), i32),
            pltpu.VMEM((RT, TILE), f32),
            pltpu.VMEM((2, RT, TILE), f32),
            pltpu.VMEM((2, RT // 2, 2 * ROWS, TILE), bf16),
            pltpu.VMEM((2, 2, RT // 2, 2 * ROWS, TILE), bf16),
            pltpu.VMEM((2, 2, NB // 2, 2 * ROWS, TILE), bf16),
            pltpu.VMEM((RT, ROWS, TILE), f32),
            pltpu.VMEM((WIN, ROWS, TILE), f32),
            pltpu.VMEM((RT, ROWS, TILE), f32),
            pltpu.VMEM((WIN * K, ROWS, TILE), f32),
            pltpu.VMEM((6 * SEG, ROWS, TILE), f32),
            pltpu.VMEM((2, 2, RT // 2, 2 * ROWS, TILE), bf16),
            pltpu.VMEM((2, 2, NB // 2, 2 * ROWS, TILE), bf16),
            pltpu.VMEM((2, 2, RT // 2, 2 * ROWS, TILE), bf16),
            pltpu.VMEM((2, 2, NB // 2, 2 * ROWS, TILE), bf16),
            pltpu.VMEM((ROWS, TILE), f32),
            pltpu.VMEM((n_cells, ROWS, TILE), f32),
            pltpu.VMEM((2, ROWS, TILE), f32),
            pltpu.VMEM((2, ROWS, TILE), f32),
            pltpu.VMEM((2, ROWS, TILE), f32),
            pltpu.VMEM((2, ROWS, RT * TILE), f32),
            pltpu.VMEM((2, ROWS, RT * TILE), f32),
            pltpu.VMEM((RT, TILE), i32),
            pltpu.VMEM((ROWS, TILE), f32),
            pltpu.VMEM((ROWS, TILE), f32),
            pltpu.VMEM((2, NB // 2, 2 * ROWS, TILE), bf16),
            pltpu.VMEM((2, NB // 2, 2 * ROWS, TILE), bf16),
            pltpu.VMEM((RT, ROWS, TILE), f32),
            dma((2,)), dma((2,)),
            dma((3,)), dma((3,)),
            dma((3,)), dma((3,)),
            dma((4,)), dma((4,)), dma((5,)),
            dma((14,)), dma((14,)), dma((16,)), dma((16,)),
            dma((2, 2)), dma((2, 2)), dma((2, 2)), dma((2, 2)),
            dma((2, 4)), dma((2, 4)), dma((2, 4)), dma((2, 4)),
            dma((n_cells,)), dma((n_cells,)),
        ]

        def run(*refs):
            kernel(n_cells, *refs)

        state = jax.ShapeDtypeStruct((ROWS, RT * TILE), f32)
        final, adjoint, grad = pl.pallas_call(
            run,
            out_shape=(state, state, jax.ShapeDtypeStruct((ROWS, TILE), f32)),
            in_specs=[anywhere, anywhere, anywhere, smem, smem, anywhere, smem, smem, anywhere],
            out_specs=(anywhere, anywhere, vmem),
            scratch_shapes=scratch,
            compiler_params=pltpu.CompilerParams(
                collective_id=0, has_side_effects=True, vmem_limit_bytes=60 << 20
            ),
        )(
            init_state, tiles_exp, tiles_imp, cols_exp.T, cols_imp.T, surface.reshape(RT, TILE),
            piston, atmosphere, final_cot,
        )
        return final, adjoint, grad[:, 0]

    placed = (
        P("samples", "cells"),
        P(("cells", "samples"), None, None, None),
        P("cells", None),
        P(("cells", "samples"), None, None, None),
        P("cells", None),
        P("cells"),
        P("samples"),
        P("samples"),
        P("samples", "cells"),
    )
    return jax.shard_map(
        body,
        mesh=mesh,
        in_specs=placed,
        out_specs=(P("samples", "cells"), P("samples", "cells"), P("samples")),
        check_vma=False,
    )
```

```python
import math

import jax
import jax.numpy as jnp
from jax import lax
from jax.experimental import pallas as pl
from jax.experimental.pallas import tpu as pltpu
from jax.sharding import PartitionSpec as P

STEPS = 8
RT = 16
K = 6
NB = 4
TILE = 128
ROWS = 8
GROUP = 4 * K
WIN = RT + 2 * NB
WIDE = WIN + 2 * RT
LOW = RT - NB
EDGE = RT + NB
SEG = GROUP + 1

step_length = 0.5
buffer_gain = 0.5
MESH = pl.DeviceIdType.MESH
f32, bf16 = jnp.float32, jnp.bfloat16


def kernel(
    n_cells,
    init_ref, te_ref, ti_ref, cols_exp_ref, cols_imp_ref, surf_ref, piston_ref, air_ref, cot_ref,
    out_ref, grad_ref,
    te, ti, x, src, gas, bend, half, meta, meta_in, idx,
    surf_own, surf_in, send1, recv1, recv2, a, u, part, contrib, seg,
    out1, out2, in1, in2, gacc, gin, levels, levels_in, levels_used, states, leaving, surf_int, grad_out, grad_in, upper_out, upper_in, upper_full, same,
    s_upper, r_upper, s_out, r_out, s_swap, r_swap, s_small, r_small, l_sem, s_gather, r_gather, s_core, r_core, s_halo, r_halo, s_hcore, r_hcore,
    s_fwd, r_fwd, s_adj, r_adj, s_grad, r_grad,
):
    c = lax.axis_index("cells")
    s = lax.axis_index("samples")
    y, l, k = s // 4, (s // 2) % 2, s % 2

    def rem(v, m):
        return lax.rem(v + m, m)

    def block(delta):
        return (rem(c + delta, n_cells), s if delta % 2 == 0 else s + 3 - 2 * (s % 4))

    def plane(yy, ll, kk):
        return (c, yy * 4 + ll * 2 + kk)

    up, down = plane(rem(y + 1, 4), l, k), plane(rem(y - 1, 4), l, k)
    across, other = plane(y, 1 - l, k), plane(y, l, 1 - k)
    partner = plane(y, 1 - l, 1 - k)
    odd = lax.rem(c, 2) == 1

    def copy(source, target, send, recv, device):
        return pltpu.make_async_remote_copy(source, target, send, recv, device_id=device, device_id_type=MESH)

    barrier = pltpu.get_barrier_semaphore()
    peers = [up, down, across, other, partner] + [block(d) for d in range(1, n_cells)]
    for device in peers:
        pl.semaphore_signal(barrier, inc=1, device_id=device, device_id_type=MESH)

    own_tiles = [
        pltpu.make_async_copy(te_ref.at[0], te.at[NB + s], l_sem.at[0]),
        pltpu.make_async_copy(ti_ref.at[0], ti.at[s], l_sem.at[1]),
    ]
    for cp in own_tiles:
        cp.start()
    surf_copy = pltpu.make_async_copy(surf_ref, surf_int, l_sem.at[2])
    surf_copy.start()
    stay = [
        pltpu.make_async_copy(init_ref, states.at[0], l_sem.at[3]),
        pltpu.make_async_copy(cot_ref, states.at[1], l_sem.at[4]),
    ]

    @pl.when(jnp.logical_not(odd))
    def _():
        for cp in stay:
            cp.start()

    row_of = lax.broadcasted_iota(jnp.int32, (ROWS, TILE), 0)
    piston = jnp.zeros((ROWS, TILE), f32)
    air = jnp.zeros((ROWS, TILE), f32)
    for i in range(ROWS):
        piston = jnp.where(row_of == i, piston_ref[i], piston)
        air = jnp.where(row_of == i, air_ref[i], air)
    levels[0] = piston
    levels[1] = air

    def pack_state(slot):
        for j in range(RT // 2):
            pair = jnp.concatenate([x[EDGE + 2 * j], x[EDGE + 2 * j + 1]], axis=0)
            send1[slot, j] = pair.astype(bf16)

    half_nb = NB // 2

    def state_copies(slot):
        mine = send1.at[slot]
        return [
            copy(mine, recv1.at[slot, 1], s_fwd.at[slot, 0], r_fwd.at[slot, 1], block(-1)),
            copy(mine, recv1.at[slot, 0], s_fwd.at[slot, 1], r_fwd.at[slot, 0], block(1)),
            copy(mine.at[pl.ds(0, half_nb)], recv2.at[slot, 1], s_fwd.at[slot, 2], r_fwd.at[slot, 3], block(-2)),
            copy(mine.at[pl.ds(RT // 2 - half_nb, half_nb)], recv2.at[slot, 0], s_fwd.at[slot, 3], r_fwd.at[slot, 2], block(2)),
        ]

    pl.semaphore_wait(barrier, len(peers))
    swap = [
        copy(init_ref, states.at[0], s_swap.at[0], r_swap.at[0], partner),
        copy(cot_ref, states.at[1], s_swap.at[1], r_swap.at[1], partner),
        copy(levels, levels_in, s_swap.at[2], r_swap.at[2], partner),
    ]

    buf = (te, ti)

    def tile_at(which, yy, ll, kk):
        row = yy * 4 + ll * 2 + kk
        return te.at[NB + row] if which == 0 else ti.at[row]

    gathers = {}

    def hop(name, which, yy, ll, device, source=None):
        at = tile_at(which, yy, ll, k)
        number = len(gathers)
        cp = copy(at if source is None else source, at, s_gather.at[number], r_gather.at[number], device)
        gathers[name] = (number, cp)
        cp.start()

    def arrived(name, which, yy, ll):
        number, cp = gathers[name]
        at = tile_at(which, yy, ll, k)
        copy(at, at, s_gather.at[number], r_gather.at[number], up).wait_recv()
        spread(which, yy, ll)

    core_sent = []
    halo_sent = []

    def spread(which, yy, ll):
        number = len(core_sent)
        at = tile_at(which, yy, ll, k)
        slot = which * 8 + yy * 2 + ll
        cp = copy(at, at, s_core.at[number], r_core.at[slot], other)
        core_sent.append(cp)
        cp.start()
        if which == 0:
            @pl.when(yy == 3)
            def _():
                copy(at, te.at[ll * 2 + k], s_halo.at[0, ll], r_halo.at[0, ll], block(1)).start()

            @pl.when(yy == 0)
            def _():
                copy(at, te.at[NB + RT + ll * 2 + k], s_halo.at[1, ll], r_halo.at[1, ll], block(-1)).start()

    ym, yp, yo, lo = rem(y - 1, 4), rem(y + 1, 4), rem(y + 2, 4), 1 - l
    for w, own in enumerate((te_ref.at[0], ti_ref.at[0])):
        hop(("up", w), w, y, l, up, own)
        hop(("down", w), w, y, l, down, own)
        hop(("x", w), w, y, l, across, own)
    @pl.when(odd)
    def _():
        for cp in swap:
            cp.start()

    for w in range(2):
        own_tiles[w].wait()
        spread(w, y, l)
    gacc[...] = jnp.zeros((ROWS, TILE), f32)
    for g in range(6):
        seg[g * SEG + GROUP] = jnp.zeros((ROWS, TILE), f32)

    lane = lax.broadcasted_iota(jnp.int32, (8, TILE), 1)
    spot = lax.broadcasted_iota(jnp.int32, (8, TILE), 0) * TILE + lane
    cols = jnp.zeros((8, TILE), jnp.int32)
    for m, ref in enumerate((cols_exp_ref, cols_imp_ref)):
        for r in range(RT):
            for j in range(K):
                cols = jnp.where(spot == (4 * m + r // 4) * TILE + (r % 4) * K + j, ref[j, r], cols)
    cols = jnp.clip(cols, LOW, LOW + WIN - 1)
    key = cols * 32 + lane
    rank = jnp.zeros((8, TILE), jnp.int32)
    upto = jnp.zeros((8, TILE), jnp.int32)
    here = jnp.zeros((8, TILE), jnp.int32)
    for i in range(GROUP):
        one = jnp.broadcast_to(cols[:, i:i + 1], (8, TILE))
        rank = rank + jnp.where(one * 32 + i < key, 1, 0)
        upto = upto + jnp.where(one - LOW <= lane, 1, 0)
        here = here + jnp.where(one - LOW == lane, 1, 0)
    order = jnp.zeros((8, TILE), jnp.int32)
    ordered = jnp.zeros((8, TILE), jnp.int32)
    before = jnp.zeros((8, TILE), jnp.int32)
    for i in range(GROUP):
        place = jnp.broadcast_to(rank[:, i:i + 1], (8, TILE))
        one = jnp.broadcast_to(cols[:, i:i + 1], (8, TILE))
        order = order + jnp.where(place == lane, i, 0)
        ordered = ordered + jnp.where(place == lane, one, 0)
        before = before + jnp.where(place + 1 == lane, one, 0)
    meta[0] = cols
    meta[1] = order
    meta[2] = jnp.where(ordered == before, 1, 0)
    meta[3] = jnp.where(here > 0, upto - 1, GROUP)

    surf_copy.wait()
    surf_own[...] = surf_int[...].astype(f32) * step_length
    small = []
    for side, device in ((0, block(1)), (1, block(-1))):
        small.append(copy(surf_own, surf_in.at[side], s_small.at[side], r_small.at[side], device))
        small.append(copy(meta, meta_in.at[side], s_small.at[2 + side], r_small.at[2 + side], device))
    for cp in small:
        cp.start()
    own_idx = pltpu.make_async_copy(meta, idx.at[1], l_sem.at[2])
    own_idx.start()


    arrived(("x", 0), 0, y, lo)
    hop(("xup", 0), 0, y, lo, up)
    hop(("xdown", 0), 0, y, lo, down)
    arrived(("up", 0), 0, ym, l)
    hop(("far", 0), 0, ym, l, up)
    arrived(("down", 0), 0, yp, l)
    arrived(("down", 1), 1, yp, l)
    hop(("far", 1), 1, yp, l, down)
    hop(("xd", 1), 1, yp, l, across)
    arrived(("up", 1), 1, ym, l)
    hop(("xu", 1), 1, ym, l, across)
    arrived(("x", 1), 1, y, lo)

    @pl.when(odd)
    def _():
        for cp in swap:
            cp.wait_recv()
        levels_used[...] = levels_in[...]

    @pl.when(jnp.logical_not(odd))
    def _():
        for cp in stay:
            cp.wait()
        levels_used[...] = levels[...]

    piston = levels_used[0]
    air = levels_used[1]
    for i in range(RT):
        x[EDGE + i] = states[0, :, i * TILE:(i + 1) * TILE]
        a[i] = states[1, :, i * TILE:(i + 1) * TILE]
    pack_state(0)
    for cp in state_copies(0):
        cp.start()

    for cp in small:
        cp.wait()
    moves = [pltpu.make_async_copy(meta_in.at[side], idx.at[2 * side], l_sem.at[3 + side]) for side in range(2)]
    for cp in moves:
        cp.start()
    for i in range(NB):
        half[i] = jnp.broadcast_to(surf_in[0, pl.ds(RT - NB + i, 1), :], (ROWS, TILE))
        half[NB + RT + i] = jnp.broadcast_to(surf_in[1, pl.ds(i, 1), :], (ROWS, TILE))
    for i in range(RT):
        half[NB + i] = jnp.broadcast_to(surf_own[pl.ds(i, 1), :], (ROWS, TILE))

    arrived(("xup", 0), 0, ym, lo)
    hop(("farx", 0), 0, ym, lo, up)
    arrived(("xdown", 0), 0, yp, lo)
    arrived(("xd", 1), 1, yp, lo)
    hop(("farx", 1), 1, yp, lo, down)
    arrived(("far", 0), 0, yo, l)
    own_idx.wait()
    for cp in moves:
        cp.wait()
    groups = [(0, 3)] + [(1, g) for g in range(8)] + [(2, 0)]
    first_of = {at: i * GROUP for i, at in enumerate(groups)}
    for owner, group in groups:
        for p in range(1, GROUP):
            factor = idx[owner, 2, group, p].astype(f32)
            same[first_of[owner, group] + p] = jnp.full((ROWS, TILE), factor, f32)
    arrived(("far", 1), 1, yo, l)
    arrived(("xu", 1), 1, ym, lo)
    arrived(("farx", 0), 0, yo, lo)
    arrived(("farx", 1), 1, yo, lo)
    hcore = []
    for side in range(2):
        for ll in range(2):
            base = 0 if side == 0 else NB + RT
            at = te.at[base + ll * 2 + 1 - k]
            copy(at, at, s_halo.at[side, ll], r_halo.at[side, ll], other).wait_recv()
            cp = copy(at, at, s_hcore.at[side, ll], r_hcore.at[side, ll], other)
            cp.start()
            hcore.append(cp)

    @pl.when(odd)
    def _():
        for cp in swap:
            cp.wait_send()

    for _, cp in gathers.values():
        cp.wait_send()
    for cp in core_sent:
        cp.wait_send()
    for w in range(2):
        for yy in range(4):
            for ll in range(2):
                at = tile_at(w, yy, ll, 1 - k)
                copy(at, at, s_core.at[0], r_core.at[w * 8 + yy * 2 + ll], other).wait_recv()
    for side in range(2):
        for ll in range(2):
            at = te.at[ll]
            copy(at, at, s_halo.at[side, ll], r_halo.at[side, ll], other).wait_send()
    for cp in hcore:
        cp.wait()

    def exchange_at(n, w):
        t = x[RT + w]
        th = jnp.tanh(t)
        hs = half[w]
        gas[n, w] = hs * (air - t * (1.0 + buffer_gain * th))
        bend[n, w] = hs * piston * (1.0 + buffer_gain * th + buffer_gain * t * (1.0 - th * th))

    wide_rows = []
    for r in range(NB):
        wide_rows.append((r, 0, 3, r, -LOW))
    for r in range(RT):
        wide_rows.append((NB + r, 1, r // 4, r % 4, NB))
    for r in range(NB):
        wide_rows.append((NB + RT + r, 2, 0, r, NB + RT))

    def forward_row(tiles, row, field, owner, group, place, shift):
        picked = [field[idx[owner, 0, group, place * K + j] + shift] for j in range(K)]
        values = jnp.concatenate(picked, axis=1).astype(bf16)
        weights = jnp.concatenate([tiles[row, j] for j in range(K)], axis=1)
        return lax.dot_general(values, weights, (((1,), (1,)), ((), ())), preferred_element_type=f32)

    def forward_step(n, slot):
        for cp in state_copies(slot):
            cp.wait_recv()
        for j in range(RT // 2):
            for side, base in ((0, NB), (1, EDGE + RT)):
                pair = recv1[slot, side, j].astype(f32)
                x[base + 2 * j] = pair[:ROWS]
                x[base + 2 * j + 1] = pair[ROWS:]
        for j in range(half_nb):
            for side, base in ((0, 0), (1, EDGE + RT + RT)):
                pair = recv2[slot, side, j].astype(f32)
                x[base + 2 * j] = pair[:ROWS]
                x[base + 2 * j + 1] = pair[ROWS:]
        for i in range(NB):
            exchange_at(n, i)
            exchange_at(n, NB + RT + i)
        for row, owner, group, place, shift in wide_rows:
            moved = forward_row(te, row, x, owner, group, place, shift)
            src[row] = moved + piston * gas[n, row]
        for r in range(RT):
            x[EDGE + r] = forward_row(ti, r, src, 1, 4 + r // 4, r % 4, -LOW)

    def segments(first, number, owner, group):
        total = None
        for p in range(GROUP):
            value = contrib[first + idx[owner, 1, group, p]]
            if p > 0:
                value = value + total * same[first_of[owner, group] + p]
            total = value
            seg[number * SEG + p] = total

    def landed(number, owner, group, w):
        return seg[number * SEG + idx[owner, 3, group, w]]

    def adjoint_row(tiles, row, field):
        weights = jnp.concatenate([tiles[row, j] for j in range(K)], axis=1)
        spread_out = jnp.dot(field.astype(bf16), weights, preferred_element_type=f32)
        for j in range(K):
            contrib[row * K + j] = spread_out[:, j * TILE:(j + 1) * TILE]

    def adjoint_copies(slot):
        return [
            copy(out1.at[slot, 0], in1.at[slot, 1], s_adj.at[slot, 0], r_adj.at[slot, 1], block(-1)),
            copy(out1.at[slot, 1], in1.at[slot, 0], s_adj.at[slot, 1], r_adj.at[slot, 0], block(1)),
            copy(out2.at[slot, 0], in2.at[slot, 1], s_adj.at[slot, 2], r_adj.at[slot, 3], block(-2)),
            copy(out2.at[slot, 1], in2.at[slot, 0], s_adj.at[slot, 3], r_adj.at[slot, 2], block(2)),
        ]

    def grad_copy(d):
        return copy(gacc, gin.at[c], s_grad.at[d], r_grad.at[c], block(d))

    def upper_part():
        for r in range(RT):
            adjoint_row(ti, r, a[r])
        for g in range(4):
            segments(g * GROUP, g, 1, 4 + g)
        for w in range(WIN):
            upper = landed(0, 1, 4, w)
            for g in range(1, 4):
                upper = upper + landed(g, 1, 4 + g, w)
            u[w] = upper

    def adjoint_part(n, slot):
        for r in range(WIN):
            adjoint_row(te, r, u[r])
        segments(0, 0, 0, 3)
        for g in range(4):
            segments((1 + g) * GROUP, 1 + g, 1, g)
        segments(5 * GROUP, 5, 2, 0)

        def wide(i):
            total = None
            terms = []
            if i < WIN:
                terms.append(landed(0, 0, 3, i))
            if RT <= i < RT + WIN:
                for g in range(4):
                    terms.append(landed(1 + g, 1, g, i - RT))
                if n is not None:
                    terms.append(-(bend[n, i - RT] * u[i - RT]))
            if i >= 2 * RT:
                terms.append(landed(5, 2, 0, i - 2 * RT))
            for term in terms:
                total = term if total is None else total + term
            return total

        for j in range(RT // 2):
            for side, base in ((0, NB), (1, EDGE + RT)):
                pair = jnp.concatenate([wide(base + 2 * j), wide(base + 2 * j + 1)], axis=0)
                out1[slot, side, j] = pair.astype(bf16)
        for j in range(half_nb):
            for side, base in ((0, 0), (1, EDGE + 2 * RT)):
                pair = jnp.concatenate([wide(base + 2 * j), wide(base + 2 * j + 1)], axis=0)
                out2[slot, side, j] = pair.astype(bf16)
        for cp in adjoint_copies(slot):
            cp.start()
        for i in range(RT):
            part[i] = wide(EDGE + i)

    def adjoint_sum(slot):
        for cp in adjoint_copies(slot):
            cp.wait_recv()
        for j in range(RT // 2):
            both = in1[slot, 0, j].astype(f32) + in1[slot, 1, j].astype(f32)
            if j < half_nb:
                both = both + in2[slot, 0, j].astype(f32)
            if j >= RT // 2 - half_nb:
                both = both + in2[slot, 1, j - (RT // 2 - half_nb)].astype(f32)
            a[2 * j] = part[2 * j] + both[:ROWS]
            a[2 * j + 1] = part[2 * j + 1] + both[ROWS:]

    upper_copies = [
        copy(upper_out.at[0], upper_in.at[1], s_upper.at[0], r_upper.at[1], block(-1)),
        copy(upper_out.at[1], upper_in.at[0], s_upper.at[1], r_upper.at[0], block(1)),
    ]

    def first_part():
        upper_part()
        for j in range(half_nb):
            for side, base in ((0, 0), (1, NB + RT)):
                pair = jnp.concatenate([u[base + 2 * j], u[base + 2 * j + 1]], axis=0)
                upper_out[side, j] = pair.astype(bf16)
        for cp in upper_copies:
            cp.start()
        for i in range(RT):
            upper_full[i] = u[NB + i]
        adjoint_part(None, 0)

    def first_sum():
        adjoint_sum(0)
        for cp in upper_copies:
            cp.wait_recv()
        for j in range(half_nb):
            for side, base in ((0, 0), (1, RT - NB)):
                pair = upper_in[side, j].astype(f32)
                upper_full[base + 2 * j] = upper_full[base + 2 * j] + pair[:ROWS]
                upper_full[base + 2 * j + 1] = upper_full[base + 2 * j + 1] + pair[ROWS:]

    @pl.loop(0, STEPS - 1)
    def _(n):
        slot = lax.rem(n, 2)
        for i in range(RT):
            exchange_at(n, NB + i)

        @pl.when(n == 1)
        def _():
            first_part()

        @pl.when(n == 3)
        def _():
            first_sum()

        forward_step(n, slot)

        @pl.when(n > 0)
        def _():
            for cp in state_copies(1 - slot):
                cp.wait_send()

        pack_state(1 - slot)
        for cp in state_copies(1 - slot):
            cp.start()

    last = STEPS - 1
    grad = gacc[...]
    for i in range(RT):
        exchange_at(last, NB + i)
        a[i] = a[i] - bend[last, NB + i] * upper_full[i]
        grad = grad + upper_full[i] * gas[last, NB + i]
    gacc[...] = grad

    final_stays = pltpu.make_async_copy(leaving.at[0], out_ref.at[0], l_sem.at[0])
    final_copy = copy(leaving.at[0], out_ref.at[0], s_out.at[0], r_out.at[0], partner)
    adj_stays = pltpu.make_async_copy(leaving.at[1], out_ref.at[1], l_sem.at[1])
    adj_copy = copy(leaving.at[1], out_ref.at[1], s_out.at[1], r_out.at[1], partner)
    grad_swap = copy(grad_out, grad_in, s_out.at[2], r_out.at[2], partner)

    @pl.loop(1, STEPS)
    def _(back):
        n = STEPS - 1 - back
        slot = lax.rem(back, 2)
        upper_part()
        grad = gacc[...]
        for w in range(WIN):
            grad = grad + u[w] * gas[n, w]
        gacc[...] = grad

        @pl.when(back == STEPS - 1)
        def _():
            for d in range(1, n_cells):
                grad_copy(d).start()

        @pl.when(back > 1)
        def _():
            for cp in adjoint_copies(slot):
                cp.wait_send()

        adjoint_part(n, slot)

        @pl.when(back == 1)
        def _():
            forward_step(last, last % 2)
            for i in range(RT):
                leaving[0, :, i * TILE:(i + 1) * TILE] = x[EDGE + i]

            @pl.when(odd)
            def _():
                final_copy.start()

            @pl.when(jnp.logical_not(odd))
            def _():
                final_stays.start()

        adjoint_sum(slot)

    for i in range(RT):
        leaving[1, :, i * TILE:(i + 1) * TILE] = a[i]

    @pl.when(odd)
    def _():
        adj_copy.start()

    @pl.when(jnp.logical_not(odd))
    def _():
        adj_stays.start()

    total = gacc[...]
    for d in range(1, n_cells):
        source = rem(c - d, n_cells)
        copy(gacc, gin.at[source], s_grad.at[d], r_grad.at[source], block(d)).wait_recv()
        total = total + gin[source]
    scale = 1.0 / math.sqrt(n_cells * RT * TILE)
    grad_out[...] = jnp.broadcast_to(jnp.sum(total, axis=1, keepdims=True) * scale, (ROWS, TILE))

    @pl.when(odd)
    def _():
        grad_swap.start()

    for d in range(1, n_cells):
        grad_copy(d).wait_send()
    for slot in range(2):
        for cp in adjoint_copies(slot):
            cp.wait_send()
        for cp in state_copies(slot):
            cp.wait_send()
    for cp in upper_copies:
        cp.wait_send()

    @pl.when(odd)
    def _():
        grad_swap.wait()
        final_copy.wait()
        adj_copy.wait()
        grad_ref[...] = grad_in[...]

    @pl.when(jnp.logical_not(odd))
    def _():
        final_stays.wait()
        adj_stays.wait()
        grad_ref[...] = grad_out[...]


def solution(mesh):
    n_cells = mesh.shape["cells"]

    def body(init_state, tiles_exp, cols_exp, tiles_imp, cols_imp, surface, piston, atmosphere, final_cot):
        vmem, smem = pl.BlockSpec(memory_space=pltpu.VMEM), pl.BlockSpec(memory_space=pltpu.SMEM)
        anywhere = pl.BlockSpec(memory_space=pl.ANY)
        dma, i32 = pltpu.SemaphoreType.DMA, jnp.int32
        scratch = [
            pltpu.VMEM((WIN, K, TILE, TILE), bf16),
            pltpu.VMEM((RT, K, TILE, TILE), bf16),
            pltpu.VMEM((WIDE, ROWS, TILE), f32),
            pltpu.VMEM((WIN, ROWS, TILE), f32),
            pltpu.VMEM((STEPS, WIN, ROWS, TILE), f32),
            pltpu.VMEM((STEPS, WIN, ROWS, TILE), f32),
            pltpu.VMEM((WIN, ROWS, TILE), f32),
            pltpu.VMEM((4, 8, TILE), i32),
            pltpu.VMEM((2, 4, 8, TILE), i32),
            pltpu.SMEM((3, 4, 8, TILE), i32),
            pltpu.VMEM((RT, TILE), f32),
            pltpu.VMEM((2, RT, TILE), f32),
            pltpu.VMEM((2, RT // 2, 2 * ROWS, TILE), bf16),
            pltpu.VMEM((2, 2, RT // 2, 2 * ROWS, TILE), bf16),
            pltpu.VMEM((2, 2, NB // 2, 2 * ROWS, TILE), bf16),
            pltpu.VMEM((RT, ROWS, TILE), f32),
            pltpu.VMEM((WIN, ROWS, TILE), f32),
            pltpu.VMEM((RT, ROWS, TILE), f32),
            pltpu.VMEM((WIN * K, ROWS, TILE), f32),
            pltpu.VMEM((6 * SEG, ROWS, TILE), f32),
            pltpu.VMEM((2, 2, RT // 2, 2 * ROWS, TILE), bf16),
            pltpu.VMEM((2, 2, NB // 2, 2 * ROWS, TILE), bf16),
            pltpu.VMEM((2, 2, RT // 2, 2 * ROWS, TILE), bf16),
            pltpu.VMEM((2, 2, NB // 2, 2 * ROWS, TILE), bf16),
            pltpu.VMEM((ROWS, TILE), f32),
            pltpu.VMEM((n_cells, ROWS, TILE), f32),
            pltpu.VMEM((2, ROWS, TILE), f32),
            pltpu.VMEM((2, ROWS, TILE), f32),
            pltpu.VMEM((2, ROWS, TILE), f32),
            pltpu.VMEM((2, ROWS, RT * TILE), f32),
            pltpu.VMEM((2, ROWS, RT * TILE), f32),
            pltpu.VMEM((RT, TILE), i32),
            pltpu.VMEM((ROWS, TILE), f32),
            pltpu.VMEM((ROWS, TILE), f32),
            pltpu.VMEM((2, NB // 2, 2 * ROWS, TILE), bf16),
            pltpu.VMEM((2, NB // 2, 2 * ROWS, TILE), bf16),
            pltpu.VMEM((RT, ROWS, TILE), f32),
            pltpu.VMEM((10 * GROUP, ROWS, TILE), f32),
            dma((2,)), dma((2,)),
            dma((3,)), dma((3,)),
            dma((3,)), dma((3,)),
            dma((4,)), dma((4,)), dma((5,)),
            dma((14,)), dma((14,)), dma((16,)), dma((16,)),
            dma((2, 2)), dma((2, 2)), dma((2, 2)), dma((2, 2)),
            dma((2, 4)), dma((2, 4)), dma((2, 4)), dma((2, 4)),
            dma((n_cells,)), dma((n_cells,)),
        ]

        def run(*refs):
            kernel(n_cells, *refs)

        states = jax.ShapeDtypeStruct((2, ROWS, RT * TILE), f32)
        both, grad = pl.pallas_call(
            run,
            out_shape=(states, jax.ShapeDtypeStruct((ROWS, TILE), f32)),
            in_specs=[anywhere, anywhere, anywhere, smem, smem, anywhere, smem, smem, anywhere],
            out_specs=(anywhere, vmem),
            scratch_shapes=scratch,
            compiler_params=pltpu.CompilerParams(
                collective_id=0, has_side_effects=True, vmem_limit_bytes=60 << 20
            ),
        )(
            init_state, tiles_exp, tiles_imp, cols_exp.T, cols_imp.T, surface.reshape(RT, TILE),
            piston, atmosphere, final_cot,
        )
        return both[0], both[1], grad[:, 0]

    placed = (
        P("samples", "cells"),
        P(("cells", "samples"), None, None, None),
        P("cells", None),
        P(("cells", "samples"), None, None, None),
        P("cells", None),
        P("cells"),
        P("samples"),
        P("samples"),
        P("samples", "cells"),
    )
    return jax.shard_map(
        body,
        mesh=mesh,
        in_specs=placed,
        out_specs=(P("samples", "cells"), P("samples", "cells"), P("samples")),
        check_vma=False,
    )
```

```python
import math

import jax
import jax.numpy as jnp
from jax import lax
from jax.experimental import pallas as pl
from jax.experimental.pallas import tpu as pltpu
from jax.sharding import PartitionSpec as P

STEPS = 8
RT = 16
K = 6
NB = 4
TILE = 128
ROWS = 8
GROUP = 4 * K
WIN = RT + 2 * NB
WIDE = WIN + 2 * RT
LOW = RT - NB
EDGE = RT + NB
SEG = GROUP + 1

step_length = 0.5
buffer_gain = 0.5
MESH = pl.DeviceIdType.MESH
f32, bf16 = jnp.float32, jnp.bfloat16


def kernel(
    n_cells,
    init_ref, te_ref, ti_ref, cols_exp_ref, cols_imp_ref, surf_ref, piston_ref, air_ref, cot_ref,
    out_ref, grad_ref,
    te, ti, x, src, gas, bend, half, meta, meta_in, idx,
    surf_own, surf_in, send1, recv1, recv2, a, u, part, contrib, seg,
    out1, out2, in1, in2, gacc, gin, levels, levels_in, levels_used, states, leaving, surf_int, end1, end2, part_in, upper_out, upper_in, upper_full, same,
    s_upper, r_upper, s_end, r_end, s_out, r_out, s_swap, r_swap, s_small, r_small, l_sem, s_gather, r_gather, s_core, r_core, s_halo, r_halo, s_hcore, r_hcore,
    s_fwd, r_fwd, s_adj, r_adj, s_grad, r_grad,
):
    c = lax.axis_index("cells")
    s = lax.axis_index("samples")
    y, l, k = s // 4, (s // 2) % 2, s % 2

    def rem(v, m):
        return lax.rem(v + m, m)

    def block(delta):
        return (rem(c + delta, n_cells), s if delta % 2 == 0 else s + 3 - 2 * (s % 4))

    def plane(yy, ll, kk):
        return (c, yy * 4 + ll * 2 + kk)

    up, down = plane(rem(y + 1, 4), l, k), plane(rem(y - 1, 4), l, k)
    across, other = plane(y, 1 - l, k), plane(y, l, 1 - k)
    partner = plane(y, 1 - l, 1 - k)
    odd = lax.rem(c, 2) == 1

    def copy(source, target, send, recv, device):
        return pltpu.make_async_remote_copy(source, target, send, recv, device_id=device, device_id_type=MESH)

    barrier = pltpu.get_barrier_semaphore()
    flip = 3 - 2 * (s % 4)

    def owner_of(delta):
        return (rem(c + delta, n_cells), s + lax.rem(c, 2) * flip)

    def worker(delta):
        there = rem(c + delta, n_cells)
        return (there, s + lax.rem(there, 2) * flip)

    peers = [up, down, across, other, partner] + [block(d) for d in (-2, -1, 1, 2)]
    peers = peers + [worker(d) for d in range(1, n_cells)]
    for device in peers:
        pl.semaphore_signal(barrier, inc=1, device_id=device, device_id_type=MESH)

    own_tiles = [
        pltpu.make_async_copy(te_ref.at[0], te.at[NB + s], l_sem.at[0]),
        pltpu.make_async_copy(ti_ref.at[0], ti.at[s], l_sem.at[1]),
    ]
    for cp in own_tiles:
        cp.start()
    surf_copy = pltpu.make_async_copy(surf_ref, surf_int, l_sem.at[2])
    surf_copy.start()
    stay = [
        pltpu.make_async_copy(init_ref, states.at[0], l_sem.at[3]),
        pltpu.make_async_copy(cot_ref, states.at[1], l_sem.at[4]),
    ]

    @pl.when(jnp.logical_not(odd))
    def _():
        for cp in stay:
            cp.start()

    row_of = lax.broadcasted_iota(jnp.int32, (ROWS, TILE), 0)
    piston = jnp.zeros((ROWS, TILE), f32)
    air = jnp.zeros((ROWS, TILE), f32)
    for i in range(ROWS):
        piston = jnp.where(row_of == i, piston_ref[i], piston)
        air = jnp.where(row_of == i, air_ref[i], air)
    levels[0] = piston
    levels[1] = air

    def pack_state(slot):
        for j in range(RT // 2):
            pair = jnp.concatenate([x[EDGE + 2 * j], x[EDGE + 2 * j + 1]], axis=0)
            send1[slot, j] = pair.astype(bf16)

    half_nb = NB // 2

    def state_copies(slot):
        mine = send1.at[slot]
        return [
            copy(mine, recv1.at[slot, 1], s_fwd.at[slot, 0], r_fwd.at[slot, 1], block(-1)),
            copy(mine, recv1.at[slot, 0], s_fwd.at[slot, 1], r_fwd.at[slot, 0], block(1)),
            copy(mine.at[pl.ds(0, half_nb)], recv2.at[slot, 1], s_fwd.at[slot, 2], r_fwd.at[slot, 3], block(-2)),
            copy(mine.at[pl.ds(RT // 2 - half_nb, half_nb)], recv2.at[slot, 0], s_fwd.at[slot, 3], r_fwd.at[slot, 2], block(2)),
        ]

    pl.semaphore_wait(barrier, len(peers))
    swap = [
        copy(init_ref, states.at[0], s_swap.at[0], r_swap.at[0], partner),
        copy(cot_ref, states.at[1], s_swap.at[1], r_swap.at[1], partner),
        copy(levels, levels_in, s_swap.at[2], r_swap.at[2], partner),
    ]

    buf = (te, ti)

    def tile_at(which, yy, ll, kk):
        row = yy * 4 + ll * 2 + kk
        return te.at[NB + row] if which == 0 else ti.at[row]

    gathers = {}

    def hop(name, which, yy, ll, device, source=None):
        at = tile_at(which, yy, ll, k)
        number = len(gathers)
        cp = copy(at if source is None else source, at, s_gather.at[number], r_gather.at[number], device)
        gathers[name] = (number, cp)
        cp.start()

    def arrived(name, which, yy, ll):
        number, cp = gathers[name]
        at = tile_at(which, yy, ll, k)
        copy(at, at, s_gather.at[number], r_gather.at[number], up).wait_recv()
        spread(which, yy, ll)

    core_sent = []
    halo_sent = []

    def spread(which, yy, ll):
        number = len(core_sent)
        at = tile_at(which, yy, ll, k)
        slot = which * 8 + yy * 2 + ll
        cp = copy(at, at, s_core.at[number], r_core.at[slot], other)
        core_sent.append(cp)
        cp.start()
        if which == 0:
            @pl.when(yy == 3)
            def _():
                copy(at, te.at[ll * 2 + k], s_halo.at[0, ll], r_halo.at[0, ll], block(1)).start()

            @pl.when(yy == 0)
            def _():
                copy(at, te.at[NB + RT + ll * 2 + k], s_halo.at[1, ll], r_halo.at[1, ll], block(-1)).start()

    ym, yp, yo, lo = rem(y - 1, 4), rem(y + 1, 4), rem(y + 2, 4), 1 - l
    for w, own in enumerate((te_ref.at[0], ti_ref.at[0])):
        hop(("up", w), w, y, l, up, own)
        hop(("down", w), w, y, l, down, own)
        hop(("x", w), w, y, l, across, own)
    @pl.when(odd)
    def _():
        for cp in swap:
            cp.start()

    for w in range(2):
        own_tiles[w].wait()
        spread(w, y, l)
    gacc[...] = jnp.zeros((ROWS, TILE), f32)
    for g in range(6):
        seg[g * SEG + GROUP] = jnp.zeros((ROWS, TILE), f32)

    lane = lax.broadcasted_iota(jnp.int32, (8, TILE), 1)
    spot = lax.broadcasted_iota(jnp.int32, (8, TILE), 0) * TILE + lane
    cols = jnp.zeros((8, TILE), jnp.int32)
    for m, ref in enumerate((cols_exp_ref, cols_imp_ref)):
        for r in range(RT):
            for j in range(K):
                cols = jnp.where(spot == (4 * m + r // 4) * TILE + (r % 4) * K + j, ref[j, r], cols)
    cols = jnp.clip(cols, LOW, LOW + WIN - 1)
    key = cols * 32 + lane
    rank = jnp.zeros((8, TILE), jnp.int32)
    upto = jnp.zeros((8, TILE), jnp.int32)
    here = jnp.zeros((8, TILE), jnp.int32)
    for i in range(GROUP):
        one = jnp.broadcast_to(cols[:, i:i + 1], (8, TILE))
        rank = rank + jnp.where(one * 32 + i < key, 1, 0)
        upto = upto + jnp.where(one - LOW <= lane, 1, 0)
        here = here + jnp.where(one - LOW == lane, 1, 0)
    order = jnp.zeros((8, TILE), jnp.int32)
    ordered = jnp.zeros((8, TILE), jnp.int32)
    before = jnp.zeros((8, TILE), jnp.int32)
    for i in range(GROUP):
        place = jnp.broadcast_to(rank[:, i:i + 1], (8, TILE))
        one = jnp.broadcast_to(cols[:, i:i + 1], (8, TILE))
        order = order + jnp.where(place == lane, i, 0)
        ordered = ordered + jnp.where(place == lane, one, 0)
        before = before + jnp.where(place + 1 == lane, one, 0)
    meta[0] = cols
    meta[1] = order
    meta[2] = jnp.where(ordered == before, 1, 0)
    meta[3] = jnp.where(here > 0, upto - 1, GROUP)

    surf_copy.wait()
    surf_own[...] = surf_int[...].astype(f32) * step_length
    small = []
    for side, device in ((0, block(1)), (1, block(-1))):
        small.append(copy(surf_own, surf_in.at[side], s_small.at[side], r_small.at[side], device))
        small.append(copy(meta, meta_in.at[side], s_small.at[2 + side], r_small.at[2 + side], device))
    for cp in small:
        cp.start()
    own_idx = pltpu.make_async_copy(meta, idx.at[1], l_sem.at[2])
    own_idx.start()


    arrived(("x", 0), 0, y, lo)
    hop(("xup", 0), 0, y, lo, up)
    hop(("xdown", 0), 0, y, lo, down)
    arrived(("up", 0), 0, ym, l)
    hop(("far", 0), 0, ym, l, up)
    arrived(("down", 0), 0, yp, l)
    arrived(("down", 1), 1, yp, l)
    hop(("far", 1), 1, yp, l, down)
    hop(("xd", 1), 1, yp, l, across)
    arrived(("up", 1), 1, ym, l)
    hop(("xu", 1), 1, ym, l, across)
    arrived(("x", 1), 1, y, lo)

    @pl.when(odd)
    def _():
        for cp in swap:
            cp.wait_recv()
        levels_used[...] = levels_in[...]

    @pl.when(jnp.logical_not(odd))
    def _():
        for cp in stay:
            cp.wait()
        levels_used[...] = levels[...]

    piston = levels_used[0]
    air = levels_used[1]
    for i in range(RT):
        x[EDGE + i] = states[0, :, i * TILE:(i + 1) * TILE]
        a[i] = states[1, :, i * TILE:(i + 1) * TILE]
    pack_state(0)
    for cp in state_copies(0):
        cp.start()

    for cp in small:
        cp.wait()
    moves = [pltpu.make_async_copy(meta_in.at[side], idx.at[2 * side], l_sem.at[3 + side]) for side in range(2)]
    for cp in moves:
        cp.start()
    for i in range(NB):
        half[i] = jnp.broadcast_to(surf_in[0, pl.ds(RT - NB + i, 1), :], (ROWS, TILE))
        half[NB + RT + i] = jnp.broadcast_to(surf_in[1, pl.ds(i, 1), :], (ROWS, TILE))
    for i in range(RT):
        half[NB + i] = jnp.broadcast_to(surf_own[pl.ds(i, 1), :], (ROWS, TILE))

    arrived(("xup", 0), 0, ym, lo)
    hop(("farx", 0), 0, ym, lo, up)
    arrived(("xdown", 0), 0, yp, lo)
    arrived(("xd", 1), 1, yp, lo)
    hop(("farx", 1), 1, yp, lo, down)
    arrived(("far", 0), 0, yo, l)
    own_idx.wait()
    for cp in moves:
        cp.wait()
    groups = [(0, 3)] + [(1, g) for g in range(8)] + [(2, 0)]
    first_of = {at: i * GROUP for i, at in enumerate(groups)}
    for owner, group in groups:
        for p in range(1, GROUP):
            factor = idx[owner, 2, group, p].astype(f32)
            same[first_of[owner, group] + p] = jnp.full((ROWS, TILE), factor, f32)
    arrived(("far", 1), 1, yo, l)
    arrived(("xu", 1), 1, ym, lo)
    arrived(("farx", 0), 0, yo, lo)
    arrived(("farx", 1), 1, yo, lo)
    hcore = []
    for side in range(2):
        for ll in range(2):
            base = 0 if side == 0 else NB + RT
            at = te.at[base + ll * 2 + 1 - k]
            copy(at, at, s_halo.at[side, ll], r_halo.at[side, ll], other).wait_recv()
            cp = copy(at, at, s_hcore.at[side, ll], r_hcore.at[side, ll], other)
            cp.start()
            hcore.append(cp)

    @pl.when(odd)
    def _():
        for cp in swap:
            cp.wait_send()

    for _, cp in gathers.values():
        cp.wait_send()
    for cp in core_sent:
        cp.wait_send()
    for w in range(2):
        for yy in range(4):
            for ll in range(2):
                at = tile_at(w, yy, ll, 1 - k)
                copy(at, at, s_core.at[0], r_core.at[w * 8 + yy * 2 + ll], other).wait_recv()
    for side in range(2):
        for ll in range(2):
            at = te.at[ll]
            copy(at, at, s_halo.at[side, ll], r_halo.at[side, ll], other).wait_send()
    for cp in hcore:
        cp.wait()

    def exchange_at(n, w):
        t = x[RT + w]
        th = jnp.tanh(t)
        hs = half[w]
        gas[n, w] = hs * (air - t * (1.0 + buffer_gain * th))
        bend[n, w] = hs * piston * (1.0 + buffer_gain * th + buffer_gain * t * (1.0 - th * th))

    wide_rows = []
    for r in range(NB):
        wide_rows.append((r, 0, 3, r, -LOW))
    for r in range(RT):
        wide_rows.append((NB + r, 1, r // 4, r % 4, NB))
    for r in range(NB):
        wide_rows.append((NB + RT + r, 2, 0, r, NB + RT))

    def forward_row(tiles, row, field, owner, group, place, shift):
        picked = [field[idx[owner, 0, group, place * K + j] + shift] for j in range(K)]
        values = jnp.concatenate(picked, axis=1).astype(bf16)
        weights = jnp.concatenate([tiles[row, j] for j in range(K)], axis=1)
        return lax.dot_general(values, weights, (((1,), (1,)), ((), ())), preferred_element_type=f32)

    def forward_step(n, slot):
        for cp in state_copies(slot):
            cp.wait_recv()
        for j in range(RT // 2):
            for side, base in ((0, NB), (1, EDGE + RT)):
                pair = recv1[slot, side, j].astype(f32)
                x[base + 2 * j] = pair[:ROWS]
                x[base + 2 * j + 1] = pair[ROWS:]
        for j in range(half_nb):
            for side, base in ((0, 0), (1, EDGE + RT + RT)):
                pair = recv2[slot, side, j].astype(f32)
                x[base + 2 * j] = pair[:ROWS]
                x[base + 2 * j + 1] = pair[ROWS:]
        for i in range(NB):
            exchange_at(n, i)
            exchange_at(n, NB + RT + i)
        for row, owner, group, place, shift in wide_rows:
            moved = forward_row(te, row, x, owner, group, place, shift)
            src[row] = moved + piston * gas[n, row]
        for r in range(RT):
            x[EDGE + r] = forward_row(ti, r, src, 1, 4 + r // 4, r % 4, -LOW)

    def segments(first, number, owner, group):
        total = None
        for p in range(GROUP):
            value = contrib[first + idx[owner, 1, group, p]]
            if p > 0:
                value = value + total * same[first_of[owner, group] + p]
            total = value
            seg[number * SEG + p] = total

    def landed(number, owner, group, w):
        return seg[number * SEG + idx[owner, 3, group, w]]

    def adjoint_row(tiles, row, field):
        weights = jnp.concatenate([tiles[row, j] for j in range(K)], axis=1)
        spread_out = jnp.dot(field.astype(bf16), weights, preferred_element_type=f32)
        for j in range(K):
            contrib[row * K + j] = spread_out[:, j * TILE:(j + 1) * TILE]

    def adjoint_copies(slot):
        return [
            copy(out1.at[slot, 0], in1.at[slot, 1], s_adj.at[slot, 0], r_adj.at[slot, 1], block(-1)),
            copy(out1.at[slot, 1], in1.at[slot, 0], s_adj.at[slot, 1], r_adj.at[slot, 0], block(1)),
            copy(out2.at[slot, 0], in2.at[slot, 1], s_adj.at[slot, 2], r_adj.at[slot, 3], block(-2)),
            copy(out2.at[slot, 1], in2.at[slot, 0], s_adj.at[slot, 3], r_adj.at[slot, 2], block(2)),
        ]

    end = (STEPS - 1) % 2
    closing = [
        copy(out1.at[end, 0], end1.at[1], s_end.at[0], r_end.at[1], owner_of(-1)),
        copy(out1.at[end, 1], end1.at[0], s_end.at[1], r_end.at[0], owner_of(1)),
        copy(out2.at[end, 0], end2.at[1], s_end.at[2], r_end.at[3], owner_of(-2)),
        copy(out2.at[end, 1], end2.at[0], s_end.at[3], r_end.at[2], owner_of(2)),
    ]
    part_copy = copy(part, part_in, s_end.at[4], r_end.at[4], partner)

    def grad_copy(d):
        return copy(gacc, gin.at[c], s_grad.at[d], r_grad.at[c], owner_of(d))

    def upper_part():
        for r in range(RT):
            adjoint_row(ti, r, a[r])
        for g in range(4):
            segments(g * GROUP, g, 1, 4 + g)
        for w in range(WIN):
            upper = landed(0, 1, 4, w)
            for g in range(1, 4):
                upper = upper + landed(g, 1, 4 + g, w)
            u[w] = upper

    def adjoint_part(n, slot):
        for r in range(WIN):
            adjoint_row(te, r, u[r])
        segments(0, 0, 0, 3)
        for g in range(4):
            segments((1 + g) * GROUP, 1 + g, 1, g)
        segments(5 * GROUP, 5, 2, 0)

        def wide(i):
            total = None
            terms = []
            if i < WIN:
                terms.append(landed(0, 0, 3, i))
            if RT <= i < RT + WIN:
                for g in range(4):
                    terms.append(landed(1 + g, 1, g, i - RT))
                if n is not None:
                    terms.append(-(bend[n, i - RT] * u[i - RT]))
            if i >= 2 * RT:
                terms.append(landed(5, 2, 0, i - 2 * RT))
            for term in terms:
                total = term if total is None else total + term
            return total

        for j in range(RT // 2):
            for side, base in ((0, NB), (1, EDGE + RT)):
                pair = jnp.concatenate([wide(base + 2 * j), wide(base + 2 * j + 1)], axis=0)
                out1[slot, side, j] = pair.astype(bf16)
        for j in range(half_nb):
            for side, base in ((0, 0), (1, EDGE + 2 * RT)):
                pair = jnp.concatenate([wide(base + 2 * j), wide(base + 2 * j + 1)], axis=0)
                out2[slot, side, j] = pair.astype(bf16)
        if n is None:
            for cp in adjoint_copies(slot):
                cp.start()
        else:
            @pl.when(n > 0)
            def _():
                for cp in adjoint_copies(slot):
                    cp.start()

            @pl.when(n == 0)
            def _():
                for cp in closing:
                    cp.start()

        for i in range(RT):
            part[i] = wide(EDGE + i)

    def adjoint_sum(slot):
        for cp in adjoint_copies(slot):
            cp.wait_recv()
        for j in range(RT // 2):
            both = in1[slot, 0, j].astype(f32) + in1[slot, 1, j].astype(f32)
            if j < half_nb:
                both = both + in2[slot, 0, j].astype(f32)
            if j >= RT // 2 - half_nb:
                both = both + in2[slot, 1, j - (RT // 2 - half_nb)].astype(f32)
            a[2 * j] = part[2 * j] + both[:ROWS]
            a[2 * j + 1] = part[2 * j + 1] + both[ROWS:]

    upper_copies = [
        copy(upper_out.at[0], upper_in.at[1], s_upper.at[0], r_upper.at[1], block(-1)),
        copy(upper_out.at[1], upper_in.at[0], s_upper.at[1], r_upper.at[0], block(1)),
    ]

    def first_part():
        upper_part()
        for j in range(half_nb):
            for side, base in ((0, 0), (1, NB + RT)):
                pair = jnp.concatenate([u[base + 2 * j], u[base + 2 * j + 1]], axis=0)
                upper_out[side, j] = pair.astype(bf16)
        for cp in upper_copies:
            cp.start()
        for i in range(RT):
            upper_full[i] = u[NB + i]
        adjoint_part(None, 0)

    def first_sum():
        adjoint_sum(0)
        for cp in upper_copies:
            cp.wait_recv()
        for j in range(half_nb):
            for side, base in ((0, 0), (1, RT - NB)):
                pair = upper_in[side, j].astype(f32)
                upper_full[base + 2 * j] = upper_full[base + 2 * j] + pair[:ROWS]
                upper_full[base + 2 * j + 1] = upper_full[base + 2 * j + 1] + pair[ROWS:]

    @pl.loop(0, STEPS - 1)
    def _(n):
        slot = lax.rem(n, 2)
        for i in range(RT):
            exchange_at(n, NB + i)

        @pl.when(n == 1)
        def _():
            first_part()

        @pl.when(n == 3)
        def _():
            first_sum()

        forward_step(n, slot)

        @pl.when(n > 0)
        def _():
            for cp in state_copies(1 - slot):
                cp.wait_send()

        pack_state(1 - slot)
        for cp in state_copies(1 - slot):
            cp.start()

    last = STEPS - 1
    grad = gacc[...]
    for i in range(RT):
        exchange_at(last, NB + i)
        a[i] = a[i] - bend[last, NB + i] * upper_full[i]
        grad = grad + upper_full[i] * gas[last, NB + i]
    gacc[...] = grad

    final_stays = pltpu.make_async_copy(leaving.at[0], out_ref.at[0], l_sem.at[0])
    final_copy = copy(leaving.at[0], out_ref.at[0], s_out.at[0], r_out.at[0], partner)
    adj_stays = pltpu.make_async_copy(leaving.at[1], out_ref.at[1], l_sem.at[1])

    @pl.loop(1, STEPS)
    def _(back):
        n = STEPS - 1 - back
        slot = lax.rem(back, 2)
        upper_part()
        grad = gacc[...]
        for w in range(WIN):
            grad = grad + u[w] * gas[n, w]
        gacc[...] = grad

        @pl.when(back == STEPS - 1)
        def _():
            for d in range(1, n_cells):
                grad_copy(d).start()

            @pl.when(odd)
            def _():
                grad_copy(0).start()

        @pl.when(back > 1)
        def _():
            for cp in adjoint_copies(slot):
                cp.wait_send()

        adjoint_part(n, slot)

        @pl.when(back == 1)
        def _():
            forward_step(last, last % 2)
            for i in range(RT):
                leaving[0, :, i * TILE:(i + 1) * TILE] = x[EDGE + i]

            @pl.when(odd)
            def _():
                final_copy.start()

            @pl.when(jnp.logical_not(odd))
            def _():
                final_stays.start()

        @pl.when(back < STEPS - 1)
        def _():
            adjoint_sum(slot)

    @pl.when(odd)
    def _():
        part_copy.start()
        part_copy.wait_recv()
        for i in range(RT):
            a[i] = part_in[i]

    @pl.when(jnp.logical_not(odd))
    def _():
        for i in range(RT):
            a[i] = part[i]

    for cp in closing:
        cp.wait_recv()
    for j in range(RT // 2):
        both = end1[0, j].astype(f32) + end1[1, j].astype(f32)
        if j < half_nb:
            both = both + end2[0, j].astype(f32)
        if j >= RT // 2 - half_nb:
            both = both + end2[1, j - (RT // 2 - half_nb)].astype(f32)
        for h in range(2):
            i = 2 * j + h
            leaving[1, :, i * TILE:(i + 1) * TILE] = a[i] + both[h * ROWS:(h + 1) * ROWS]

    adj_stays.start()

    @pl.when(odd)
    def _():
        grad_copy(0).wait_recv()
        part_copy.wait_send()

    @pl.when(jnp.logical_not(odd))
    def _():
        gin[c] = gacc[...]

    total = gin[c]
    for d in range(1, n_cells):
        source = rem(c - d, n_cells)
        copy(gacc, gin.at[source], s_grad.at[d], r_grad.at[source], owner_of(d)).wait_recv()
        total = total + gin[source]
    scale = 1.0 / math.sqrt(n_cells * RT * TILE)
    grad_ref[...] = jnp.broadcast_to(jnp.sum(total, axis=1, keepdims=True) * scale, (ROWS, TILE))

    for d in range(1, n_cells):
        grad_copy(d).wait_send()
    for cp in adjoint_copies(1 - end):
        cp.wait_send()
    for cp in closing:
        cp.wait_send()
    for slot in range(2):
        for cp in state_copies(slot):
            cp.wait_send()
    for cp in upper_copies:
        cp.wait_send()

    @pl.when(odd)
    def _():
        grad_copy(0).wait_send()
        final_copy.wait()

    @pl.when(jnp.logical_not(odd))
    def _():
        final_stays.wait()

    adj_stays.wait()


def solution(mesh):
    n_cells = mesh.shape["cells"]

    def body(init_state, tiles_exp, cols_exp, tiles_imp, cols_imp, surface, piston, atmosphere, final_cot):
        vmem, smem = pl.BlockSpec(memory_space=pltpu.VMEM), pl.BlockSpec(memory_space=pltpu.SMEM)
        anywhere = pl.BlockSpec(memory_space=pl.ANY)
        dma, i32 = pltpu.SemaphoreType.DMA, jnp.int32
        scratch = [
            pltpu.VMEM((WIN, K, TILE, TILE), bf16),
            pltpu.VMEM((RT, K, TILE, TILE), bf16),
            pltpu.VMEM((WIDE, ROWS, TILE), f32),
            pltpu.VMEM((WIN, ROWS, TILE), f32),
            pltpu.VMEM((STEPS, WIN, ROWS, TILE), f32),
            pltpu.VMEM((STEPS, WIN, ROWS, TILE), f32),
            pltpu.VMEM((WIN, ROWS, TILE), f32),
            pltpu.VMEM((4, 8, TILE), i32),
            pltpu.VMEM((2, 4, 8, TILE), i32),
            pltpu.SMEM((3, 4, 8, TILE), i32),
            pltpu.VMEM((RT, TILE), f32),
            pltpu.VMEM((2, RT, TILE), f32),
            pltpu.VMEM((2, RT // 2, 2 * ROWS, TILE), bf16),
            pltpu.VMEM((2, 2, RT // 2, 2 * ROWS, TILE), bf16),
            pltpu.VMEM((2, 2, NB // 2, 2 * ROWS, TILE), bf16),
            pltpu.VMEM((RT, ROWS, TILE), f32),
            pltpu.VMEM((WIN, ROWS, TILE), f32),
            pltpu.VMEM((RT, ROWS, TILE), f32),
            pltpu.VMEM((WIN * K, ROWS, TILE), f32),
            pltpu.VMEM((6 * SEG, ROWS, TILE), f32),
            pltpu.VMEM((2, 2, RT // 2, 2 * ROWS, TILE), bf16),
            pltpu.VMEM((2, 2, NB // 2, 2 * ROWS, TILE), bf16),
            pltpu.VMEM((2, 2, RT // 2, 2 * ROWS, TILE), bf16),
            pltpu.VMEM((2, 2, NB // 2, 2 * ROWS, TILE), bf16),
            pltpu.VMEM((ROWS, TILE), f32),
            pltpu.VMEM((n_cells, ROWS, TILE), f32),
            pltpu.VMEM((2, ROWS, TILE), f32),
            pltpu.VMEM((2, ROWS, TILE), f32),
            pltpu.VMEM((2, ROWS, TILE), f32),
            pltpu.VMEM((2, ROWS, RT * TILE), f32),
            pltpu.VMEM((2, ROWS, RT * TILE), f32),
            pltpu.VMEM((RT, TILE), i32),
            pltpu.VMEM((2, RT // 2, 2 * ROWS, TILE), bf16),
            pltpu.VMEM((2, NB // 2, 2 * ROWS, TILE), bf16),
            pltpu.VMEM((RT, ROWS, TILE), f32),
            pltpu.VMEM((2, NB // 2, 2 * ROWS, TILE), bf16),
            pltpu.VMEM((2, NB // 2, 2 * ROWS, TILE), bf16),
            pltpu.VMEM((RT, ROWS, TILE), f32),
            pltpu.VMEM((10 * GROUP, ROWS, TILE), f32),
            dma((2,)), dma((2,)),
            dma((5,)), dma((5,)),
            dma((1,)), dma((1,)),
            dma((3,)), dma((3,)),
            dma((4,)), dma((4,)), dma((5,)),
            dma((14,)), dma((14,)), dma((16,)), dma((16,)),
            dma((2, 2)), dma((2, 2)), dma((2, 2)), dma((2, 2)),
            dma((2, 4)), dma((2, 4)), dma((2, 4)), dma((2, 4)),
            dma((n_cells,)), dma((n_cells,)),
        ]

        def run(*refs):
            kernel(n_cells, *refs)

        states = jax.ShapeDtypeStruct((2, ROWS, RT * TILE), f32)
        both, grad = pl.pallas_call(
            run,
            out_shape=(states, jax.ShapeDtypeStruct((ROWS, TILE), f32)),
            in_specs=[anywhere, anywhere, anywhere, smem, smem, anywhere, smem, smem, anywhere],
            out_specs=(anywhere, vmem),
            scratch_shapes=scratch,
            compiler_params=pltpu.CompilerParams(
                collective_id=0, has_side_effects=True, vmem_limit_bytes=60 << 20
            ),
        )(
            init_state, tiles_exp, tiles_imp, cols_exp.T, cols_imp.T, surface.reshape(RT, TILE),
            piston, atmosphere, final_cot,
        )
        return both[0], both[1], grad[:, 0]

    placed = (
        P("samples", "cells"),
        P(("cells", "samples"), None, None, None),
        P("cells", None),
        P(("cells", "samples"), None, None, None),
        P("cells", None),
        P("cells"),
        P("samples"),
        P("samples"),
        P("samples", "cells"),
    )
    return jax.shard_map(
        body,
        mesh=mesh,
        in_specs=placed,
        out_specs=(P("samples", "cells"), P("samples", "cells"), P("samples")),
        check_vma=False,
    )
```

```python
import math

import jax
import jax.numpy as jnp
from jax import lax
from jax.experimental import pallas as pl
from jax.experimental.pallas import tpu as pltpu
from jax.sharding import PartitionSpec as P

STEPS = 8
RT = 16
K = 6
NB = 4
TILE = 128
ROWS = 8
GROUP = 4 * K
WIN = RT + 2 * NB
WIDE = WIN + 2 * RT
LOW = RT - NB
EDGE = RT + NB
SEG = GROUP + 1

step_length = 0.5
buffer_gain = 0.5
MESH = pl.DeviceIdType.MESH
f32, bf16 = jnp.float32, jnp.bfloat16


def kernel(
    n_cells,
    init_ref, te_ref, ti_ref, cols_exp_ref, cols_imp_ref, surf_ref, piston_ref, air_ref, cot_ref,
    out_ref, grad_ref,
    te, ti, x, src, gas, bend, half, meta, meta_in, idx,
    surf_own, surf_in, send1, recv1, recv2, a, u, part, contrib, seg,
    out1, out2, in1, in2, gacc, gin, levels, levels_in, levels_used, states, leaving, surf_int, end1, end2, part_in, upper_out, upper_in, upper_full, same,
    s_upper, r_upper, s_end, r_end, s_out, r_out, s_swap, r_swap, s_small, r_small, l_sem, s_gather, r_gather, s_core, r_core, s_halo, r_halo, s_hcore, r_hcore,
    s_fwd, r_fwd, s_adj, r_adj, s_grad, r_grad,
):
    c = lax.axis_index("cells")
    s = lax.axis_index("samples")
    y, l, k = s // 4, (s // 2) % 2, s % 2

    def rem(v, m):
        return lax.rem(v + m, m)

    def block(delta):
        return (rem(c + delta, n_cells), s if delta % 2 == 0 else s + 3 - 2 * (s % 4))

    def plane(yy, ll, kk):
        return (c, yy * 4 + ll * 2 + kk)

    up, down = plane(rem(y + 1, 4), l, k), plane(rem(y - 1, 4), l, k)
    across, other = plane(y, 1 - l, k), plane(y, l, 1 - k)
    partner = plane(y, 1 - l, 1 - k)
    odd = lax.rem(c, 2) == 1

    def copy(source, target, send, recv, device):
        return pltpu.make_async_remote_copy(source, target, send, recv, device_id=device, device_id_type=MESH)

    barrier = pltpu.get_barrier_semaphore()
    flip = 3 - 2 * (s % 4)

    def owner_of(delta):
        return (rem(c + delta, n_cells), s + lax.rem(c, 2) * flip)

    def worker(delta):
        there = rem(c + delta, n_cells)
        return (there, s + lax.rem(there, 2) * flip)

    peers = [up, down, across, other, partner] + [block(d) for d in (-2, -1, 1, 2)]
    peers = peers + [worker(d) for d in range(1, n_cells)]
    for device in peers:
        pl.semaphore_signal(barrier, inc=1, device_id=device, device_id_type=MESH)

    own_tiles = [
        pltpu.make_async_copy(te_ref.at[0], te.at[NB + s], l_sem.at[0]),
        pltpu.make_async_copy(ti_ref.at[0], ti.at[s], l_sem.at[1]),
    ]
    for cp in own_tiles:
        cp.start()
    surf_copy = pltpu.make_async_copy(surf_ref, surf_int, l_sem.at[2])
    surf_copy.start()
    stay = [
        pltpu.make_async_copy(init_ref, states.at[0], l_sem.at[3]),
        pltpu.make_async_copy(cot_ref, states.at[1], l_sem.at[4]),
    ]

    @pl.when(jnp.logical_not(odd))
    def _():
        for cp in stay:
            cp.start()

    row_of = lax.broadcasted_iota(jnp.int32, (ROWS, TILE), 0)
    piston = jnp.zeros((ROWS, TILE), f32)
    air = jnp.zeros((ROWS, TILE), f32)
    for i in range(ROWS):
        piston = jnp.where(row_of == i, piston_ref[i], piston)
        air = jnp.where(row_of == i, air_ref[i], air)
    levels[0] = piston
    levels[1] = air

    def pack_state(slot):
        for j in range(RT // 2):
            pair = jnp.concatenate([x[EDGE + 2 * j], x[EDGE + 2 * j + 1]], axis=0)
            send1[slot, j] = pair.astype(bf16)

    half_nb = NB // 2

    def state_copies(slot):
        mine = send1.at[slot]
        return [
            copy(mine, recv1.at[slot, 1], s_fwd.at[slot, 0], r_fwd.at[slot, 1], block(-1)),
            copy(mine, recv1.at[slot, 0], s_fwd.at[slot, 1], r_fwd.at[slot, 0], block(1)),
            copy(mine.at[pl.ds(0, half_nb)], recv2.at[slot, 1], s_fwd.at[slot, 2], r_fwd.at[slot, 3], block(-2)),
            copy(mine.at[pl.ds(RT // 2 - half_nb, half_nb)], recv2.at[slot, 0], s_fwd.at[slot, 3], r_fwd.at[slot, 2], block(2)),
        ]

    pl.semaphore_wait(barrier, len(peers))
    swap = [
        copy(init_ref, states.at[0], s_swap.at[0], r_swap.at[0], partner),
        copy(cot_ref, states.at[1], s_swap.at[1], r_swap.at[1], partner),
        copy(levels, levels_in, s_swap.at[2], r_swap.at[2], partner),
    ]

    buf = (te, ti)

    def tile_at(which, yy, ll, kk):
        row = yy * 4 + ll * 2 + kk
        return te.at[NB + row] if which == 0 else ti.at[row]

    gathers = {}

    def hop(name, which, yy, ll, device, source=None):
        at = tile_at(which, yy, ll, k)
        number = len(gathers)
        cp = copy(at if source is None else source, at, s_gather.at[number], r_gather.at[number], device)
        gathers[name] = (number, cp)
        cp.start()

    def arrived(name, which, yy, ll):
        number, cp = gathers[name]
        at = tile_at(which, yy, ll, k)
        copy(at, at, s_gather.at[number], r_gather.at[number], up).wait_recv()
        spread(which, yy, ll)

    core_sent = []
    halo_sent = []

    def spread(which, yy, ll):
        number = len(core_sent)
        at = tile_at(which, yy, ll, k)
        slot = which * 8 + yy * 2 + ll
        cp = copy(at, at, s_core.at[number], r_core.at[slot], other)
        core_sent.append(cp)
        cp.start()
        if which == 0:
            @pl.when(yy == 3)
            def _():
                copy(at, te.at[ll * 2 + k], s_halo.at[0, ll], r_halo.at[0, ll], block(1)).start()

            @pl.when(yy == 0)
            def _():
                copy(at, te.at[NB + RT + ll * 2 + k], s_halo.at[1, ll], r_halo.at[1, ll], block(-1)).start()

    ym, yp, yo, lo = rem(y - 1, 4), rem(y + 1, 4), rem(y + 2, 4), 1 - l
    for w, own in enumerate((te_ref.at[0], ti_ref.at[0])):
        hop(("up", w), w, y, l, up, own)
        hop(("down", w), w, y, l, down, own)
        hop(("x", w), w, y, l, across, own)
    @pl.when(odd)
    def _():
        for cp in swap:
            cp.start()

    for w in range(2):
        own_tiles[w].wait()
        spread(w, y, l)
    gacc[...] = jnp.zeros((ROWS, TILE), f32)
    for g in range(6):
        seg[g * SEG + GROUP] = jnp.zeros((ROWS, TILE), f32)

    lane = lax.broadcasted_iota(jnp.int32, (8, TILE), 1)
    spot = lax.broadcasted_iota(jnp.int32, (8, TILE), 0) * TILE + lane
    cols = jnp.zeros((8, TILE), jnp.int32)
    for m, ref in enumerate((cols_exp_ref, cols_imp_ref)):
        for r in range(RT):
            for j in range(K):
                cols = jnp.where(spot == (4 * m + r // 4) * TILE + (r % 4) * K + j, ref[j, r], cols)
    cols = jnp.clip(cols, LOW, LOW + WIN - 1)
    key = cols * 32 + lane
    rank = jnp.zeros((8, TILE), jnp.int32)
    upto = jnp.zeros((8, TILE), jnp.int32)
    here = jnp.zeros((8, TILE), jnp.int32)
    for i in range(GROUP):
        one = jnp.broadcast_to(cols[:, i:i + 1], (8, TILE))
        rank = rank + jnp.where(one * 32 + i < key, 1, 0)
        upto = upto + jnp.where(one - LOW <= lane, 1, 0)
        here = here + jnp.where(one - LOW == lane, 1, 0)
    order = jnp.zeros((8, TILE), jnp.int32)
    ordered = jnp.zeros((8, TILE), jnp.int32)
    before = jnp.zeros((8, TILE), jnp.int32)
    for i in range(GROUP):
        place = jnp.broadcast_to(rank[:, i:i + 1], (8, TILE))
        one = jnp.broadcast_to(cols[:, i:i + 1], (8, TILE))
        order = order + jnp.where(place == lane, i, 0)
        ordered = ordered + jnp.where(place == lane, one, 0)
        before = before + jnp.where(place + 1 == lane, one, 0)
    meta[0] = cols
    meta[1] = order
    meta[2] = jnp.where(ordered == before, 1, 0)
    meta[3] = jnp.where(here > 0, upto - 1, GROUP)

    surf_copy.wait()
    surf_own[...] = surf_int[...].astype(f32) * step_length
    small = []
    for side, device in ((0, block(1)), (1, block(-1))):
        small.append(copy(surf_own, surf_in.at[side], s_small.at[side], r_small.at[side], device))
        small.append(copy(meta, meta_in.at[side], s_small.at[2 + side], r_small.at[2 + side], device))
    for cp in small:
        cp.start()
    own_idx = pltpu.make_async_copy(meta, idx.at[1], l_sem.at[2])
    own_idx.start()


    arrived(("x", 0), 0, y, lo)
    hop(("xup", 0), 0, y, lo, up)
    hop(("xdown", 0), 0, y, lo, down)
    arrived(("up", 0), 0, ym, l)
    hop(("far", 0), 0, ym, l, up)
    arrived(("down", 0), 0, yp, l)
    arrived(("down", 1), 1, yp, l)
    hop(("far", 1), 1, yp, l, down)
    hop(("xd", 1), 1, yp, l, across)
    arrived(("up", 1), 1, ym, l)
    hop(("xu", 1), 1, ym, l, across)
    arrived(("x", 1), 1, y, lo)

    @pl.when(odd)
    def _():
        for cp in swap:
            cp.wait_recv()
        levels_used[...] = levels_in[...]

    @pl.when(jnp.logical_not(odd))
    def _():
        for cp in stay:
            cp.wait()
        levels_used[...] = levels[...]

    piston = levels_used[0]
    air = levels_used[1]
    for i in range(RT):
        x[EDGE + i] = states[0, :, i * TILE:(i + 1) * TILE]
        a[i] = states[1, :, i * TILE:(i + 1) * TILE]
    pack_state(0)
    for cp in state_copies(0):
        cp.start()

    for cp in small:
        cp.wait()
    moves = [pltpu.make_async_copy(meta_in.at[side], idx.at[2 * side], l_sem.at[3 + side]) for side in range(2)]
    for cp in moves:
        cp.start()
    for i in range(NB):
        half[i] = jnp.broadcast_to(surf_in[0, pl.ds(RT - NB + i, 1), :], (ROWS, TILE))
        half[NB + RT + i] = jnp.broadcast_to(surf_in[1, pl.ds(i, 1), :], (ROWS, TILE))
    for i in range(RT):
        half[NB + i] = jnp.broadcast_to(surf_own[pl.ds(i, 1), :], (ROWS, TILE))

    arrived(("xup", 0), 0, ym, lo)
    hop(("farx", 0), 0, ym, lo, up)
    arrived(("xdown", 0), 0, yp, lo)
    arrived(("xd", 1), 1, yp, lo)
    hop(("farx", 1), 1, yp, lo, down)
    arrived(("far", 0), 0, yo, l)
    own_idx.wait()
    for cp in moves:
        cp.wait()
    groups = [(0, 3)] + [(1, g) for g in range(8)] + [(2, 0)]
    first_of = {at: i * GROUP for i, at in enumerate(groups)}
    for owner, group in groups:
        for p in range(1, GROUP):
            factor = idx[owner, 2, group, p].astype(f32)
            same[first_of[owner, group] + p] = jnp.full((ROWS, TILE), factor, f32)
    arrived(("far", 1), 1, yo, l)
    arrived(("xu", 1), 1, ym, lo)
    arrived(("farx", 0), 0, yo, lo)
    arrived(("farx", 1), 1, yo, lo)
    hcore = []
    for side in range(2):
        for ll in range(2):
            base = 0 if side == 0 else NB + RT
            at = te.at[base + ll * 2 + 1 - k]
            copy(at, at, s_halo.at[side, ll], r_halo.at[side, ll], other).wait_recv()
            cp = copy(at, at, s_hcore.at[side, ll], r_hcore.at[side, ll], other)
            cp.start()
            hcore.append(cp)

    @pl.when(odd)
    def _():
        for cp in swap:
            cp.wait_send()

    for _, cp in gathers.values():
        cp.wait_send()
    for cp in core_sent:
        cp.wait_send()
    for w in range(2):
        for yy in range(4):
            for ll in range(2):
                at = tile_at(w, yy, ll, 1 - k)
                copy(at, at, s_core.at[0], r_core.at[w * 8 + yy * 2 + ll], other).wait_recv()
    for side in range(2):
        for ll in range(2):
            at = te.at[ll]
            copy(at, at, s_halo.at[side, ll], r_halo.at[side, ll], other).wait_send()
    for cp in hcore:
        cp.wait()

    def exchange_at(n, w):
        t = x[RT + w]
        th = jnp.tanh(t)
        hs = half[w]
        gas[n, w] = hs * (air - t * (1.0 + buffer_gain * th))
        bend[n, w] = hs * piston * (1.0 + buffer_gain * th + buffer_gain * t * (1.0 - th * th))

    wide_rows = []
    for r in range(NB):
        wide_rows.append((r, 0, 3, r, -LOW))
    for r in range(RT):
        wide_rows.append((NB + r, 1, r // 4, r % 4, NB))
    for r in range(NB):
        wide_rows.append((NB + RT + r, 2, 0, r, NB + RT))

    def forward_row(tiles, row, field, owner, group, place, shift):
        picked = [field[idx[owner, 0, group, place * K + j] + shift] for j in range(K)]
        values = jnp.concatenate(picked, axis=1).astype(bf16)
        weights = jnp.concatenate([tiles[row, j] for j in range(K)], axis=1)
        return lax.dot_general(values, weights, (((1,), (1,)), ((), ())), preferred_element_type=f32)

    def forward_step(n, slot):
        for cp in state_copies(slot):
            cp.wait_recv()
        for j in range(RT // 2):
            for side, base in ((0, NB), (1, EDGE + RT)):
                pair = recv1[slot, side, j].astype(f32)
                x[base + 2 * j] = pair[:ROWS]
                x[base + 2 * j + 1] = pair[ROWS:]
        for j in range(half_nb):
            for side, base in ((0, 0), (1, EDGE + RT + RT)):
                pair = recv2[slot, side, j].astype(f32)
                x[base + 2 * j] = pair[:ROWS]
                x[base + 2 * j + 1] = pair[ROWS:]
        for i in range(NB):
            exchange_at(n, i)
            exchange_at(n, NB + RT + i)
        for row, owner, group, place, shift in wide_rows:
            moved = forward_row(te, row, x, owner, group, place, shift)
            src[row] = moved + piston * gas[n, row]
        for r in range(RT):
            x[EDGE + r] = forward_row(ti, r, src, 1, 4 + r // 4, r % 4, -LOW)

    def segments(first, number, owner, group):
        total = None
        for p in range(GROUP):
            value = contrib[first + idx[owner, 1, group, p]]
            if p > 0:
                value = value + total * same[first_of[owner, group] + p]
            total = value
            seg[number * SEG + p] = total

    def landed(number, owner, group, w):
        return seg[number * SEG + idx[owner, 3, group, w]]

    def adjoint_row(tiles, row, field):
        weights = jnp.concatenate([tiles[row, j] for j in range(K)], axis=1)
        spread_out = jnp.dot(field.astype(bf16), weights, preferred_element_type=f32)
        for j in range(K):
            contrib[row * K + j] = spread_out[:, j * TILE:(j + 1) * TILE]

    def adjoint_copies(slot):
        return [
            copy(out1.at[slot, 0], in1.at[slot, 1], s_adj.at[slot, 0], r_adj.at[slot, 1], block(-1)),
            copy(out1.at[slot, 1], in1.at[slot, 0], s_adj.at[slot, 1], r_adj.at[slot, 0], block(1)),
            copy(out2.at[slot, 0], in2.at[slot, 1], s_adj.at[slot, 2], r_adj.at[slot, 3], block(-2)),
            copy(out2.at[slot, 1], in2.at[slot, 0], s_adj.at[slot, 3], r_adj.at[slot, 2], block(2)),
        ]

    end = (STEPS - 1) % 2
    closing = [
        copy(out1.at[end, 0], end1.at[1], s_end.at[0], r_end.at[1], owner_of(-1)),
        copy(out1.at[end, 1], end1.at[0], s_end.at[1], r_end.at[0], owner_of(1)),
        copy(out2.at[end, 0], end2.at[1], s_end.at[2], r_end.at[3], owner_of(-2)),
        copy(out2.at[end, 1], end2.at[0], s_end.at[3], r_end.at[2], owner_of(2)),
    ]
    part_copy = copy(part, part_in, s_end.at[4], r_end.at[4], partner)

    def grad_copy(d):
        return copy(gacc, gin.at[c], s_grad.at[d], r_grad.at[c], owner_of(d))

    def upper_part():
        for r in range(RT):
            adjoint_row(ti, r, a[r])
        for g in range(4):
            segments(g * GROUP, g, 1, 4 + g)
        for w in range(WIN):
            upper = landed(0, 1, 4, w)
            for g in range(1, 4):
                upper = upper + landed(g, 1, 4 + g, w)
            u[w] = upper

    def adjoint_part(n, slot):
        for r in range(WIN):
            adjoint_row(te, r, u[r])
        segments(0, 0, 0, 3)
        for g in range(4):
            segments((1 + g) * GROUP, 1 + g, 1, g)
        segments(5 * GROUP, 5, 2, 0)

        def wide(i):
            total = None
            terms = []
            if i < WIN:
                terms.append(landed(0, 0, 3, i))
            if RT <= i < RT + WIN:
                for g in range(4):
                    terms.append(landed(1 + g, 1, g, i - RT))
                if n is not None:
                    terms.append(-(bend[n, i - RT] * u[i - RT]))
            if i >= 2 * RT:
                terms.append(landed(5, 2, 0, i - 2 * RT))
            for term in terms:
                total = term if total is None else total + term
            return total

        for j in range(RT // 2):
            for side, base in ((0, NB), (1, EDGE + RT)):
                pair = jnp.concatenate([wide(base + 2 * j), wide(base + 2 * j + 1)], axis=0)
                out1[slot, side, j] = pair.astype(bf16)
        for j in range(half_nb):
            for side, base in ((0, 0), (1, EDGE + 2 * RT)):
                pair = jnp.concatenate([wide(base + 2 * j), wide(base + 2 * j + 1)], axis=0)
                out2[slot, side, j] = pair.astype(bf16)
        if n is None:
            for cp in adjoint_copies(slot):
                cp.start()
        else:
            @pl.when(n > 0)
            def _():
                for cp in adjoint_copies(slot):
                    cp.start()

            @pl.when(n == 0)
            def _():
                for cp in closing:
                    cp.start()

        for i in range(RT):
            part[i] = wide(EDGE + i)

    def adjoint_sum(slot):
        for cp in adjoint_copies(slot):
            cp.wait_recv()
        for j in range(RT // 2):
            both = in1[slot, 0, j].astype(f32) + in1[slot, 1, j].astype(f32)
            if j < half_nb:
                both = both + in2[slot, 0, j].astype(f32)
            if j >= RT // 2 - half_nb:
                both = both + in2[slot, 1, j - (RT // 2 - half_nb)].astype(f32)
            a[2 * j] = part[2 * j] + both[:ROWS]
            a[2 * j + 1] = part[2 * j + 1] + both[ROWS:]

    upper_copies = [
        copy(upper_out.at[0], upper_in.at[1], s_upper.at[0], r_upper.at[1], block(-1)),
        copy(upper_out.at[1], upper_in.at[0], s_upper.at[1], r_upper.at[0], block(1)),
    ]

    def first_part():
        upper_part()
        for j in range(half_nb):
            for side, base in ((0, 0), (1, NB + RT)):
                pair = jnp.concatenate([u[base + 2 * j], u[base + 2 * j + 1]], axis=0)
                upper_out[side, j] = pair.astype(bf16)
        for cp in upper_copies:
            cp.start()
        for i in range(RT):
            upper_full[i] = u[NB + i]
        adjoint_part(None, 0)

    def first_sum():
        adjoint_sum(0)
        for cp in upper_copies:
            cp.wait_recv()
        for j in range(half_nb):
            for side, base in ((0, 0), (1, RT - NB)):
                pair = upper_in[side, j].astype(f32)
                upper_full[base + 2 * j] = upper_full[base + 2 * j] + pair[:ROWS]
                upper_full[base + 2 * j + 1] = upper_full[base + 2 * j + 1] + pair[ROWS:]

    @pl.loop(0, STEPS - 1)
    def _(n):
        slot = lax.rem(n, 2)
        for i in range(RT):
            exchange_at(n, NB + i)

        @pl.when(n == 1)
        def _():
            first_part()

        @pl.when(n == 3)
        def _():
            first_sum()

        forward_step(n, slot)

        @pl.when(n > 0)
        def _():
            for cp in state_copies(1 - slot):
                cp.wait_send()

        pack_state(1 - slot)
        for cp in state_copies(1 - slot):
            cp.start()

    last = STEPS - 1
    grad = gacc[...]
    for i in range(RT):
        exchange_at(last, NB + i)
        a[i] = a[i] - bend[last, NB + i] * upper_full[i]
        grad = grad + upper_full[i] * gas[last, NB + i]
    gacc[...] = grad

    final_stays = pltpu.make_async_copy(leaving.at[0], out_ref.at[0], l_sem.at[0])
    final_copy = copy(leaving.at[0], out_ref.at[0], s_out.at[0], r_out.at[0], partner)
    adj_stays = pltpu.make_async_copy(leaving.at[1], out_ref.at[1], l_sem.at[1])

    @pl.loop(1, STEPS)
    def _(back):
        n = STEPS - 1 - back
        slot = lax.rem(back, 2)
        upper_part()
        grad = gacc[...]
        for w in range(WIN):
            grad = grad + u[w] * gas[n, w]
        gacc[...] = grad

        @pl.when(back > 1)
        def _():
            for cp in adjoint_copies(slot):
                cp.wait_send()

        adjoint_part(n, slot)

        @pl.when(back == STEPS - 1)
        def _():
            for d in range(1, n_cells):
                grad_copy(d).start()

            @pl.when(odd)
            def _():
                grad_copy(0).start()

        @pl.when(back == 1)
        def _():
            forward_step(last, last % 2)
            for i in range(RT):
                leaving[0, :, i * TILE:(i + 1) * TILE] = x[EDGE + i]

            @pl.when(odd)
            def _():
                final_copy.start()

            @pl.when(jnp.logical_not(odd))
            def _():
                final_stays.start()

        @pl.when(back < STEPS - 1)
        def _():
            adjoint_sum(slot)

    @pl.when(odd)
    def _():
        part_copy.start()
        part_copy.wait_recv()
        for i in range(RT):
            a[i] = part_in[i]

    @pl.when(jnp.logical_not(odd))
    def _():
        for i in range(RT):
            a[i] = part[i]

    for cp in closing:
        cp.wait_recv()
    for j in range(RT // 2):
        both = end1[0, j].astype(f32) + end1[1, j].astype(f32)
        if j < half_nb:
            both = both + end2[0, j].astype(f32)
        if j >= RT // 2 - half_nb:
            both = both + end2[1, j - (RT // 2 - half_nb)].astype(f32)
        for h in range(2):
            i = 2 * j + h
            leaving[1, :, i * TILE:(i + 1) * TILE] = a[i] + both[h * ROWS:(h + 1) * ROWS]

    adj_stays.start()

    @pl.when(odd)
    def _():
        grad_copy(0).wait_recv()
        part_copy.wait_send()

    @pl.when(jnp.logical_not(odd))
    def _():
        gin[c] = gacc[...]

    total = gin[c]
    for d in range(1, n_cells):
        source = rem(c - d, n_cells)
        copy(gacc, gin.at[source], s_grad.at[d], r_grad.at[source], owner_of(d)).wait_recv()
        total = total + gin[source]
    scale = 1.0 / math.sqrt(n_cells * RT * TILE)
    grad_ref[...] = jnp.broadcast_to(jnp.sum(total, axis=1, keepdims=True) * scale, (ROWS, TILE))

    for d in range(1, n_cells):
        grad_copy(d).wait_send()
    for cp in adjoint_copies(1 - end):
        cp.wait_send()
    for cp in closing:
        cp.wait_send()
    for slot in range(2):
        for cp in state_copies(slot):
            cp.wait_send()
    for cp in upper_copies:
        cp.wait_send()

    @pl.when(odd)
    def _():
        grad_copy(0).wait_send()
        final_copy.wait()

    @pl.when(jnp.logical_not(odd))
    def _():
        final_stays.wait()

    adj_stays.wait()


def solution(mesh):
    n_cells = mesh.shape["cells"]

    def body(init_state, tiles_exp, cols_exp, tiles_imp, cols_imp, surface, piston, atmosphere, final_cot):
        vmem, smem = pl.BlockSpec(memory_space=pltpu.VMEM), pl.BlockSpec(memory_space=pltpu.SMEM)
        anywhere = pl.BlockSpec(memory_space=pl.ANY)
        dma, i32 = pltpu.SemaphoreType.DMA, jnp.int32
        scratch = [
            pltpu.VMEM((WIN, K, TILE, TILE), bf16),
            pltpu.VMEM((RT, K, TILE, TILE), bf16),
            pltpu.VMEM((WIDE, ROWS, TILE), f32),
            pltpu.VMEM((WIN, ROWS, TILE), f32),
            pltpu.VMEM((STEPS, WIN, ROWS, TILE), f32),
            pltpu.VMEM((STEPS, WIN, ROWS, TILE), f32),
            pltpu.VMEM((WIN, ROWS, TILE), f32),
            pltpu.VMEM((4, 8, TILE), i32),
            pltpu.VMEM((2, 4, 8, TILE), i32),
            pltpu.SMEM((3, 4, 8, TILE), i32),
            pltpu.VMEM((RT, TILE), f32),
            pltpu.VMEM((2, RT, TILE), f32),
            pltpu.VMEM((2, RT // 2, 2 * ROWS, TILE), bf16),
            pltpu.VMEM((2, 2, RT // 2, 2 * ROWS, TILE), bf16),
            pltpu.VMEM((2, 2, NB // 2, 2 * ROWS, TILE), bf16),
            pltpu.VMEM((RT, ROWS, TILE), f32),
            pltpu.VMEM((WIN, ROWS, TILE), f32),
            pltpu.VMEM((RT, ROWS, TILE), f32),
            pltpu.VMEM((WIN * K, ROWS, TILE), f32),
            pltpu.VMEM((6 * SEG, ROWS, TILE), f32),
            pltpu.VMEM((2, 2, RT // 2, 2 * ROWS, TILE), bf16),
            pltpu.VMEM((2, 2, NB // 2, 2 * ROWS, TILE), bf16),
            pltpu.VMEM((2, 2, RT // 2, 2 * ROWS, TILE), bf16),
            pltpu.VMEM((2, 2, NB // 2, 2 * ROWS, TILE), bf16),
            pltpu.VMEM((ROWS, TILE), f32),
            pltpu.VMEM((n_cells, ROWS, TILE), f32),
            pltpu.VMEM((2, ROWS, TILE), f32),
            pltpu.VMEM((2, ROWS, TILE), f32),
            pltpu.VMEM((2, ROWS, TILE), f32),
            pltpu.VMEM((2, ROWS, RT * TILE), f32),
            pltpu.VMEM((2, ROWS, RT * TILE), f32),
            pltpu.VMEM((RT, TILE), i32),
            pltpu.VMEM((2, RT // 2, 2 * ROWS, TILE), bf16),
            pltpu.VMEM((2, NB // 2, 2 * ROWS, TILE), bf16),
            pltpu.VMEM((RT, ROWS, TILE), f32),
            pltpu.VMEM((2, NB // 2, 2 * ROWS, TILE), bf16),
            pltpu.VMEM((2, NB // 2, 2 * ROWS, TILE), bf16),
            pltpu.VMEM((RT, ROWS, TILE), f32),
            pltpu.VMEM((10 * GROUP, ROWS, TILE), f32),
            dma((2,)), dma((2,)),
            dma((5,)), dma((5,)),
            dma((1,)), dma((1,)),
            dma((3,)), dma((3,)),
            dma((4,)), dma((4,)), dma((5,)),
            dma((14,)), dma((14,)), dma((16,)), dma((16,)),
            dma((2, 2)), dma((2, 2)), dma((2, 2)), dma((2, 2)),
            dma((2, 4)), dma((2, 4)), dma((2, 4)), dma((2, 4)),
            dma((n_cells,)), dma((n_cells,)),
        ]

        def run(*refs):
            kernel(n_cells, *refs)

        states = jax.ShapeDtypeStruct((2, ROWS, RT * TILE), f32)
        both, grad = pl.pallas_call(
            run,
            out_shape=(states, jax.ShapeDtypeStruct((ROWS, TILE), f32)),
            in_specs=[anywhere, anywhere, anywhere, smem, smem, anywhere, smem, smem, anywhere],
            out_specs=(anywhere, vmem),
            scratch_shapes=scratch,
            compiler_params=pltpu.CompilerParams(
                collective_id=0, has_side_effects=True, vmem_limit_bytes=60 << 20
            ),
        )(
            init_state, tiles_exp, tiles_imp, cols_exp.T, cols_imp.T, surface.reshape(RT, TILE),
            piston, atmosphere, final_cot,
        )
        return both[0], both[1], grad[:, 0]

    placed = (
        P("samples", "cells"),
        P(("cells", "samples"), None, None, None),
        P("cells", None),
        P(("cells", "samples"), None, None, None),
        P("cells", None),
        P("cells"),
        P("samples"),
        P("samples"),
        P("samples", "cells"),
    )
    return jax.shard_map(
        body,
        mesh=mesh,
        in_specs=placed,
        out_specs=(P("samples", "cells"), P("samples", "cells"), P("samples")),
        check_vma=False,
    )
```
